32 devices in a mesh: dp: 8 (over z, y), seq: 4 (over x, core).
Axes of the slice: x: 2, y: 2, z: 4, core: 2. Of those that a mesh axis runs over, the one named last changes fastest.
Arguments:
- block_input: bfloat16 [8, 608, 1024], P('dp', 'seq'), may hold values from -6 to 6
- cotangent: bfloat16 [8, 608, 1024], P('dp', 'seq'), may hold values from -6 to 6
- image_valid: int32 [8], P('dp'), may hold values 0 or 1
- token_valid: int32 [608], replicated, may hold values 0 or 1
- first_gain: bfloat16 [1024], P(('dp', 'seq')), may hold values from 0.5 to 1.5
- first_shift: bfloat16 [1024], P(('dp', 'seq')), may hold values from -2 to 2
- query_weight: bfloat16 [1024, 1024], P('dp', 'seq'), may hold values from -0.1875 to 0.1875
- query_bias: bfloat16 [1024], P(('dp', 'seq')), may hold values from -2 to 2
- key_weight: bfloat16 [1024, 1024], P('dp', 'seq'), may hold values from -0.1875 to 0.1875
- value_weight: bfloat16 [1024, 1024], P('dp', 'seq'), may hold values from -0.1875 to 0.1875
- value_bias: bfloat16 [1024], P(('dp', 'seq')), may hold values from -2 to 2
- output_weight: bfloat16 [1024, 1024], P('dp', 'seq'), may hold values from -2.5 to 2.5
- output_bias: bfloat16 [1024], P(('dp', 'seq')), may hold values from -2 to 2
- second_gain: bfloat16 [1024], P(('dp', 'seq')), may hold values from 0.5 to 1.5
- second_shift: bfloat16 [1024], P(('dp', 'seq')), may hold values from -2 to 2
- expand_weight: bfloat16 [1024, 4096], P('dp', 'seq'), may hold values from -0.1875 to 0.1875
- expand_bias: bfloat16 [4096], P(('dp', 'seq')), may hold values from -2 to 2
- reduce_weight: bfloat16 [4096, 1024], P('dp', 'seq'), may hold values from -0.09375 to 0.09375
- reduce_bias: bfloat16 [1024], P(('dp', 'seq')), may hold values from -2 to 2
Outputs:
- block_output: bfloat16 [8, 608, 1024], P('dp', 'seq')
- input_gradient: bfloat16 [8, 608, 1024], P('dp', 'seq')
- first_gain_gradient: float32 [1024], P(('dp', 'seq'))
- first_shift_gradient: float32 [1024], P(('dp', 'seq'))
- query_weight_gradient: float32 [1024, 1024], P('dp', 'seq')
- query_bias_gradient: float32 [1024], P(('dp', 'seq'))
- key_weight_gradient: float32 [1024, 1024], P('dp', 'seq')
- value_weight_gradient: float32 [1024, 1024], P('dp', 'seq')
- value_bias_gradient: float32 [1024], P(('dp', 'seq'))
- output_weight_gradient: float32 [1024, 1024], P('dp', 'seq')
- output_bias_gradient: float32 [1024], P(('dp', 'seq'))
- second_gain_gradient: float32 [1024], P(('dp', 'seq'))
- second_shift_gradient: float32 [1024], P(('dp', 'seq'))
- expand_weight_gradient: float32 [1024, 4096], P('dp', 'seq')
- expand_bias_gradient: float32 [4096], P(('dp', 'seq'))
- reduce_weight_gradient: float32 [4096, 1024], P('dp', 'seq')
- reduce_bias_gradient: float32 [1024], P(('dp', 'seq'))
The draws below stay inside these ranges and needn't reach their ends.
All inputs are finite; a program needn't handle non-finite values. No bound on the sum of `image_valid` on one device may be relied on, other than what follows from the above.
Results may differ from the reference program's by a relative error of at most 0.017.
Values may be sent and summed in bfloat16 or wider, within the bound.
No kernel may reach another device: no remote copies, remote signals or barrier semaphores. Data moves between devices by JAX's collectives and lax.ppermute only.
A program may use at most 192 MiB of HBM per device.

```python
import jax
import jax.numpy as jnp
from jax import lax

D = 1024
HEADS = 16
HEAD_DIM = 64
FF = 4096
TOK_IMG = 608
SLOTS = 8


def plant(drawn, own_key, smallest, high):
    longest = drawn.shape.index(max(drawn.shape))
    spots = []
    for shift in (0, 1):
        where = [jax.random.randint(jax.random.fold_in(own_key, axis), (), 0, length) for axis, length in enumerate(drawn.shape)]
        where[longest] = (where[longest] + shift) % drawn.shape[longest]
        spots.append(tuple(where))
    return drawn.at[spots[0]].set(smallest).at[spots[1]].set(high)


def levels(stream_key, extent, shards, least, top_value):
    def one(axis_at, blocks):
        steps = jax.random.uniform(jax.random.fold_in(jax.random.fold_in(stream_key, 6), axis_at), (blocks,), jnp.float32, least / len(shards), top_value / len(shards))
        return jnp.repeat(jnp.exp(steps), extent[axis_at] // blocks).reshape((-1,) + (1,) * (len(extent) - axis_at - 1))

    level = one(*shards[0])
    for cut in shards[1:]:
        level = level * one(*cut)
    return level


def bell_draw(rng, shape, width, most, split=(), dtype=jnp.bfloat16):
    loudness = levels(rng, shape, split, -0.22, 0.18) if split else 1.0
    drawn = jax.random.normal(rng, shape, jnp.float32) * width * loudness
    return jnp.minimum(jnp.maximum(drawn, -most), most).astype(dtype)


def setup_inputs(seed: int = 0) -> dict:
    arg_keys = jax.random.split(jax.random.key(seed), 20)
    return {
        "block_input": bell_draw(arg_keys[0], (SLOTS, TOK_IMG, D), 1.0, 6.0, ((0, 8), (1, 4))),
        "cotangent": bell_draw(arg_keys[1], (SLOTS, TOK_IMG, D), 1.0, 6.0, ((0, 8), (1, 4))),
        "image_valid": plant((jax.random.randint(arg_keys[2], (SLOTS,), 0, 8) < 7).astype(jnp.int32), jax.random.fold_in(arg_keys[2], 1), 0, 1),
        "token_valid": plant((jax.random.randint(arg_keys[3], (TOK_IMG,), 0, 16) < 15).astype(jnp.int32), jax.random.fold_in(arg_keys[3], 1), 0, 1),
        "first_gain": jnp.clip(1.0 + 0.1 * jax.random.normal(arg_keys[4], (D,), jnp.float32), 0.5, 1.5).astype(jnp.bfloat16),
        "first_shift": bell_draw(arg_keys[5], (D,), 0.3, 2.0, ((0, 32),)),
        "query_weight": bell_draw(arg_keys[6], (D, D), D ** -0.5, 0.1875, ((0, 8), (1, 4))),
        "query_bias": bell_draw(arg_keys[7], (D,), 0.3, 2.0, ((0, 32),)),
        "key_weight": bell_draw(arg_keys[8], (D, D), D ** -0.5, 0.1875, ((0, 8), (1, 4))),
        "value_weight": bell_draw(arg_keys[9], (D, D), D ** -0.5, 0.1875, ((0, 8), (1, 4))),
        "value_bias": bell_draw(arg_keys[10], (D,), 0.3, 2.0, ((0, 32),)),
        "output_weight": bell_draw(arg_keys[11], (D, D), (D * 4 // TOK_IMG) ** -0.5, 2.5, ((0, 8), (1, 4))),
        "output_bias": bell_draw(arg_keys[12], (D,), 0.3, 2.0, ((0, 32),)),
        "second_gain": jnp.clip(1.0 + 0.1 * jax.random.normal(arg_keys[13], (D,), jnp.float32), 0.5, 1.5).astype(jnp.bfloat16),
        "second_shift": bell_draw(arg_keys[14], (D,), 0.3, 2.0, ((0, 32),)),
        "expand_weight": bell_draw(arg_keys[15], (D, FF), D ** -0.5, 0.1875, ((0, 8), (1, 4))),
        "expand_bias": bell_draw(arg_keys[16], (FF,), 0.3, 2.0, ((0, 32),)),
        "reduce_weight": bell_draw(arg_keys[17], (FF, D), FF ** -0.5, 0.09375, ((0, 8), (1, 4))),
        "reduce_bias": bell_draw(arg_keys[18], (D,), 0.3, 2.0, ((0, 32),)),
    }


@jax.custom_vjp
def low(v):
    return lax.optimization_barrier(v.astype(jnp.bfloat16)).astype(jnp.float32)

@jax.custom_vjp
def low_back(v):
    return v

def low_keep(v):
    return (low(v), None)

def low_pass(kept, grad):
    return (grad,)

def back_keep(v):
    return (v, None)

def back_low(kept, grad):
    return (low(grad),)
low.defvjp(low_keep, low_pass)
low_back.defvjp(back_keep, back_low)

def matmul(left, right):
    return jnp.dot(left, right, precision=lax.Precision.HIGHEST, preferred_element_type=jnp.float32)

def normalize(values, gain, shift):
    center = values - lax.optimization_barrier(jnp.mean(values, axis=-1, keepdims=True))
    scale = lax.rsqrt(lax.optimization_barrier(jnp.mean(center * center, axis=-1, keepdims=True)) + 1e-06)
    return center * scale * gain + shift

def split_heads(values):
    return values.reshape(TOK_IMG, HEADS, HEAD_DIM).transpose(1, 0, 2)

def one_image(values, params, token_valid):
    first_gain, first_shift, query_weight, query_bias, key_weight, value_weight, value_bias, output_weight, output_bias, second_gain, second_shift, expand_weight, expand_bias, reduce_weight, reduce_bias = params
    normed = low(normalize(values, first_gain, first_shift))
    queries = low(low_back(matmul(normed, query_weight) + query_bias))
    key_rows = low(low_back(matmul(normed, key_weight)))
    value_rows = low(low_back(matmul(normed, value_weight) + value_bias))
    logits = low_back(jnp.einsum('hqd,hkd->hqk', split_heads(queries), split_heads(key_rows), precision=lax.Precision.HIGHEST))
    scores = jnp.where(token_valid[None, None, :] > 0, logits * HEAD_DIM ** (-0.5), -1000000000.0)
    weights = low(jax.nn.softmax(scores, axis=-1))
    mixed = jnp.einsum('hqk,hkd->qhd', weights, split_heads(value_rows), precision=lax.Precision.HIGHEST).reshape(TOK_IMG, D)
    mixed = low(low_back(mixed))
    branch = low_back(matmul(mixed, output_weight) + output_bias)
    middle = values + branch
    second = low(normalize(middle, second_gain, second_shift))
    expanded = low_back(matmul(second, expand_weight) + expand_bias)
    active = low(jax.nn.gelu(expanded, approximate=False))
    branch_two = low_back(matmul(active, reduce_weight) + reduce_bias)
    return middle + branch_two

def reference(block_input, cotangent, image_valid, token_valid, first_gain, first_shift, query_weight, query_bias, key_weight, value_weight, value_bias, output_weight, output_bias, second_gain, second_shift, expand_weight, expand_bias, reduce_weight, reduce_bias):
    params = tuple((p.astype(jnp.float32) for p in (first_gain, first_shift, query_weight, query_bias, key_weight, value_weight, value_bias, output_weight, output_bias, second_gain, second_shift, expand_weight, expand_bias, reduce_weight, reduce_bias)))
    inputs = block_input.astype(jnp.float32)

    def forward(images, weights):
        per_image = jax.checkpoint(lambda image: one_image(image, weights, token_valid))
        return lax.map(per_image, images)
    result, pullback = jax.vjp(forward, inputs, params)
    factor = image_valid.astype(jnp.float32)[:, None, None] * token_valid.astype(jnp.float32)[None, :, None]
    upstream = cotangent.astype(jnp.float32) * factor
    input_grad, param_grads = pullback(upstream)
    return (result.astype(jnp.bfloat16), input_grad.astype(jnp.bfloat16), param_grads[0], param_grads[1], param_grads[2], param_grads[3], param_grads[4], param_grads[5], param_grads[6], param_grads[7], param_grads[8], param_grads[9], param_grads[10], param_grads[11], param_grads[12], param_grads[13], param_grads[14])
```

```python
import jax
import jax.numpy as jnp
from jax import lax
from jax.experimental import pallas as pl
from jax.experimental.pallas import tpu as pltpu
from jax.sharding import PartitionSpec as P

HEADS = 16
EPS = 1e-06
BF = jnp.bfloat16
F32 = jnp.float32
SEQ = 4
BLOCKS = 8
MIB = 1 << 20


def mm(a, b):
    return lax.dot_general(a, b, (((1,), (0,)), ((), ())), preferred_element_type=F32)


def mm_nt(a, b):
    return lax.dot_general(a, b, (((1,), (1,)), ((), ())), preferred_element_type=F32)


def mm_tn(a, b):
    return lax.dot_general(a, b, (((0,), (0,)), ((), ())), preferred_element_type=F32)


def standardize(values):
    center = values - jnp.mean(values, axis=-1, keepdims=True)
    scale = lax.rsqrt(jnp.mean(center * center, axis=-1, keepdims=True) + EPS)
    return center * scale, scale


def rows_at(start, size):
    return pl.ds(pl.multiple_of(start, size), size)


def kernel_call(body, outs, *args, scratch=(), flops=0, vmem=32):
    specs = [
        pl.BlockSpec(memory_space=pltpu.SMEM if a.dtype == jnp.int32 else pltpu.VMEM) for a in args
    ]
    moved = sum(a.size * a.dtype.itemsize for a in args)
    moved += sum(o.size * o.dtype.itemsize for o in outs)
    return pl.pallas_call(
        body,
        out_shape=tuple(outs),
        in_specs=specs,
        out_specs=tuple(pl.BlockSpec(memory_space=pltpu.VMEM) for _ in outs),
        scratch_shapes=list(scratch),
        compiler_params=pltpu.CompilerParams(vmem_limit_bytes=vmem * MIB),
        cost_estimate=pl.CostEstimate(flops=int(flops), bytes_accessed=int(moved), transcendentals=0),
    )(*args)


def shape(dims, dtype):
    return jax.ShapeDtypeStruct(tuple(dims), dtype)


def norm_one(x0, x1, x2, x3, gain, shift, a_out, n_out, hold):
    rows = x0.shape[0]
    for k, ref in enumerate((x0, x1, x2, x3)):
        normal, _ = standardize(ref[...].astype(F32))
        hold[k * rows : (k + 1) * rows, :] = normal
    normal = hold[...]
    n_out[...] = normal.astype(BF)
    a_out[...] = (normal * gain[...] + shift[...]).astype(BF)


def mask_rows(c0, c1, c2, c3, factor, g_out, hold):
    rows = c0.shape[0]
    for k, ref in enumerate((c0, c1, c2, c3)):
        hold[k * rows : (k + 1) * rows, :] = ref[...].astype(F32)
    g_out[...] = (hold[...] * factor[...]).astype(BF)


def head_lanes(width, head, size):
    lane = lax.broadcasted_iota(jnp.int32, (1, width), 1)
    return (lane >= head * size) & (lane < (head + 1) * size)


def attend(idx, a, *refs):
    pieces = refs[:BLOCKS]
    bias, key_mask, q_out, k_out, v_out, o_out, stat_out, w_out = refs[BLOCKS:]
    step = pieces[0].shape[0]
    for k in range(BLOCKS):
        w_out[rows_at(idx[k] * step, step), :] = pieces[k][...]
    width = q_out.shape[1]
    qkv = (mm(a[...], w_out[...]) + bias[...]).astype(BF)
    q = qkv[:, :width]
    key = qkv[:, width : 2 * width]
    value = qkv[:, 2 * width :]
    q_out[...] = q
    k_out[...] = key
    v_out[...] = value
    size = width // (HEADS // SEQ)
    valid = key_mask[...] > 0
    total = None
    for h in range(HEADS // SEQ):
        lanes = head_lanes(width, h, size)
        logits = mm_nt(jnp.where(lanes, q, jnp.zeros_like(q)), key)
        scores = jnp.where(valid, logits * size ** (-0.5), -1000000000.0)
        top = jnp.max(scores, axis=-1, keepdims=True)
        weights = jnp.exp(scores - top)
        inverse = 1.0 / jnp.sum(weights, axis=-1, keepdims=True)
        probs = (weights * inverse).astype(BF)
        mixed = mm(probs, jnp.where(lanes, value, jnp.zeros_like(value)))
        total = mixed if total is None else total + mixed
        stat_out[:, h : h + 1] = top
        stat_out[:, HEADS // SEQ + h : HEADS // SEQ + h + 1] = inverse
    o_out[...] = total.astype(BF)


def middle(idx, order, *refs):
    o = refs[:SEQ]
    w = refs[SEQ : 2 * SEQ]
    x = refs[2 * SEQ : 3 * SEQ]
    bias, gain, shift, c_out, x_out, w_out, hold = refs[3 * SEQ :]
    rows = x[0].shape[0]
    width = o[0].shape[1]
    step = w[0].shape[0] // BLOCKS
    for k in range(BLOCKS):
        for m in range(SEQ):
            w_out[rows_at(idx[k] * step, step), rows_at(order[m] * width, width)] = w[m][
                k * step : (k + 1) * step, :
            ]
    for k in range(SEQ):
        hold[k * rows : (k + 1) * rows, :] = x[k][...].astype(F32) + bias[...]
    for m in range(SEQ):
        part = mm(o[m][...], w_out[rows_at(order[m] * width, width), :])
        for k in range(SEQ):
            there = (k ^ m) * rows
            hold[there : there + rows, :] += part[k * rows : (k + 1) * rows, :]
    x_out[...] = hold[0:rows, :]
    normal, _ = standardize(hold[...])
    c_out[...] = (normal * gain[...] + shift[...]).astype(BF)


def expand(idx, c, *refs):
    pieces = refs[:BLOCKS]
    bias, h_out, p_out, w_out = refs[BLOCKS:]
    step = pieces[0].shape[0]
    for k in range(BLOCKS):
        w_out[rows_at(idx[k] * step, step), :] = pieces[k][...]
    width = h_out.shape[1]
    chunk = 256
    for n in range(0, width, chunk):
        u = mm(c[...], w_out[:, n : n + chunk]) + bias[:, n : n + chunk]
        cdf = 0.5 * (1.0 + lax.erf(u * (0.5**0.5)))
        density = jnp.exp(-0.5 * u * u) * 0.3989422804014327
        h_out[:, n : n + chunk] = (u * cdf).astype(BF)
        p_out[:, n : n + chunk] = cdf + u * density


def reduce_part(idx, h, *refs):
    pieces = refs[:BLOCKS]
    outs = refs[BLOCKS : BLOCKS + SEQ]
    w_out = refs[BLOCKS + SEQ]
    deep, wide = pieces[0].shape
    for k in range(BLOCKS):
        w_out[rows_at(idx[k] // SEQ * deep, deep), rows_at(idx[k] % SEQ * wide, wide)] = pieces[k][...]
    y = mm(h[...], w_out[...])
    rows = outs[0].shape[0]
    for k in range(SEQ):
        outs[k][...] = y[k * rows : (k + 1) * rows, :].astype(BF)


def feed_back(g, w_reduce, w_expand, pull, u_out, bias_out, *outs):
    for n in range(0, u_out.shape[1], 256):
        part = mm_nt(g[...], w_reduce[n : n + 256, :]) * pull[:, n : n + 256]
        low = part.astype(BF)
        u_out[:, n : n + 256] = low
        bias_out[:, n : n + 256] = jnp.sum(low.astype(F32), axis=0, keepdims=True)
    rows = outs[0].shape[0]
    c = mm_nt(u_out[...], w_expand[...])
    for k in range(SEQ):
        outs[k][...] = c[k * rows : (k + 1) * rows, :].astype(BF)


def reduce_grad(idx, h, g, near, far, hold):
    deep, wide = near.shape[1:]
    for half in range(0, h.shape[1], deep):
        hold[half : half + deep, :] = mm_tn(h[:, half : half + deep], g[...]).astype(BF)
    for k in range(BLOCKS):
        piece = hold[rows_at(idx[k] // SEQ * deep, deep), rows_at(idx[k] % SEQ * wide, wide)]
        out = near if k < BLOCKS // 2 else far
        out[k % (BLOCKS // 2)] = piece


def outer_grad(idx, left, right, near, far):
    step = near.shape[1]
    for k in range(BLOCKS):
        piece = mm_tn(left[:, rows_at(idx[k] * step, step)], right[...]).astype(BF)
        out = near if k < BLOCKS // 2 else far
        out[k % (BLOCKS // 2)] = piece


def norm_pull(upper, normal, scale, gain):
    inner = upper * gain
    return scale * (
        inner
        - jnp.mean(inner, axis=-1, keepdims=True)
        - normal * jnp.mean(inner * normal, axis=-1, keepdims=True)
    )


def middle_back(part0, part1, part2, x, cot, factor, gain, grad_out, low_out, sums_out):
    upper = part0[...].astype(F32) + part1[...].astype(F32) + part2[...].astype(F32)
    normal, scale = standardize(x[...])
    upstream = cot[...].astype(F32) * factor[...]
    grad = upstream + norm_pull(upper, normal, scale, gain[...])
    low = grad.astype(BF)
    grad_out[...] = grad
    low_out[...] = low
    sums_out[0:1, :] = jnp.sum(upper * normal, axis=0, keepdims=True)
    sums_out[1:2, :] = jnp.sum(upper, axis=0, keepdims=True)
    sums_out[2:3, :] = jnp.sum(low.astype(F32), axis=0, keepdims=True)
    sums_out[3:4, :] = jnp.sum(upstream, axis=0, keepdims=True)


def attend_back(order, *refs):
    grads = refs[:SEQ]
    w, q_in, k_in, v_in, stat, key_mask, g_out, out, sums_out, hold = refs[SEQ:]
    rows = grads[0].shape[0]
    for k in range(SEQ):
        hold[k * rows : (k + 1) * rows, :] = grads[k][...].astype(F32)
    g_out[...] = hold[...].astype(BF)
    width = q_in.shape[1]
    size = width // (HEADS // SEQ)
    d_out = mm_nt(g_out[...], w[rows_at(order[0] * width, width), :]).astype(BF)
    q, key, value = q_in[...], k_in[...], v_in[...]
    valid = key_mask[...] > 0
    dq = dk = dv = None
    for h in range(HEADS // SEQ):
        lanes = head_lanes(width, h, size)
        q_h = jnp.where(lanes, q, jnp.zeros_like(q))
        d_h = jnp.where(lanes, d_out, jnp.zeros_like(d_out))
        logits = mm_nt(q_h, key)
        scores = jnp.where(valid, logits * size ** (-0.5), -1000000000.0)
        top = stat[:, h : h + 1]
        inverse = stat[:, HEADS // SEQ + h : HEADS // SEQ + h + 1]
        probs = jnp.exp(scores - top) * inverse
        prob_grad = mm_nt(d_h, value)
        center = jnp.sum(probs * prob_grad, axis=-1, keepdims=True)
        low = jnp.where(valid, probs * (prob_grad - center) * size ** (-0.5), 0.0).astype(BF)
        dv_h = mm_tn(probs.astype(BF), d_h)
        dk_h = mm_tn(low, q_h)
        dq_h = mm(low, jnp.where(lanes, key, jnp.zeros_like(key)))
        dq = dq_h if dq is None else dq + dq_h
        dk = dk_h if dk is None else dk + dk_h
        dv = dv_h if dv is None else dv + dv_h
    dq, dk, dv = dq.astype(BF), dk.astype(BF), dv.astype(BF)
    out[:, :width] = dq
    out[:, width : 2 * width] = dk
    out[:, 2 * width :] = dv
    sums_out[0:1, :] = jnp.sum(dq.astype(F32), axis=0, keepdims=True)
    sums_out[1:2, :] = jnp.sum(dv.astype(F32), axis=0, keepdims=True)


def output_grad(idx, order, g, *refs):
    o = refs[:SEQ]
    near, far, hold, turned = refs[SEQ:]
    rows = g.shape[0] // SEQ
    width = o[0].shape[1]
    step = near.shape[1]
    mine = g[:, rows_at(order[0] * width, width)].astype(F32)
    for m in range(SEQ):
        for k in range(SEQ):
            there = (k ^ m) * rows
            turned[k * rows : (k + 1) * rows, :] = mine[there : there + rows, :]
        hold[rows_at(order[m] * width, width), :] = mm_tn(o[m][...], turned[...].astype(BF)).astype(BF)
    for k in range(BLOCKS):
        out = near if k < BLOCKS // 2 else far
        out[k % (BLOCKS // 2)] = hold[rows_at(idx[k] * step, step), :]


def normed_back(d, w, normal, sums_out, *outs):
    rows = outs[0].shape[0]
    upper = mm_nt(d[...], w[...])
    for k in range(SEQ):
        outs[k][...] = upper[k * rows : (k + 1) * rows, :].astype(BF)
    sums_out[0:1, :] = jnp.sum(upper * normal[...].astype(F32), axis=0, keepdims=True)
    sums_out[1:2, :] = jnp.sum(upper, axis=0, keepdims=True)


def input_back(part0, part1, part2, x, grad, gain, out):
    upper = part0[...].astype(F32) + part1[...].astype(F32) + part2[...].astype(F32)
    normal, scale = standardize(x[...].astype(F32))
    out[...] = (grad[...] + norm_pull(upper, normal, scale, gain[...])).astype(BF)


def seq_swap(value, flip):
    return lax.ppermute(value, "seq", [(s, s ^ flip) for s in range(SEQ)])


def gather_seq(value):
    two = seq_swap(value, 2)
    one = seq_swap(value, 1)
    return [value, one, two, seq_swap(two, 1)]


def scatter_seq(parts):
    one = seq_swap(parts[1], 1)
    three = seq_swap(parts[3], 1)
    both = (parts[2].astype(F32) + three.astype(F32)).astype(BF)
    return [parts[0], one, seq_swap(both, 2)]


def dp_turn(value, data_count, turn):
    far = data_count // 2
    return lax.ppermute(
        value,
        "dp",
        [(z * 2 + y, (z + turn) % far * 2 + y) for z in range(far) for y in range(2)],
    )


def dp_swap(value, data_count):
    return lax.ppermute(value, "dp", [(d, d ^ 1) for d in range(data_count)])


def relative_order(data_count):
    if data_count != BLOCKS:
        return jnp.arange(BLOCKS, dtype=jnp.int32)
    me = lax.axis_index("dp")
    z, y = me // 2, me % 2
    turns = jnp.arange(BLOCKS // 2, dtype=jnp.int32)
    near = (z - turns + 4) % 4 * 2
    return jnp.concatenate([near + y, near + 1 - y]).astype(jnp.int32)


def gather_dp(value, data_count):
    if data_count != BLOCKS:
        whole = lax.all_gather(value, "dp", axis=0, tiled=True)
        return list(jnp.split(whole, BLOCKS, axis=0))
    near = [value] + [dp_turn(value, data_count, t) for t in (1, 2, 3)]
    return near + [dp_swap(v, data_count) for v in near]


def scatter_dp(near, far, data_count):
    if data_count != BLOCKS:
        whole = jnp.concatenate([near, far], axis=0)
        whole = whole.reshape((-1,) + whole.shape[2:])
        return lax.psum_scatter(whole, "dp", scatter_dimension=0, tiled=True).astype(F32)
    came = dp_swap(far, data_count)
    both = [(near[k].astype(F32) + came[k].astype(F32)).astype(BF) for k in range(BLOCKS // 2)]
    total = both[0].astype(F32)
    for t in (1, 2, 3):
        total = total + dp_turn(both[t], data_count, BLOCKS // 2 - t).astype(F32)
    return total


def regroup(value, data_count, back=False):
    per = data_count // SEQ
    pairs = []
    for i in range(data_count):
        for j in range(SEQ):
            source = i * SEQ + j
            target = ((i % per) * SEQ + j) * SEQ + i // per
            pairs.append((target, source) if back else (source, target))
    return lax.ppermute(value, ("dp", "seq"), pairs)


def reduce_blocks(value, data_count):
    if data_count == BLOCKS:
        return gather_dp(value, data_count)
    whole = lax.all_gather(value, "dp", axis=0, tiled=True)
    deep, wide = value.shape
    group = data_count // BLOCKS
    whole = whole.reshape(2, group, SEQ, deep, wide).transpose(0, 2, 1, 3, 4)
    return list(whole.reshape(BLOCKS, group * deep, wide))


def reduce_scatter_blocks(near, far, data_count):
    if data_count == BLOCKS:
        return scatter_dp(near, far, data_count)
    whole = jnp.concatenate([near, far], axis=0)
    group = data_count // BLOCKS
    deep, wide = whole.shape[1] // group, whole.shape[2]
    whole = whole.reshape(2, SEQ, group, deep, wide).transpose(0, 2, 1, 3, 4)
    whole = whole.reshape(-1, wide)
    return lax.psum_scatter(whole, "dp", scatter_dimension=0, tiled=True).astype(F32)


def local(
    block_input,
    cotangent,
    image_valid,
    token_valid,
    first_gain,
    first_shift,
    query_weight,
    query_bias,
    key_weight,
    value_weight,
    value_bias,
    output_weight,
    output_bias,
    second_gain,
    second_shift,
    expand_weight,
    expand_bias,
    reduce_weight,
    reduce_bias,
):
    data_count = lax.axis_size("dp")
    me = lax.axis_index("seq")
    rows, width = block_input.shape[1:]
    tokens = rows * SEQ
    part = width // SEQ
    deep = expand_weight.shape[1]
    idx = relative_order(data_count)
    order = jnp.stack([me ^ k for k in range(SEQ)]).astype(jnp.int32)

    vectors = (
        first_gain,
        first_shift,
        query_bias,
        value_bias,
        output_bias,
        second_gain,
        second_shift,
        reduce_bias,
        expand_bias,
    )
    lengths = [v.shape[0] for v in vectors]
    offsets = [sum(lengths[:i]) for i in range(len(lengths))]
    table = lax.all_gather(jnp.concatenate(vectors), ("dp", "seq"), axis=0, tiled=False)

    def vector(i):
        return table[:, offsets[i] : offsets[i] + lengths[i]].reshape(1, -1).astype(F32)

    gain_one, shift_one, bias_q, bias_v, bias_o, gain_two, shift_two, bias_r, bias_e = map(vector, range(9))

    def own_part(v, size):
        return lax.dynamic_slice_in_dim(v, me * size, size, 1)

    valid = token_valid.astype(F32).reshape(SEQ, rows)
    valid = jnp.concatenate([lax.dynamic_slice_in_dim(valid, order[k], 1, 0) for k in range(SEQ)], axis=1)
    factor = (valid * image_valid.astype(F32)[0]).reshape(tokens, 1)

    x = block_input[0]
    cot = cotangent[0]
    x_all = gather_seq(x)
    qkv_piece = jnp.concatenate([query_weight, key_weight, value_weight], axis=1)
    qkv_blocks = gather_dp(qkv_piece, data_count)
    output_blocks = gather_dp(output_weight, data_count)
    expand_blocks = gather_dp(expand_weight, data_count)
    reduce_own = regroup(reduce_weight, data_count)
    cot_all = gather_seq(cot)
    reduce_pieces = reduce_blocks(reduce_own, data_count)
    output_all = gather_seq(jnp.concatenate(output_blocks, axis=0))

    full = shape((tokens, width), BF)
    a, normal = kernel_call(
        norm_one, (full, full), *x_all, gain_one, shift_one, scratch=[pltpu.VMEM((tokens, width), F32)]
    )
    head = shape((tokens, part), BF)
    bias_qkv = jnp.concatenate(
        [own_part(bias_q, part), jnp.zeros((1, part), F32), own_part(bias_v, part)], axis=1
    )
    q, key, value, o, stat, w_qkv = kernel_call(
        attend,
        (head, head, head, head, shape((tokens, 128), F32), shape((width, 3 * part), BF)),
        idx,
        a,
        *qkv_blocks,
        bias_qkv,
        valid,
        flops=2 * tokens * part * (3 * width + 8 * tokens),
        vmem=44,
    )
    o_all = gather_seq(o)
    c, x_mid, w_o = kernel_call(
        middle,
        (full, shape((rows, width), F32), shape((width, width), BF)),
        idx,
        order,
        *o_all,
        *output_all,
        *x_all,
        bias_o,
        gain_two,
        shift_two,
        scratch=[pltpu.VMEM((tokens, width), F32)],
        flops=2 * tokens * width * width,
        vmem=44,
    )
    h, pull, w_e = kernel_call(
        expand,
        (shape((tokens, deep), BF), shape((tokens, deep), F32), shape((width, deep), BF)),
        idx,
        c,
        *expand_blocks,
        own_part(bias_e, deep),
        flops=2 * tokens * width * deep,
        vmem=44,
    )
    block = shape((rows, width), BF)
    *y_parts, w_r = kernel_call(
        reduce_part,
        (block, block, block, block, shape((deep, width), BF)),
        idx,
        h,
        *reduce_pieces,
        flops=2 * tokens * width * deep,
        vmem=44,
    )
    y0, y1, y2 = scatter_seq(y_parts)
    y = x_mid + bias_r + y0.astype(F32) + y1.astype(F32) + y2.astype(F32)
    block_output = y.astype(BF)[None]

    (g,) = kernel_call(mask_rows, (full,), *cot_all, factor, scratch=[pltpu.VMEM((tokens, width), F32)])
    du, sum_e, *c_parts = kernel_call(
        feed_back,
        (shape((tokens, deep), BF), shape((1, deep), F32), block, block, block, block),
        g,
        w_r,
        w_e,
        pull,
        flops=4 * tokens * width * deep,
        vmem=44,
    )
    c0, c1, c2 = scatter_seq(c_parts)
    half = BLOCKS // 2
    reduce_near, reduce_far = kernel_call(
        reduce_grad,
        (shape((half, deep // 2, part), BF),) * 2,
        idx,
        h,
        g,
        scratch=[pltpu.VMEM((deep, width), BF)],
        flops=2 * tokens * width * deep,
        vmem=44,
    )
    reduce_sum = reduce_scatter_blocks(reduce_near, reduce_far, data_count)
    reduce_weight_grad = regroup(reduce_sum.astype(BF), data_count, back=True).astype(F32)
    expand_near, expand_far = kernel_call(
        outer_grad,
        (shape((half, width // BLOCKS, deep), BF),) * 2,
        idx,
        c,
        du,
        flops=2 * tokens * width * deep,
        vmem=44,
    )
    expand_weight_grad = scatter_dp(expand_near, expand_far, data_count)
    mid_grad, branch, sums_mid = kernel_call(
        middle_back,
        (shape((rows, width), F32), block, shape((4, width), F32)),
        c0,
        c1,
        c2,
        x_mid,
        cot,
        factor[:rows],
        gain_two,
    )
    branch_all = gather_seq(branch)
    branch_full, dqkv, sums_qv = kernel_call(
        attend_back,
        (full, shape((tokens, 3 * part), BF), shape((2, part), F32)),
        order,
        *branch_all,
        w_o,
        q,
        key,
        value,
        stat,
        valid,
        scratch=[pltpu.VMEM((tokens, width), F32)],
        flops=2 * tokens * part * (width + 20 * tokens),
        vmem=48,
    )
    sums_in, *a_parts = kernel_call(
        normed_back,
        (shape((2, width), F32), block, block, block, block),
        dqkv,
        w_qkv,
        normal,
        flops=6 * tokens * width * part,
        vmem=44,
    )
    a0, a1, a2 = scatter_seq(a_parts)
    qkv_near, qkv_far = kernel_call(
        outer_grad,
        (shape((half, width // BLOCKS, 3 * part), BF),) * 2,
        idx,
        a,
        dqkv,
        flops=6 * tokens * width * part,
        vmem=44,
    )
    output_near, output_far = kernel_call(
        output_grad,
        (shape((half, width // BLOCKS, part), BF),) * 2,
        idx,
        order,
        branch_full,
        *o_all,
        scratch=[pltpu.VMEM((width, part), BF), pltpu.VMEM((tokens, part), F32)],
        flops=2 * tokens * width * part,
        vmem=44,
    )
    output_weight_grad = scatter_dp(output_near, output_far, data_count)
    qkv_grad = scatter_dp(qkv_near, qkv_far, data_count)

    def spread(v, size):
        return lax.dynamic_update_slice(jnp.zeros((1, size), F32), v, (0, me * v.shape[1]))

    sums = (
        sums_in[0:1],
        sums_in[1:2],
        spread(sums_qv[0:1], width),
        spread(sums_qv[1:2], width),
        sums_mid[2:3],
        sums_mid[0:1],
        sums_mid[1:2],
        sums_mid[3:4],
        spread(sum_e, SEQ * deep),
    )
    laid = jnp.concatenate([s.reshape(data_count * SEQ, -1) for s in sums], axis=1)
    vector_grads = lax.psum_scatter(laid, ("dp", "seq"), scatter_dimension=0, tiled=True)[0]

    def vector_grad(i):
        return vector_grads[offsets[i] : offsets[i] + lengths[i]]

    (input_gradient,) = kernel_call(input_back, (block,), a0, a1, a2, x, mid_grad, gain_one)
    return (
        block_output,
        input_gradient[None],
        vector_grad(0),
        vector_grad(1),
        qkv_grad[:, :part],
        vector_grad(2),
        qkv_grad[:, part : 2 * part],
        qkv_grad[:, 2 * part :],
        vector_grad(3),
        output_weight_grad,
        vector_grad(4),
        vector_grad(5),
        vector_grad(6),
        expand_weight_grad,
        vector_grad(8),
        reduce_weight_grad,
        vector_grad(7),
    )


def solution(mesh):
    vector = P(("dp", "seq"))
    matrix = P("dp", "seq")
    tokens = P("dp", "seq", None)
    return jax.shard_map(
        local,
        mesh=mesh,
        in_specs=(
            tokens,
            tokens,
            P("dp"),
            P(),
            vector,
            vector,
            matrix,
            vector,
            matrix,
            matrix,
            vector,
            matrix,
            vector,
            vector,
            vector,
            matrix,
            vector,
            matrix,
            vector,
        ),
        out_specs=(
            tokens,
            tokens,
            vector,
            vector,
            matrix,
            vector,
            matrix,
            matrix,
            vector,
            matrix,
            vector,
            vector,
            vector,
            matrix,
            vector,
            matrix,
            vector,
        ),
        check_vma=False,
    )
```

```python
import jax
import jax.numpy as jnp
from jax import lax
from jax.experimental import pallas as pl
from jax.experimental.pallas import tpu as pltpu
from jax.sharding import PartitionSpec as P

HEADS = 16
EPS = 1e-06
BF = jnp.bfloat16
F32 = jnp.float32
SEQ = 4
BLOCKS = 8
MIB = 1 << 20
GAIN_ONE, SHIFT_ONE, BIAS_Q, BIAS_V, BIAS_O, GAIN_TWO, SHIFT_TWO, BIAS_R = (
    slice(i, i + 1) for i in range(8)
)


def mm(a, b):
    return lax.dot_general(a, b, (((1,), (0,)), ((), ())), preferred_element_type=F32)


def mm_nt(a, b):
    return lax.dot_general(a, b, (((1,), (1,)), ((), ())), preferred_element_type=F32)


def mm_tn(a, b):
    return lax.dot_general(a, b, (((0,), (0,)), ((), ())), preferred_element_type=F32)


def standardize(values):
    center = values - jnp.mean(values, axis=-1, keepdims=True)
    scale = lax.rsqrt(jnp.mean(center * center, axis=-1, keepdims=True) + EPS)
    return center * scale, scale


def rows_at(start, size):
    return pl.ds(pl.multiple_of(start, size), size)


def kernel_call(body, outs, *args, scratch=(), flops=0, vmem=32):
    specs = [
        pl.BlockSpec(memory_space=pltpu.SMEM if a.dtype == jnp.int32 else pltpu.VMEM) for a in args
    ]
    moved = sum(a.size * a.dtype.itemsize for a in args)
    moved += sum(o.size * o.dtype.itemsize for o in outs)
    return pl.pallas_call(
        body,
        out_shape=tuple(outs),
        in_specs=specs,
        out_specs=tuple(pl.BlockSpec(memory_space=pltpu.VMEM) for _ in outs),
        scratch_shapes=list(scratch),
        compiler_params=pltpu.CompilerParams(vmem_limit_bytes=vmem * MIB),
        cost_estimate=pl.CostEstimate(flops=int(flops), bytes_accessed=int(moved), transcendentals=0),
    )(*args)


def shape(dims, dtype):
    return jax.ShapeDtypeStruct(tuple(dims), dtype)


def norm_one(x0, x1, x2, x3, table, a_out, n_out, hold):
    rows, width = x0.shape
    for k, ref in enumerate((x0, x1, x2, x3)):
        normal, _ = standardize(ref[...].astype(F32))
        hold[k * rows : (k + 1) * rows, :] = normal
    normal = hold[...]
    n_out[...] = normal.astype(BF)
    a_out[...] = (normal * table[GAIN_ONE, :width] + table[SHIFT_ONE, :width]).astype(BF)


def mask_rows(c0, c1, c2, c3, factor, g_out, hold):
    rows = c0.shape[0]
    for k, ref in enumerate((c0, c1, c2, c3)):
        hold[k * rows : (k + 1) * rows, :] = ref[...].astype(F32)
    g_out[...] = (hold[...] * factor[...]).astype(BF)


def head_lanes(width, head, size):
    lane = lax.broadcasted_iota(jnp.int32, (1, width), 1)
    return (lane >= head * size) & (lane < (head + 1) * size)


def stack_rows(idx, *refs):
    outs = refs[BLOCKS:]
    step = refs[0].shape[0]
    for k in range(BLOCKS):
        first = 0
        for out in outs:
            wide = out.shape[1]
            out[rows_at(idx[k] * step, step), :] = refs[k][:, first : first + wide]
            first += wide


def pack_hidden(order, w_expand, w_reduce, *outs):
    step, part = w_expand.shape[0], w_reduce.shape[1]
    half = part // 2
    deep = w_expand.shape[1] // 2
    quarter = w_reduce.shape[0] // SEQ
    for m in range(SEQ):
        outs[m][:step, :half] = w_expand[:, rows_at(order[m] * half, half)]
        outs[m][:step, half:] = w_expand[:, pl.ds(pl.multiple_of(deep + order[m] * half, half), half)]
        outs[m][step:, :] = w_reduce[rows_at(order[m] * quarter, quarter), :]


def join_hidden(order, p0, p1, p2, p3, e_out, r_out):
    step, part = e_out.shape[0], p0.shape[1]
    for m, ref in enumerate((p0, p1, p2, p3)):
        e_out[:, rows_at(order[m] * part, part)] = ref[:step, :]
        r_out[:, rows_at(order[m] * part, part)] = ref[step:, :]


def part_hidden(order, e0, e1, e2, r0, r1, r2, mine, *outs):
    step, part = e0.shape[0], outs[0].shape[1]
    for m in range(SEQ):
        lanes = rows_at(order[m] * part, part)
        e = e0[:, lanes].astype(F32) + e1[:, lanes].astype(F32) + e2[:, lanes].astype(F32)
        r = r0[:, lanes].astype(F32) + r1[:, lanes].astype(F32) + r2[:, lanes].astype(F32)
        if m == 0:
            mine[:step, :] = e
            mine[step:, :] = r
        else:
            outs[m - 1][:step, :] = e.astype(BF)
            outs[m - 1][step:, :] = r.astype(BF)


def place_hidden(order, p0, p1, p2, p3, e_out, r_out):
    step, part = e_out.shape[0], p0.shape[1]
    half = part // 2
    deep = e_out.shape[1] // 2
    quarter = r_out.shape[0] // SEQ
    for m, ref in enumerate((p0, p1, p2, p3)):
        e_out[:, rows_at(order[m] * half, half)] = ref[:step, :half].astype(F32)
        e_out[:, pl.ds(pl.multiple_of(deep + order[m] * half, half), half)] = ref[:step, half:].astype(F32)
        r_out[rows_at(order[m] * quarter, quarter), :] = ref[step:, :].astype(F32)


def attend(order, a, w, table, key_mask, q_out, k_out, v_out, o_out, stat_out):
    width = q_out.shape[1]
    qkv = mm(a[...], w[...])
    mine = rows_at(order[0] * width, width)
    q = (qkv[:, :width] + table[BIAS_Q, mine]).astype(BF)
    key = qkv[:, width : 2 * width].astype(BF)
    value = (qkv[:, 2 * width :] + table[BIAS_V, mine]).astype(BF)
    q_out[...] = q
    k_out[...] = key
    v_out[...] = value
    size = width // (HEADS // SEQ)
    valid = key_mask[...] > 0
    total = None
    for h in range(HEADS // SEQ):
        lanes = head_lanes(width, h, size)
        logits = mm_nt(jnp.where(lanes, q, jnp.zeros_like(q)), key)
        scores = jnp.where(valid, logits * size ** (-0.5), -1000000000.0)
        top = jnp.max(scores, axis=-1, keepdims=True)
        weights = jnp.exp(scores - top)
        inverse = 1.0 / jnp.sum(weights, axis=-1, keepdims=True)
        probs = (weights * inverse).astype(BF)
        mixed = mm(probs, jnp.where(lanes, value, jnp.zeros_like(value)))
        total = mixed if total is None else total + mixed
        stat_out[:, h : h + 1] = top
        stat_out[:, HEADS // SEQ + h : HEADS // SEQ + h + 1] = inverse
    o_out[...] = total.astype(BF)


def middle(order, *refs):
    o = refs[:SEQ]
    w = refs[SEQ : 2 * SEQ]
    x = refs[2 * SEQ : 3 * SEQ]
    table, c_out, x_out, w_out, hold = refs[3 * SEQ :]
    rows, full = x[0].shape
    width = o[0].shape[1]
    for m in range(SEQ):
        w_out[:, rows_at(order[m] * width, width)] = w[m][...]
    for k in range(SEQ):
        hold[k * rows : (k + 1) * rows, :] = x[k][...].astype(F32) + table[BIAS_O, :full]
    for m in range(SEQ):
        part = mm(o[m][...], w_out[rows_at(order[m] * width, width), :])
        for k in range(SEQ):
            there = (k ^ m) * rows
            hold[there : there + rows, :] += part[k * rows : (k + 1) * rows, :]
    x_out[...] = hold[0:rows, :]
    normal, _ = standardize(hold[...])
    c_out[...] = (normal * table[GAIN_TWO, :full] + table[SHIFT_TWO, :full]).astype(BF)


def expand(idx, order, c, *refs):
    pieces = refs[:BLOCKS]
    table, h_out, p_out, w_out = refs[BLOCKS:]
    step = pieces[0].shape[0]
    for k in range(BLOCKS):
        w_out[rows_at(idx[k] * step, step), :] = pieces[k][...]
    width = h_out.shape[1]
    group = width // BLOCKS
    bias = table[:, pl.ds(pl.multiple_of(w_out.shape[0] + order[0] * group, group), group)]
    chunk = 2 * group
    for n in range(0, width, chunk):
        r = n // group
        row = jnp.concatenate([bias[r : r + 1], bias[r + 1 : r + 2]], axis=1)
        u = mm(c[...], w_out[:, n : n + chunk]) + row
        cdf = 0.5 * (1.0 + lax.erf(u * (0.5**0.5)))
        density = jnp.exp(-0.5 * u * u) * 0.3989422804014327
        h_out[:, n : n + chunk] = (u * cdf).astype(BF)
        p_out[:, n : n + chunk] = cdf + u * density


def reduce_part(idx, h, *refs):
    pieces = refs[:BLOCKS]
    outs = refs[BLOCKS : BLOCKS + SEQ]
    w_out = refs[BLOCKS + SEQ]
    step = pieces[0].shape[0]
    for k in range(BLOCKS):
        w_out[rows_at(idx[k] * step, step), :] = pieces[k][...]
    y = mm(h[...], w_out[...])
    rows = outs[0].shape[0]
    for k in range(SEQ):
        outs[k][...] = y[k * rows : (k + 1) * rows, :].astype(BF)


def feed_back(g, w_reduce, w_expand, pull, u_out, bias_out, *outs):
    group = bias_out.shape[1]
    chunk = 2 * group
    for n in range(0, u_out.shape[1], chunk):
        part = mm_nt(g[...], w_reduce[n : n + chunk, :]) * pull[:, n : n + chunk]
        low = part.astype(BF)
        u_out[:, n : n + chunk] = low
        total = jnp.sum(low.astype(F32), axis=0, keepdims=True)
        bias_out[n // group : n // group + 1, :] = total[:, :group]
        bias_out[n // group + 1 : n // group + 2, :] = total[:, group:]
    rows = outs[0].shape[0]
    c = mm_nt(u_out[...], w_expand[...])
    for k in range(SEQ):
        outs[k][...] = c[k * rows : (k + 1) * rows, :].astype(BF)


def outer_grad(idx, left, right, *outs):
    step = outs[0].shape[0]
    for k in range(BLOCKS):
        outs[k][...] = mm_tn(left[:, rows_at(idx[k] * step, step)], right[...]).astype(BF)


def norm_pull(upper, normal, scale, gain):
    inner = upper * gain
    return scale * (
        inner
        - jnp.mean(inner, axis=-1, keepdims=True)
        - normal * jnp.mean(inner * normal, axis=-1, keepdims=True)
    )


def middle_back(part0, part1, part2, x, cot, factor, table, grad_out, low_out, sums_out):
    upper = part0[...].astype(F32) + part1[...].astype(F32) + part2[...].astype(F32)
    normal, scale = standardize(x[...])
    upstream = cot[...].astype(F32) * factor[...]
    grad = upstream + norm_pull(upper, normal, scale, table[GAIN_TWO, : x.shape[1]])
    low = grad.astype(BF)
    grad_out[...] = grad
    low_out[...] = low
    sums_out[0:1, :] = jnp.sum(upper * normal, axis=0, keepdims=True)
    sums_out[1:2, :] = jnp.sum(upper, axis=0, keepdims=True)
    sums_out[2:3, :] = jnp.sum(low.astype(F32), axis=0, keepdims=True)
    sums_out[3:4, :] = jnp.sum(upstream, axis=0, keepdims=True)


def attend_back(order, *refs):
    grads = refs[:SEQ]
    w, q_in, k_in, v_in, stat, key_mask, g_out, out, sums_out, hold = refs[SEQ:]
    rows = grads[0].shape[0]
    for k in range(SEQ):
        hold[k * rows : (k + 1) * rows, :] = grads[k][...].astype(F32)
    g_out[...] = hold[...].astype(BF)
    width = q_in.shape[1]
    size = width // (HEADS // SEQ)
    d_out = mm_nt(g_out[...], w[rows_at(order[0] * width, width), :]).astype(BF)
    q, key, value = q_in[...], k_in[...], v_in[...]
    valid = key_mask[...] > 0
    dq = dk = dv = None
    for h in range(HEADS // SEQ):
        lanes = head_lanes(width, h, size)
        q_h = jnp.where(lanes, q, jnp.zeros_like(q))
        d_h = jnp.where(lanes, d_out, jnp.zeros_like(d_out))
        logits = mm_nt(q_h, key)
        scores = jnp.where(valid, logits * size ** (-0.5), -1000000000.0)
        top = stat[:, h : h + 1]
        inverse = stat[:, HEADS // SEQ + h : HEADS // SEQ + h + 1]
        probs = jnp.exp(scores - top) * inverse
        prob_grad = mm_nt(d_h, value)
        center = jnp.sum(probs * prob_grad, axis=-1, keepdims=True)
        low = jnp.where(valid, probs * (prob_grad - center) * size ** (-0.5), 0.0).astype(BF)
        dv_h = mm_tn(probs.astype(BF), d_h)
        dk_h = mm_tn(low, q_h)
        dq_h = mm(low, jnp.where(lanes, key, jnp.zeros_like(key)))
        dq = dq_h if dq is None else dq + dq_h
        dk = dk_h if dk is None else dk + dk_h
        dv = dv_h if dv is None else dv + dv_h
    dq, dk, dv = dq.astype(BF), dk.astype(BF), dv.astype(BF)
    out[:, :width] = dq
    out[:, width : 2 * width] = dk
    out[:, 2 * width :] = dv
    sums_out[0:1, :] = jnp.sum(dq.astype(F32), axis=0, keepdims=True)
    sums_out[1:2, :] = jnp.sum(dv.astype(F32), axis=0, keepdims=True)


def attention_grads(idx, order, a, d, g, *refs):
    o = refs[:SEQ]
    outs = refs[SEQ : SEQ + BLOCKS]
    hold, turned = refs[SEQ + BLOCKS :]
    rows = g.shape[0] // SEQ
    width = o[0].shape[1]
    step = outs[0].shape[0]
    mine = g[:, rows_at(order[0] * width, width)].astype(F32)
    for m in range(SEQ):
        for k in range(SEQ):
            there = (k ^ m) * rows
            turned[k * rows : (k + 1) * rows, :] = mine[there : there + rows, :]
        hold[rows_at(order[m] * width, width), :] = mm_tn(o[m][...], turned[...].astype(BF)).astype(BF)
    for k in range(BLOCKS):
        at = rows_at(idx[k] * step, step)
        outs[k][:, : 3 * width] = mm_tn(a[:, at], d[...]).astype(BF)
        outs[k][:, 3 * width :] = hold[at, :]


def normed_back(d, w, normal, sums_out, *outs):
    rows = outs[0].shape[0]
    upper = mm_nt(d[...], w[...])
    for k in range(SEQ):
        outs[k][...] = upper[k * rows : (k + 1) * rows, :].astype(BF)
    sums_out[0:1, :] = jnp.sum(upper * normal[...].astype(F32), axis=0, keepdims=True)
    sums_out[1:2, :] = jnp.sum(upper, axis=0, keepdims=True)


def input_back(part0, part1, part2, x, grad, table, out):
    upper = part0[...].astype(F32) + part1[...].astype(F32) + part2[...].astype(F32)
    normal, scale = standardize(x[...].astype(F32))
    out[...] = (grad[...] + norm_pull(upper, normal, scale, table[GAIN_ONE, : x.shape[1]])).astype(BF)


def seq_swap(value, flip):
    return lax.ppermute(value, "seq", [(s, s ^ flip) for s in range(SEQ)])


def gather_seq(value):
    two = seq_swap(value, 2)
    one = seq_swap(value, 1)
    return [value, one, two, seq_swap(two, 1)]


def scatter_seq(parts):
    one = seq_swap(parts[1], 1)
    three = seq_swap(parts[3], 1)
    both = (parts[2].astype(F32) + three.astype(F32)).astype(BF)
    return [parts[0], one, seq_swap(both, 2)]


def ring_order(data_count):
    return list(range(0, data_count, 2)) + list(range(data_count - 1, 0, -2))


def ring_hop(value, data_count, step):
    ring = ring_order(data_count)
    pairs = [(ring[r], ring[(r + step) % data_count]) for r in range(data_count)]
    return lax.ppermute(value, "dp", pairs)


RELATIVE = (0, -1, -2, -3, 4, 1, 2, 3)


def relative_order(data_count):
    if data_count != BLOCKS:
        return jnp.arange(BLOCKS, dtype=jnp.int32)
    me = lax.axis_index("dp")
    z, y = me // 2, me % 2
    place = jnp.where(y == 0, z, BLOCKS - 1 - z)
    there = (place + jnp.array(RELATIVE, dtype=jnp.int32) + BLOCKS) % BLOCKS
    half = BLOCKS // 2
    return jnp.where(there < half, 2 * there, 2 * (BLOCKS - 1 - there) + 1).astype(jnp.int32)


def gather_dp(value, data_count):
    if data_count != BLOCKS:
        whole = lax.all_gather(value, "dp", axis=0, tiled=True)
        return list(jnp.split(whole, BLOCKS, axis=0))
    ahead, back = [], []
    left = right = value
    for k in range(BLOCKS // 2):
        left = ring_hop(left, data_count, 1)
        back.append(left)
        if k < BLOCKS // 2 - 1:
            right = ring_hop(right, data_count, -1)
            ahead.append(right)
    return [value] + back + ahead


def scatter_dp(pieces, data_count):
    if data_count != BLOCKS:
        whole = jnp.concatenate(pieces, axis=0)
        return [lax.psum_scatter(whole, "dp", scatter_dimension=0, tiled=True)]
    own = dict(zip(RELATIVE, pieces))
    left = ring_hop(own[4], data_count, 1)
    right = ring_hop(own[-3], data_count, -1)
    for d in (3, 2, 1):
        left = ring_hop(add(left, own[d]), data_count, 1)
        if d > 1:
            right = ring_hop(add(right, own[1 - d]), data_count, -1)
    return [own[0], left, right]


def add(a, b):
    return (a.astype(F32) + b.astype(F32)).astype(BF)


def dp_turn(value, data_count, turn):
    far = data_count // 2
    pairs = [(z * 2 + y, (z + turn) % far * 2 + y) for z in range(far) for y in range(2)]
    return lax.ppermute(value, "dp", pairs)


def sum_all(value, data_count):
    if data_count != BLOCKS:
        return lax.psum(value, ("dp", "seq"))
    value = value + seq_swap(value, 1)
    value = value + seq_swap(value, 2)
    value = value + lax.ppermute(value, "dp", [(d, d ^ 1) for d in range(data_count)])
    return value + dp_turn(value, data_count, 1) + dp_turn(value, data_count, 2) + dp_turn(value, data_count, 3)


def swap_hidden(order, w_expand, w_reduce, data_count):
    high, deep = w_expand.shape
    low, part = w_reduce.shape[0] // SEQ, w_reduce.shape[1]
    if data_count != BLOCKS:
        e = w_expand.reshape(high, -1, SEQ, low).transpose(2, 0, 1, 3).reshape(SEQ, high, part)
        both = jnp.concatenate([e, w_reduce.reshape(SEQ, low, part)], axis=1)
        both = lax.all_to_all(both, "seq", 0, 0).transpose(1, 0, 2).reshape(high + low, -1)
        return both[:high], both[high:]
    piece = shape((high + low, part), BF)
    sent = kernel_call(pack_hidden, (piece,) * SEQ, order, w_expand, w_reduce, vmem=8)
    sent = [sent[0]] + [seq_swap(sent[m], m) for m in range(1, SEQ)]
    return kernel_call(
        join_hidden, (shape((high, deep), BF), shape((low, SEQ * part), BF)), order, *sent, vmem=8
    )


def swap_hidden_back(order, e_terms, r_terms, e_shape, r_shape, data_count):
    high, deep = e_shape
    low, part = r_shape[0] // SEQ, r_shape[1]
    if data_count != BLOCKS:
        both = jnp.concatenate([e_terms[0], r_terms[0]], axis=0)
        both = both.reshape(high + low, SEQ, part).transpose(1, 0, 2)
        both = lax.all_to_all(both, "seq", 0, 0).astype(F32)
        e = both[:, :high].reshape(SEQ, high, -1, low).transpose(1, 2, 0, 3).reshape(e_shape)
        return e, both[:, high:].reshape(r_shape)
    piece = (high + low, part)
    mine, *sent = kernel_call(
        part_hidden, (shape(piece, F32),) + (shape(piece, BF),) * (SEQ - 1), order, *e_terms, *r_terms, vmem=8
    )
    sent = [seq_swap(sent[m - 1], m) for m in range(1, SEQ)]
    return kernel_call(
        place_hidden, (shape(e_shape, F32), shape(r_shape, F32)), order, mine, *sent, vmem=8
    )


def local(
    block_input,
    cotangent,
    image_valid,
    token_valid,
    first_gain,
    first_shift,
    query_weight,
    query_bias,
    key_weight,
    value_weight,
    value_bias,
    output_weight,
    output_bias,
    second_gain,
    second_shift,
    expand_weight,
    expand_bias,
    reduce_weight,
    reduce_bias,
):
    data_count = lax.axis_size("dp")
    me = lax.axis_index("seq")
    rows, width = block_input.shape[1:]
    tokens = rows * SEQ
    part = width // SEQ
    deep = expand_weight.shape[1]
    step = width // BLOCKS
    idx = relative_order(data_count)
    order = jnp.stack([me ^ k for k in range(SEQ)]).astype(jnp.int32)

    vectors = (
        first_gain,
        first_shift,
        query_bias,
        value_bias,
        output_bias,
        second_gain,
        second_shift,
        reduce_bias,
    )
    each = first_gain.shape[0]
    place = lax.axis_index("dp") * SEQ + me
    stacked = sum(
        jnp.pad(v.astype(F32)[None], ((i, len(vectors) - 1 - i), (0, 0))) for i, v in enumerate(vectors)
    )
    spots = lax.broadcasted_iota(jnp.int32, (each, width), 1) == place * each + lax.broadcasted_iota(
        jnp.int32, (each, width), 0
    )
    placed = jnp.dot(stacked.astype(BF), spots.astype(BF), preferred_element_type=F32)
    hidden = deep // BLOCKS
    bias_length = expand_bias.shape[0]
    bias_at = lax.axis_index("dp") * bias_length
    bias_at = (bias_at // hidden, me * hidden + bias_at % hidden)
    placed_bias = lax.dynamic_update_slice(
        jnp.zeros((BLOCKS, SEQ * hidden), F32), expand_bias.astype(F32)[None], bias_at
    )
    table = sum_all(jnp.concatenate([placed, placed_bias], axis=1), data_count)

    valid = token_valid.astype(F32).reshape(SEQ, rows)
    valid = jnp.concatenate([lax.dynamic_slice_in_dim(valid, order[k], 1, 0) for k in range(SEQ)], axis=1)
    factor = (valid * image_valid.astype(F32)[0]).reshape(tokens, 1)

    x = block_input[0]
    cot = cotangent[0]
    attention_piece = jnp.concatenate([query_weight, key_weight, value_weight, output_weight], axis=1)
    attention_blocks = gather_dp(attention_piece, data_count)
    expand_piece, reduce_piece = swap_hidden(order, expand_weight, reduce_weight, data_count)
    x_all = gather_seq(x)
    cot_all = gather_seq(cot)
    expand_blocks = gather_dp(expand_piece, data_count)
    reduce_blocks = gather_dp(reduce_piece, data_count)
    w_qkv, w_mine = kernel_call(
        stack_rows,
        (shape((width, 3 * part), BF), shape((width, part), BF)),
        idx,
        *attention_blocks,
        vmem=8,
    )
    w_all = gather_seq(w_mine)

    full = shape((tokens, width), BF)
    a, normal = kernel_call(
        norm_one, (full, full), *x_all, table, scratch=[pltpu.VMEM((tokens, width), F32)], vmem=16
    )
    head = shape((tokens, part), BF)
    q, key, value, o, stat = kernel_call(
        attend,
        (head, head, head, head, shape((tokens, 128), F32)),
        order,
        a,
        w_qkv,
        table,
        valid,
        flops=2 * tokens * part * (3 * width + 8 * tokens),
        vmem=24,
    )
    o_all = gather_seq(o)
    c, x_mid, w_o = kernel_call(
        middle,
        (full, shape((rows, width), F32), shape((width, width), BF)),
        order,
        *o_all,
        *w_all,
        *x_all,
        table,
        scratch=[pltpu.VMEM((tokens, width), F32)],
        flops=2 * tokens * width * width,
        vmem=24,
    )
    h, pull, w_e = kernel_call(
        expand,
        (shape((tokens, deep), BF), shape((tokens, deep), F32), shape((width, deep), BF)),
        idx,
        order,
        c,
        *expand_blocks,
        table,
        flops=2 * tokens * width * deep,
        vmem=24,
    )
    block = shape((rows, width), BF)
    *y_parts, w_r = kernel_call(
        reduce_part,
        (block, block, block, block, shape((deep, width), BF)),
        idx,
        h,
        *reduce_blocks,
        flops=2 * tokens * width * deep,
        vmem=24,
    )

    (g,) = kernel_call(
        mask_rows, (full,), *cot_all, factor, scratch=[pltpu.VMEM((tokens, width), F32)], vmem=16
    )
    du, sum_e, *c_parts = kernel_call(
        feed_back,
        (shape((tokens, deep), BF), shape((BLOCKS, hidden), F32), block, block, block, block),
        g,
        w_r,
        w_e,
        pull,
        flops=4 * tokens * width * deep,
        vmem=24,
    )
    c0, c1, c2 = scatter_seq(c_parts)
    reduce_pieces = kernel_call(
        outer_grad,
        (shape((deep // BLOCKS, width), BF),) * BLOCKS,
        idx,
        h,
        g,
        flops=2 * tokens * width * deep,
        vmem=24,
    )
    reduce_terms = scatter_dp(reduce_pieces, data_count)
    expand_pieces = kernel_call(
        outer_grad,
        (shape((step, deep), BF),) * BLOCKS,
        idx,
        c,
        du,
        flops=2 * tokens * width * deep,
        vmem=24,
    )
    expand_terms = scatter_dp(expand_pieces, data_count)
    mid_grad, branch, sums_mid = kernel_call(
        middle_back,
        (shape((rows, width), F32), block, shape((4, width), F32)),
        c0,
        c1,
        c2,
        x_mid,
        cot,
        factor[:rows],
        table,
        vmem=16,
    )
    branch_all = gather_seq(branch)
    y0, y1, y2 = scatter_seq(y_parts)
    y = x_mid + table[BIAS_R, :width] + y0.astype(F32) + y1.astype(F32) + y2.astype(F32)
    block_output = y.astype(BF)[None]
    branch_full, dqkv, sums_qv = kernel_call(
        attend_back,
        (full, shape((tokens, 3 * part), BF), shape((2, part), F32)),
        order,
        *branch_all,
        w_o,
        q,
        key,
        value,
        stat,
        valid,
        scratch=[pltpu.VMEM((tokens, width), F32)],
        flops=2 * tokens * part * (width + 20 * tokens),
        vmem=32,
    )
    sums_in, *a_parts = kernel_call(
        normed_back,
        (shape((2, width), F32), block, block, block, block),
        dqkv,
        w_qkv,
        normal,
        flops=6 * tokens * width * part,
        vmem=24,
    )
    a0, a1, a2 = scatter_seq(a_parts)
    attention_pieces = kernel_call(
        attention_grads,
        (shape((step, width), BF),) * BLOCKS,
        idx,
        order,
        a,
        dqkv,
        branch_full,
        *o_all,
        scratch=[pltpu.VMEM((width, part), BF), pltpu.VMEM((tokens, part), F32)],
        flops=8 * tokens * width * part,
        vmem=24,
    )
    attention_sum = sum(t.astype(F32) for t in scatter_dp(attention_pieces, data_count))

    expand_weight_grad, reduce_weight_grad = swap_hidden_back(
        order, expand_terms, reduce_terms, expand_weight.shape, reduce_weight.shape, data_count
    )

    def spread(v, size):
        return lax.dynamic_update_slice(jnp.zeros((1, size), F32), v, (0, me * v.shape[1]))

    sums = jnp.concatenate(
        [
            sums_in,
            spread(sums_qv[0:1], width),
            spread(sums_qv[1:2], width),
            sums_mid[2:3],
            sums_mid[0:2],
            sums_mid[3:4],
        ],
        axis=0,
    )
    bias_sums = lax.dynamic_update_slice(
        jnp.zeros((BLOCKS, SEQ * hidden), F32), sum_e, (0, me * hidden)
    )
    totals = sum_all(jnp.concatenate([sums, bias_sums], axis=1), data_count)
    grads = lax.dynamic_slice_in_dim(totals, place * each, each, 1)
    expand_bias_grad = lax.dynamic_slice(totals[:, width:], bias_at, (1, bias_length))[0]

    (input_gradient,) = kernel_call(input_back, (block,), a0, a1, a2, x, mid_grad, table, vmem=16)
    return (
        block_output,
        input_gradient[None],
        grads[0],
        grads[1],
        attention_sum[:, :part],
        grads[2],
        attention_sum[:, part : 2 * part],
        attention_sum[:, 2 * part : 3 * part],
        grads[3],
        attention_sum[:, 3 * part :],
        grads[4],
        grads[5],
        grads[6],
        expand_weight_grad,
        expand_bias_grad,
        reduce_weight_grad,
        grads[7],
    )


def solution(mesh):
    vector = P(("dp", "seq"))
    matrix = P("dp", "seq")
    tokens = P("dp", "seq", None)
    return jax.shard_map(
        local,
        mesh=mesh,
        in_specs=(
            tokens,
            tokens,
            P("dp"),
            P(),
            vector,
            vector,
            matrix,
            vector,
            matrix,
            matrix,
            vector,
            matrix,
            vector,
            vector,
            vector,
            matrix,
            vector,
            matrix,
            vector,
        ),
        out_specs=(
            tokens,
            tokens,
            vector,
            vector,
            matrix,
            vector,
            matrix,
            matrix,
            vector,
            matrix,
            vector,
            vector,
            vector,
            matrix,
            vector,
            matrix,
            vector,
        ),
        check_vma=False,
    )
```

```python
import jax
import jax.numpy as jnp
from jax import lax
from jax.experimental import pallas as pl
from jax.experimental.pallas import tpu as pltpu
from jax.sharding import PartitionSpec as P

HEADS = 16
EPS = 1e-06
BF = jnp.bfloat16
F32 = jnp.float32
SEQ = 4
BLOCKS = 8
RING = 8
MIB = 1 << 20
VMEM = {
    "pack_columns": 60,
    "pack_hidden": 56,
    "join_hidden": 2,
    "stack_rows": 4,
    "norm_one": 8,
    "attend": 10,
    "middle": 14,
    "expand": 8,
    "reduce_part": 8,
    "mask_rows": 4,
    "feed_back": 6,
    "feed_grads": 6,
    "add_two": 2,
    "middle_back": 6,
    "attend_back": 12,
    "normed_back": 6,
    "attention_grads": 5,
    "part_hidden": 2,
    "place_hidden": 3,
    "last": 6,
}
GAIN_ONE, SHIFT_ONE, BIAS_Q, BIAS_V, BIAS_O, GAIN_TWO, SHIFT_TWO, BIAS_R = (
    slice(i, i + 1) for i in range(8)
)


def mm(a, b):
    return lax.dot_general(a, b, (((1,), (0,)), ((), ())), preferred_element_type=F32)


def mm_nt(a, b):
    return lax.dot_general(a, b, (((1,), (1,)), ((), ())), preferred_element_type=F32)


def mm_tn(a, b):
    return lax.dot_general(a, b, (((0,), (0,)), ((), ())), preferred_element_type=F32)


def standardize(values):
    center = values - jnp.mean(values, axis=-1, keepdims=True)
    scale = lax.rsqrt(jnp.mean(center * center, axis=-1, keepdims=True) + EPS)
    return center * scale, scale


def rows_at(start, size):
    return pl.ds(pl.multiple_of(start, size), size)


def kernel_call(body, outs, *args, scratch=(), flops=0, far=()):
    specs = [
        pl.BlockSpec(memory_space=pltpu.SMEM if a.dtype == jnp.int32 else pltpu.VMEM) for a in args
    ]
    for i in far:
        specs[i] = pl.BlockSpec(memory_space=pl.ANY)
    moved = sum(a.size * a.dtype.itemsize for a in args)
    moved += sum(o.size * o.dtype.itemsize for o in outs)
    return pl.pallas_call(
        body,
        out_shape=tuple(outs),
        in_specs=specs,
        out_specs=tuple(pl.BlockSpec(memory_space=pltpu.VMEM) for _ in outs),
        scratch_shapes=list(scratch),
        compiler_params=pltpu.CompilerParams(vmem_limit_bytes=VMEM[body.__name__] * MIB),
        cost_estimate=pl.CostEstimate(flops=int(flops) * 5 + 1000000000, bytes_accessed=int(moved), transcendentals=0),
    )(*args)


def shape(dims, dtype):
    return jax.ShapeDtypeStruct(tuple(dims), dtype)


def norm_one(x0, x1, x2, x3, table, a_out, n_out, hold):
    rows, width = x0.shape
    for k, ref in enumerate((x0, x1, x2, x3)):
        normal, _ = standardize(ref[...].astype(F32))
        hold[k * rows : (k + 1) * rows, :] = normal
    normal = hold[...]
    n_out[...] = normal.astype(BF)
    a_out[...] = (normal * table[GAIN_ONE, :width] + table[SHIFT_ONE, :width]).astype(BF)


def mask_rows(c0, c1, c2, c3, factor, g_out, hold):
    rows = c0.shape[0]
    for k, ref in enumerate((c0, c1, c2, c3)):
        hold[k * rows : (k + 1) * rows, :] = ref[...].astype(F32)
    g_out[...] = (hold[...] * factor[...]).astype(BF)


def head_lanes(width, head, size):
    lane = lax.broadcasted_iota(jnp.int32, (1, width), 1)
    return (lane >= head * size) & (lane < (head + 1) * size)


def stack_rows(idx, *refs):
    outs = refs[BLOCKS + 1 :]
    step = refs[0].shape[0]
    for k in range(BLOCKS + 1):
        size = refs[k].shape[0]
        at = idx[min(k, BLOCKS - 1)] * step + (size if k == BLOCKS else 0)
        first = 0
        for out in outs:
            wide = out.shape[1]
            out[rows_at(at, size), :] = refs[k][:, first : first + wide]
            first += wide


def copy_all(copies):
    for copy in copies:
        copy.start()
    for copy in copies:
        copy.wait()


def pack_columns(w0, w1, w2, w3, out, sems):
    wide = w0.shape[1]
    copy_all(
        [
            pltpu.make_async_copy(w, out.at[:, i * wide : (i + 1) * wide], sems.at[i])
            for i, w in enumerate((w0, w1, w2, w3))
        ]
    )


def own_lanes(order, rows, wide, each):
    lane = lax.broadcasted_iota(jnp.int32, (rows, wide), 1)
    return (lane == order[0] * each + lax.broadcasted_iota(jnp.int32, (rows, wide), 0)).astype(BF)


def pack_hidden(order, w_expand, w_reduce, vectors, o0, o1, o2, o3, sems):
    step, part = w_expand.shape[0], w_reduce.shape[1]
    half = part // 2
    deep = w_expand.shape[1] // 2
    quarter = w_reduce.shape[0] // SEQ
    copies = []
    for m, out in enumerate((o0, o1, o2, o3)):
        one = rows_at(order[m] * half, half)
        two = pl.ds(pl.multiple_of(deep + order[m] * half, half), half)
        three = rows_at(order[m] * quarter, quarter)
        rows = slice(step, step + quarter)
        copies += [
            pltpu.make_async_copy(w_expand.at[:, one], out.at[:step, :half], sems.at[3 * m]),
            pltpu.make_async_copy(w_expand.at[:, two], out.at[:step, half:], sems.at[3 * m + 1]),
            pltpu.make_async_copy(w_reduce.at[three, :], out.at[rows, :], sems.at[3 * m + 2]),
        ]
    each = vectors.shape[1]
    placed = mm(vectors[...].astype(BF), own_lanes(order, each, part, each)).astype(BF)
    for out in (o0, o1, o2, o3):
        out[step + quarter :, :] = placed
    copy_all(copies)


def join_hidden(order, bias, p0, p1, p2, p3, out, table):
    part = p0.shape[1]
    rows = out.shape[0]
    count, wide = table.shape[0], bias.shape[1]
    total = None
    for m, ref in enumerate((p0, p1, p2, p3)):
        out[:, rows_at(order[m] * part, part)] = ref[:rows, :]
        block = ref[rows:, :wide].astype(F32)
        total = block if total is None else total + block
    table[...] = jnp.zeros_like(table)
    table[:, rows_at(order[SEQ] * wide, wide)] = total[:count]
    width = table.shape[1] - SEQ * wide
    row = lax.broadcasted_iota(jnp.int32, (count, wide), 0)
    lanes = pl.ds(pl.multiple_of(width + order[0] * wide, wide), wide)
    table[:, lanes] = jnp.where(row == order[SEQ], bias[...], 0.0)


def part_hidden(order, e0, e1, e2, mine, *outs):
    part = mine.shape[1]
    for m in range(SEQ):
        lanes = rows_at(order[m] * part, part)
        e = e0[:, lanes].astype(F32) + e1[:, lanes].astype(F32) + e2[:, lanes].astype(F32)
        if m == 0:
            mine[...] = e
        else:
            outs[m - 1][...] = e.astype(BF)


def place_hidden(order, p0, p1, p2, p3, e_out, r_out):
    step, part = e_out.shape[0], p0.shape[1]
    half = part // 2
    deep = e_out.shape[1] // 2
    quarter = r_out.shape[0] // SEQ
    for m, ref in enumerate((p0, p1, p2, p3)):
        e_out[:, rows_at(order[m] * half, half)] = ref[:step, :half].astype(F32)
        e_out[:, pl.ds(pl.multiple_of(deep + order[m] * half, half), half)] = ref[:step, half:].astype(F32)
        r_out[rows_at(order[m] * quarter, quarter), :] = ref[step:, :].astype(F32)


def attend(order, a, w, table, key_mask, out, o_out, stat_out):
    width = o_out.shape[1]
    qkv = mm(a[...], w[...])
    mine = rows_at(order[0] * width, width)
    q = (qkv[:, :width] + table[BIAS_Q, mine]).astype(BF)
    key = qkv[:, width : 2 * width].astype(BF)
    value = (qkv[:, 2 * width :] + table[BIAS_V, mine]).astype(BF)
    out[:, :width] = q
    out[:, width : 2 * width] = key
    out[:, 2 * width :] = value
    size = width // (HEADS // SEQ)
    valid = key_mask[...] > 0
    total = None
    for h in range(HEADS // SEQ):
        lanes = head_lanes(width, h, size)
        logits = mm_nt(jnp.where(lanes, q, jnp.zeros_like(q)), key)
        scores = jnp.where(valid, logits * size ** (-0.5), -1000000000.0)
        top = jnp.max(scores, axis=-1, keepdims=True)
        weights = jnp.exp(scores - top)
        inverse = 1.0 / jnp.sum(weights, axis=-1, keepdims=True)
        probs = (weights * inverse).astype(BF)
        mixed = mm(probs, jnp.where(lanes, value, jnp.zeros_like(value)))
        total = mixed if total is None else total + mixed
        stat_out[:, h : h + 1] = top
        stat_out[:, HEADS // SEQ + h : HEADS // SEQ + h + 1] = inverse
    o_out[...] = total.astype(BF)


def middle(order, *refs):
    o = refs[:SEQ]
    w_parts = refs[SEQ : 2 * SEQ]
    x = refs[2 * SEQ : 3 * SEQ]
    table, c_out, x_out, w_rows, hold, w = refs[3 * SEQ :]
    rows, full = x[0].shape
    width = o[0].shape[1]
    for m in range(SEQ):
        at = rows_at(order[m] * width, width)
        w[:, at] = w_parts[m][...]
        w_rows[:, at] = w_parts[m][rows_at(order[0] * width, width), :]
    for k in range(SEQ):
        hold[k * rows : (k + 1) * rows, :] = x[k][...].astype(F32) + table[BIAS_O, :full]
    for m in range(SEQ):
        part = mm(o[m][...], w[rows_at(order[m] * width, width), :])
        for k in range(SEQ):
            there = (k ^ m) * rows
            hold[there : there + rows, :] += part[k * rows : (k + 1) * rows, :]
    x_out[...] = hold[0:rows, :]
    normal, _ = standardize(hold[...])
    c_out[...] = (normal * table[GAIN_TWO, :full] + table[SHIFT_TWO, :full]).astype(BF)


def expand(idx, order, c, *refs):
    pieces = refs[:BLOCKS]
    table, h_out, p_out, w_out = refs[BLOCKS:]
    step = w_out.shape[0] // BLOCKS
    for k in range(BLOCKS):
        w_out[rows_at(idx[k] * step, step), :] = pieces[k][:step, :]
    width = h_out.shape[1]
    group = width // BLOCKS
    bias = table[:, pl.ds(pl.multiple_of(w_out.shape[0] + order[0] * group, group), group)]
    chunk = 2 * group
    for n in range(0, width, chunk):
        r = n // group
        row = jnp.concatenate([bias[r : r + 1], bias[r + 1 : r + 2]], axis=1)
        u = mm(c[...], w_out[:, n : n + chunk]) + row
        cdf = 0.5 * (1.0 + lax.erf(u * (0.5**0.5)))
        density = jnp.exp(-0.5 * u * u) * 0.3989422804014327
        h_out[:, n : n + chunk] = (u * cdf).astype(BF)
        p_out[:, n : n + chunk] = (cdf + u * density).astype(p_out.dtype)


def reduce_part(h, w, out):
    y = mm(h[...], w[...])
    rows = out.shape[1]
    for k in range(SEQ):
        out[k] = y[k * rows : (k + 1) * rows, :].astype(BF)


def feed_back(idx, g, w_expand, pull, *refs):
    pieces = refs[:BLOCKS]
    u_out, bias_out, w_out = refs[BLOCKS : BLOCKS + 3]
    outs = refs[BLOCKS + 3 :]
    step = w_out.shape[0] // BLOCKS
    for k in range(BLOCKS):
        w_out[rows_at(idx[k] * step, step), :] = pieces[k][pieces[k].shape[0] - step :, :]
    group = bias_out.shape[1]
    chunk = 2 * group
    for n in range(0, u_out.shape[1], chunk):
        part = mm_nt(g[...], w_out[n : n + chunk, :]) * pull[:, n : n + chunk].astype(F32)
        low = part.astype(BF)
        u_out[:, n : n + chunk] = low
        total = jnp.sum(low.astype(F32), axis=0, keepdims=True)
        bias_out[n // group : n // group + 1, :] = total[:, :group]
        bias_out[n // group + 1 : n // group + 2, :] = total[:, group:]
    rows = outs[0].shape[0]
    c = mm_nt(u_out[...], w_expand[...])
    for k in range(SEQ):
        outs[k][...] = c[k * rows : (k + 1) * rows, :].astype(BF)


def write_piece(outs, k, value):
    if k < BLOCKS - 1:
        outs[k][...] = value
    else:
        half = outs[k].shape[0]
        outs[k][...] = value[:half]
        outs[k + 1][...] = value[half:]


def feed_grads(idx, c, du, h, g, *outs):
    step = outs[0].shape[0] // 2
    for k in range(BLOCKS):
        at = rows_at(idx[k] * step, step)
        e = mm_tn(c[:, at], du[...]).astype(BF)
        r = mm_tn(h[:, at], g[...]).astype(BF)
        if k < BLOCKS - 1:
            outs[k][:step, :] = e
            outs[k][step:, :] = r
        else:
            outs[k][...] = e
            outs[k + 1][...] = r


def add_two(a, a_own, b, b_own, a_out, b_out):
    half = a.shape[0]
    rest = a_own.shape[0] - half
    a_out[:half, :] = (a[...].astype(F32) + a_own[:half, :].astype(F32)).astype(BF)
    b_out[rest:, :] = (b[...].astype(F32) + b_own[rest:, :].astype(F32)).astype(BF)
    if rest:
        a_out[half:, :] = a_own[half:, :]
        b_out[:rest, :] = b_own[:rest, :]


def norm_pull(upper, normal, scale, gain):
    inner = upper * gain
    return scale * (
        inner
        - jnp.mean(inner, axis=-1, keepdims=True)
        - normal * jnp.mean(inner * normal, axis=-1, keepdims=True)
    )


def middle_back(part0, part1, part2, x, cot, factor, table, grad_out, low_out, sums_out):
    upper = part0[...].astype(F32) + part1[...].astype(F32) + part2[...].astype(F32)
    normal, scale = standardize(x[...])
    upstream = cot[...].astype(F32) * factor[...]
    grad = upstream + norm_pull(upper, normal, scale, table[GAIN_TWO, : x.shape[1]])
    low = grad.astype(BF)
    grad_out[...] = grad
    low_out[...] = low
    sums_out[0:1, :] = jnp.sum(upper * normal, axis=0, keepdims=True)
    sums_out[1:2, :] = jnp.sum(upper, axis=0, keepdims=True)
    sums_out[2:3, :] = jnp.sum(low.astype(F32), axis=0, keepdims=True)
    sums_out[3:4, :] = jnp.sum(upstream, axis=0, keepdims=True)


def attend_back(order, *refs):
    grads = refs[:SEQ]
    w_rows, qkv, stat, key_mask, g_out, out, sums_out, hold = refs[SEQ:]
    rows = grads[0].shape[0]
    for k in range(SEQ):
        hold[k * rows : (k + 1) * rows, :] = grads[k][...].astype(F32)
    g_out[...] = hold[...].astype(BF)
    width = qkv.shape[1] // 3
    size = width // (HEADS // SEQ)
    d_out = mm_nt(g_out[...], w_rows[...]).astype(BF)
    q, key, value = (qkv[:, i * width : (i + 1) * width] for i in range(3))
    valid = key_mask[...] > 0
    dq = dk = dv = None
    for h in range(HEADS // SEQ):
        lanes = head_lanes(width, h, size)
        q_h = jnp.where(lanes, q, jnp.zeros_like(q))
        d_h = jnp.where(lanes, d_out, jnp.zeros_like(d_out))
        logits = mm_nt(q_h, key)
        scores = jnp.where(valid, logits * size ** (-0.5), -1000000000.0)
        top = stat[:, h : h + 1]
        inverse = stat[:, HEADS // SEQ + h : HEADS // SEQ + h + 1]
        probs = jnp.exp(scores - top) * inverse
        prob_grad = mm_nt(d_h, value)
        center = jnp.sum(probs * prob_grad, axis=-1, keepdims=True)
        low = jnp.where(valid, probs * (prob_grad - center) * size ** (-0.5), 0.0).astype(BF)
        dv_h = mm_tn(probs.astype(BF), d_h)
        dk_h = mm_tn(low, q_h)
        dq_h = mm(low, jnp.where(lanes, key, jnp.zeros_like(key)))
        dq = dq_h if dq is None else dq + dq_h
        dk = dk_h if dk is None else dk + dk_h
        dv = dv_h if dv is None else dv + dv_h
    dq, dk, dv = dq.astype(BF), dk.astype(BF), dv.astype(BF)
    out[:, :width] = dq
    out[:, width : 2 * width] = dk
    out[:, 2 * width :] = dv
    sums_out[0:1, :] = jnp.sum(dq.astype(F32), axis=0, keepdims=True)
    sums_out[1:2, :] = jnp.sum(dv.astype(F32), axis=0, keepdims=True)


def write_piece(outs, k, value):
    if k < BLOCKS - 1:
        outs[k][...] = value
    else:
        half = outs[k].shape[0]
        outs[k][...] = value[:half]
        outs[k + 1][...] = value[half:]


def attention_grads(idx, order, a, d, g, *refs):
    o = refs[:SEQ]
    outs = refs[SEQ : SEQ + BLOCKS + 1]
    hold, turned = refs[SEQ + BLOCKS + 1 :]
    rows = g.shape[0] // SEQ
    width = o[0].shape[1]
    step = outs[0].shape[0]
    mine = g[:, rows_at(order[0] * width, width)].astype(F32)
    for m in range(SEQ):
        for k in range(SEQ):
            there = (k ^ m) * rows
            turned[k * rows : (k + 1) * rows, :] = mine[there : there + rows, :]
        hold[rows_at(order[m] * width, width), :] = mm_tn(o[m][...], turned[...].astype(BF)).astype(BF)
    for k in range(BLOCKS):
        at = rows_at(idx[k] * step, step)
        value = mm_tn(a[:, at], d[...]).astype(BF)
        write_piece([out.at[:, : 3 * width] for out in outs], k, value)
        write_piece([out.at[:, 3 * width :] for out in outs], k, hold[at, :])


def normed_back(order, d, w, normal, y_part, sums_qv, sums_mid, sum_e, sums, o0, o1, o2, o3):
    rows, width = o0.shape[1:]
    part, wide = sums_qv.shape[1], sum_e.shape[1]
    upper = mm_nt(d[...], w[...])
    for k, out in enumerate((o0, o1, o2, o3)):
        out[0] = upper[k * rows : (k + 1) * rows, :].astype(BF)
        out[1] = y_part[k]
    sums[...] = jnp.zeros_like(sums)
    sums[GAIN_ONE, :width] = jnp.sum(upper * normal[...].astype(F32), axis=0, keepdims=True)
    sums[SHIFT_ONE, :width] = jnp.sum(upper, axis=0, keepdims=True)
    mine = rows_at(order[0] * part, part)
    sums[BIAS_Q, mine] = sums_qv[0:1, :]
    sums[BIAS_V, mine] = sums_qv[1:2, :]
    sums[BIAS_O, :width] = sums_mid[2:3, :]
    sums[GAIN_TWO, :width] = sums_mid[0:1, :]
    sums[SHIFT_TWO, :width] = sums_mid[1:2, :]
    sums[BIAS_R, :width] = sums_mid[3:4, :]
    sums[:, pl.ds(pl.multiple_of(width + order[0] * wide, wide), wide)] = sum_e[...]


def last(part0, part1, part2, x, grad, x_mid, table, grad_out, y_out):
    width = x.shape[1]
    upper = part0[0].astype(F32) + part1[0].astype(F32) + part2[0].astype(F32)
    normal, scale = standardize(x[...].astype(F32))
    grad_out[...] = (grad[...] + norm_pull(upper, normal, scale, table[GAIN_ONE, :width])).astype(BF)
    y = x_mid[...] + table[BIAS_R, :width] + part0[1].astype(F32)
    y_out[...] = (y + part1[1].astype(F32) + part2[1].astype(F32)).astype(BF)


def seq_swap(value, flip):
    return lax.ppermute(value, "seq", [(s, s ^ flip) for s in range(SEQ)])


def after(value, *others):
    return lax.optimization_barrier((value,) + others)[0]


def dp_flip(value, data_count, bit):
    return lax.ppermute(value, "dp", [(d, d ^ bit) for d in range(data_count)])


def add(a, b):
    return (a.astype(F32) + b.astype(F32)).astype(BF)


def ring_order(data_count):
    return list(range(0, data_count, 2)) + list(range(data_count - 1, 0, -2))


def ring_hop(value, data_count, step):
    ring = ring_order(data_count)
    pairs = [(ring[r], ring[(r + step) % data_count]) for r in range(data_count)]
    return lax.ppermute(value, "dp", pairs)


RELATIVE = (0, -1, -2, -3, 1, 2, 3, 4)


def relative_order(data_count):
    if data_count != RING:
        return jnp.arange(BLOCKS, dtype=jnp.int32)
    me = lax.axis_index("dp")
    z, y = me // 2, me % 2
    place = jnp.where(y == 0, z, BLOCKS - 1 - z)
    there = (place + jnp.array(RELATIVE, dtype=jnp.int32) + BLOCKS) % BLOCKS
    half = BLOCKS // 2
    return jnp.where(there < half, 2 * there, 2 * (BLOCKS - 1 - there) + 1).astype(jnp.int32)


@jax.tree_util.register_pytree_node_class
class Gather:
    def __init__(self, value, data_count, parts, back=(), front=()):
        self.value, self.data_count, self.parts = value, data_count, parts
        self.back, self.front = list(back), list(front)

    def tree_flatten(self):
        return (self.value, self.back, self.front), (self.data_count, self.parts)

    @classmethod
    def tree_unflatten(cls, aux, parts):
        return cls(parts[0], *aux, *parts[1:])

    def hop(self):
        if self.data_count != RING:
            if not self.back:
                whole = lax.all_gather(self.value, "dp", axis=0, tiled=False)
                parts = [p.reshape((BLOCKS, -1) + p.shape[2:]) for p in jnp.split(whole, self.parts, axis=1)]
                self.back = list(jnp.concatenate(parts, axis=1))
            return
        back, front = (self.back or [self.value])[-1], (self.front or [self.value])[-1]
        if len(self.back) == BLOCKS // 2 - 1:
            half = self.value.shape[0] // 2
            back, front = back[:half], front[half:]
        self.back.append(ring_hop(back, self.data_count, 1))
        self.front.append(ring_hop(front, self.data_count, -1))

    def blocks(self, last=(0, 1)):
        if self.data_count != RING:
            half = self.back[-1].shape[0] // 2
            halves = (self.back[-1][:half], self.back[-1][half:])
            return self.back[:-1] + [halves[i] for i in last]
        halves = (self.back[3], self.front[3])
        return [self.value] + self.back[:3] + self.front[:3] + [halves[i] for i in last]


@jax.tree_util.register_pytree_node_class
class Scatter:
    def __init__(self, pieces, data_count, parts, hops=0, left=None, right=None):
        self.pieces, self.data_count, self.parts = pieces, data_count, parts
        self.hops, self.left, self.right = hops, left, right

    def tree_flatten(self):
        return (self.pieces, self.left, self.right), (self.data_count, self.parts, self.hops)

    @classmethod
    def tree_unflatten(cls, aux, parts):
        return cls(parts[0], *aux, *parts[1:])

    def hop(self):
        n, self.hops = self.hops, self.hops + 1
        if self.data_count != RING:
            if n == 0:
                whole = jnp.concatenate(self.pieces, axis=0)
                wide = whole.shape[1]
                whole = whole.reshape(BLOCKS, self.parts, self.data_count // BLOCKS, -1, wide)
                whole = whole.transpose(0, 2, 1, 3, 4).reshape(-1, wide)
                self.left = lax.psum_scatter(whole, "dp", scatter_dimension=0, tiled=True)
            return self.left
        own = dict(zip(RELATIVE, self.pieces))
        left, right = self.left, self.right
        if n == 0:
            left, right = self.pieces[-2:]
        else:
            ahead, behind = own[4 - n], own[n - 4]
            outs = (shape(ahead.shape, BF),) * 2
            left, right = kernel_call(add_two, outs, left, ahead, right, behind)
        self.left = ring_hop(left, self.data_count, 1)
        self.right = ring_hop(right, self.data_count, -1)
        return left

    def terms(self):
        if self.data_count != RING:
            return [self.left, jnp.zeros_like(self.left), jnp.zeros_like(self.left)]
        return [self.pieces[0], self.left, self.right]


def trade(parts, data_count):
    return [parts[0]] + [seq_swap(parts[m], m) for m in range(1, SEQ)]


def pack_hidden_weights(order, w_expand, w_reduce, vectors, data_count):
    high, low, part = w_expand.shape[0], w_reduce.shape[0] // SEQ, w_reduce.shape[1]
    if data_count == RING:
        piece = shape((high + low + vectors.shape[0], part), BF)
        sems = [pltpu.SemaphoreType.DMA((3 * SEQ,))]
        args = (order, w_expand, w_reduce, vectors)
        return list(kernel_call(pack_hidden, (piece,) * SEQ, *args, far=(1, 2), scratch=sems))
    e = w_expand.reshape(high, -1, SEQ, low).transpose(2, 0, 1, 3).reshape(SEQ, high, part)
    both = jnp.concatenate([e, w_reduce.reshape(SEQ, low, part)], axis=1)
    return [lax.dynamic_index_in_dim(both, order[m], 0, False) for m in range(SEQ)]


def join_hidden_weights(order, bias, parts, table, high, low, data_count):
    part = parts[0].shape[1]
    if data_count == RING:
        return kernel_call(join_hidden, (shape((high + low, SEQ * part), BF), table), order, bias, *parts)
    both = jnp.zeros((high + low, SEQ * part), BF)
    for m in range(SEQ):
        both = lax.dynamic_update_slice(both, parts[m], (0, order[m] * part))
    return both, jnp.zeros(table.shape, table.dtype)


def part_hidden_grads(order, terms, part, data_count):
    if data_count == RING:
        piece = (terms[0].shape[0], part)
        outs = (shape(piece, F32),) + (shape(piece, BF),) * (SEQ - 1)
        return list(kernel_call(part_hidden, outs, order, *terms))
    return [lax.dynamic_slice_in_dim(terms[0], order[m] * part, part, 1) for m in range(SEQ)]


def place_hidden_grads(order, parts, e_shape, r_shape, data_count):
    if data_count == RING:
        outs = (shape(e_shape, F32), shape(r_shape, F32))
        return kernel_call(place_hidden, outs, order, *parts)
    high, low = e_shape[0], r_shape[0] // SEQ
    both = jnp.zeros((SEQ,) + parts[0].shape, F32)
    for m in range(SEQ):
        both = lax.dynamic_update_slice(both, parts[m].astype(F32)[None], (order[m], 0, 0))
    e = both[:, :high].reshape(SEQ, high, -1, low).transpose(1, 2, 0, 3).reshape(e_shape)
    return e, both[:, high:].reshape(r_shape)


def eight(deep, wide):
    return (shape((deep, wide), BF),) * (BLOCKS - 1) + (shape((deep // 2, wide), BF),) * 2


def sync(state):
    return lax.optimization_barrier(state)


def local(
    block_input,
    cotangent,
    image_valid,
    token_valid,
    first_gain,
    first_shift,
    query_weight,
    query_bias,
    key_weight,
    value_weight,
    value_bias,
    output_weight,
    output_bias,
    second_gain,
    second_shift,
    expand_weight,
    expand_bias,
    reduce_weight,
    reduce_bias,
):
    data_count = lax.axis_size("dp")
    ring = data_count == RING
    me = lax.axis_index("seq")
    rows, width = block_input.shape[1:]
    tokens = rows * SEQ
    part = width // SEQ
    deep = expand_weight.shape[1]
    step = width // BLOCKS
    hidden = deep // BLOCKS
    full = shape((tokens, width), BF)
    block = shape((rows, width), BF)
    s = {}
    s["idx"] = relative_order(data_count)
    dp = lax.axis_index("dp")
    s["order"] = jnp.stack([me ^ k for k in range(SEQ)] + [dp]).astype(jnp.int32)

    vectors = (
        first_gain,
        first_shift,
        query_bias,
        value_bias,
        output_bias,
        second_gain,
        second_shift,
        reduce_bias,
    )
    each = first_gain.shape[0]
    place = dp * SEQ + me
    count = len(vectors)
    stacked = sum(
        jnp.pad(v.astype(F32)[None], ((i, 2 * count - 1 - i), (0, 0))) for i, v in enumerate(vectors)
    )
    bias_row = expand_bias.astype(F32)[None]
    bias_length = expand_bias.shape[0]
    bias_at = dp * bias_length
    bias_at = (bias_at // hidden, me * hidden + bias_at % hidden)
    table = shape((count, width + SEQ * hidden), F32)

    valid = token_valid.astype(F32).reshape(SEQ, rows)
    valid = jnp.concatenate([lax.dynamic_slice_in_dim(valid, s["order"][k], 1, 0) for k in range(SEQ)], axis=1)
    s["valid"] = valid
    s["factor"] = (valid * image_valid.astype(F32)[0]).reshape(tokens, 1)

    attention_weights = (query_weight, key_weight, value_weight, output_weight)
    high, low = expand_weight.shape[0], reduce_weight.shape[0] // SEQ
    if ring:
        sems = [pltpu.SemaphoreType.DMA((SEQ,))]
        outs = (shape((step, width), BF),)
        (piece,) = kernel_call(pack_columns, outs, *attention_weights, far=(0, 1, 2, 3), scratch=sems)
    else:
        piece = jnp.concatenate(attention_weights, axis=1)
    s["attention"] = Gather(piece, data_count, 1)
    s["attention"].hop()
    stacked = after(stacked, piece)
    s["x"] = [block_input[0]]
    s["x"] += [seq_swap(s["x"][0], m) for m in (1, 2)]
    s["cot"] = [cotangent[0]]
    s["hidden"] = pack_hidden_weights(s["order"], expand_weight, reduce_weight, stacked, data_count)
    s = sync(s)

    s["attention"].hop()
    s["hidden"] = trade(s["hidden"], data_count)
    s = sync(s)

    s["attention"].hop()
    feed, s["table"] = join_hidden_weights(
        s["order"], bias_row, s.pop("hidden"), table, high, low, data_count
    )
    s["feed"] = Gather(feed, data_count, 2)
    s["x"].append(seq_swap(s["x"][2], 1))
    if ring:
        s["got"] = dp_flip(s["table"], data_count, 1)
    else:
        every = lax.broadcasted_iota(jnp.int32, (each, width), 1)
        every = every == place * each + lax.broadcasted_iota(jnp.int32, (each, width), 0)
        placed = jnp.dot(stacked[:count].astype(BF), every.astype(BF), preferred_element_type=F32)
        placed_bias = lax.dynamic_update_slice(jnp.zeros((count, SEQ * hidden), F32), bias_row, bias_at)
        s["table"] = lax.psum(jnp.concatenate([placed, placed_bias], axis=1), ("dp", "seq"))
    s = sync(s)

    s["attention"].hop()
    s["feed"].hop()
    if ring:
        s["table"] = s["table"] + s.pop("got")
        s["got"] = dp_flip(s["table"], data_count, 2)
    s = sync(s)

    s["feed"].hop()
    s["w_qkv"], w_mine = kernel_call(
        stack_rows,
        (shape((width, 3 * part), BF), shape((width, part), BF)),
        s["idx"],
        *s.pop("attention").blocks(),
    )
    s["w"] = [w_mine] + [seq_swap(w_mine, m) for m in (1, 2)]
    if ring:
        s["table"] = s["table"] + s.pop("got")
        s["table"] = s["table"] + dp_flip(s["table"], data_count, 4)
    s["a"], s["normal"] = kernel_call(
        norm_one, (full, full), *s["x"], s["table"], scratch=[pltpu.VMEM((tokens, width), F32)]
    )
    s["qkv"], o, s["stat"] = kernel_call(
        attend,
        (shape((tokens, 3 * part), BF), shape((tokens, part), BF), shape((tokens, 128), F32)),
        s["order"],
        s["a"],
        s["w_qkv"],
        s["table"],
        s["valid"],
        flops=2 * tokens * part * (3 * width + 8 * tokens),
    )
    s["o"] = [o]
    s = sync(s)

    s["feed"].hop()
    s["o"] += [seq_swap(s["o"][0], m) for m in (1, 2)]
    s["w"].append(seq_swap(s["w"][2], 1))
    s = sync(s)

    s["feed"].hop()
    s["o"].append(seq_swap(s["o"][2], 1))
    s["cot"] += [seq_swap(s["cot"][0], m) for m in (1, 2)]
    s["c"], s["x_mid"], s["w_rows"] = kernel_call(
        middle,
        (full, shape((rows, width), F32), shape((part, width), BF)),
        s["order"],
        *s["o"],
        *s.pop("w"),
        *s["x"],
        s["table"],
        scratch=[pltpu.VMEM((tokens, width), F32), pltpu.VMEM((width, width), BF)],
        flops=2 * tokens * width * width,
    )
    s["x"] = s["x"][0]
    s = sync(s)

    s["cot"].append(seq_swap(s["cot"][2], 1))
    (s["g"],) = kernel_call(
        mask_rows, (full,), *s["cot"], s["factor"], scratch=[pltpu.VMEM((tokens, width), F32)]
    )
    s["cot"] = s["cot"][0]
    s["h"], s["pull"], w_e = kernel_call(
        expand,
        (shape((tokens, deep), BF), shape((tokens, deep), BF), shape((width, deep), BF)),
        s["idx"],
        s["order"],
        s["c"],
        *s["feed"].blocks((0,)),
        s["table"],
        flops=2 * tokens * width * deep,
    )

    s["du"], s["sum_e"], w_r, *s["c_part"] = kernel_call(
        feed_back,
        (shape((tokens, deep), BF), shape((BLOCKS, hidden), F32), shape((deep, width), BF), block, block, block, block),
        s["idx"],
        s["g"],
        w_e,
        s.pop("pull"),
        *s.pop("feed").blocks((1,)),
        flops=4 * tokens * width * deep,
    )
    s["c_got"] = [seq_swap(s["c_part"][m], 1) for m in (1, 3)]
    (s["y_part"],) = kernel_call(
        reduce_part,
        (shape((SEQ, rows, width), BF),),
        s["h"],
        w_r,
        flops=2 * tokens * width * deep,
    )
    s = sync(s)

    s["c_two"] = seq_swap(add(s["c_part"][2], s["c_got"][1]), 2)
    pieces = kernel_call(
        feed_grads,
        eight(2 * step, deep),
        s["idx"],
        s.pop("c"),
        s.pop("du"),
        s.pop("h"),
        s.pop("g"),
        flops=4 * tokens * width * deep,
    )
    s["feed_grad"] = Scatter(list(pieces), data_count, 2)
    s["feed_grad"].hop()
    s = sync(s)

    s["mid_grad"], branch, s["sums_mid"] = kernel_call(
        middle_back,
        (shape((rows, width), F32), block, shape((4, width), F32)),
        s.pop("c_part")[0],
        s.pop("c_got")[0],
        s.pop("c_two"),
        s["x_mid"],
        s["cot"],
        s["factor"][:rows],
        s["table"],
    )
    s["branch"] = [branch] + [seq_swap(branch, m) for m in (1, 2)]
    s["feed_grad"].hop()
    s = sync(s)

    s["branch"].append(seq_swap(s["branch"][2], 1))
    s["feed_grad"].hop()
    s["branch_full"], s["dqkv"], s["sums_qv"] = kernel_call(
        attend_back,
        (full, shape((tokens, 3 * part), BF), shape((2, part), F32)),
        s["order"],
        *s.pop("branch"),
        s.pop("w_rows"),
        s.pop("qkv"),
        s.pop("stat"),
        s["valid"],
        scratch=[pltpu.VMEM((tokens, width), F32)],
        flops=2 * tokens * part * (width + 20 * tokens),
    )
    s = sync(s)

    sent = s["feed_grad"].hop()
    both = shape((2, rows, width), BF)
    s["sums"], *s["a_part"] = kernel_call(
        normed_back,
        (table, both, both, both, both),
        s["order"],
        after(s["dqkv"], sent),
        s.pop("w_qkv"),
        s.pop("normal"),
        s.pop("y_part"),
        s.pop("sums_qv"),
        s.pop("sums_mid"),
        s.pop("sum_e"),
        flops=6 * tokens * width * part,
    )
    s["a_got"] = [seq_swap(s["a_part"][m], 1) for m in (1, 3)]
    a_two = seq_swap(add(s["a_part"][2], s["a_got"][1]), 2)
    if ring:
        s["sums"] = s["sums"] + seq_swap(s["sums"], 1)
        s["sums"] = s["sums"] + seq_swap(s["sums"], 2)
        s["sums"] = s["sums"] + dp_flip(s["sums"], data_count, 1)
    else:
        s["sums"] = lax.psum(s["sums"], ("dp", "seq"))
    pieces = kernel_call(
        attention_grads,
        eight(step, width),
        s["idx"],
        s["order"],
        s.pop("a"),
        s.pop("dqkv"),
        s.pop("branch_full"),
        *s.pop("o"),
        scratch=[pltpu.VMEM((width, part), BF), pltpu.VMEM((tokens, part), F32)],
        flops=8 * tokens * width * part,
    )
    s["attention_grad"] = Scatter(list(pieces), data_count, 1)
    s = sync(s)

    s["attention_grad"].hop()
    s["hidden"] = part_hidden_grads(s["order"], s.pop("feed_grad").terms(), part, data_count)
    s = sync(s)

    s["attention_grad"].hop()
    s["hidden_got"] = [seq_swap(s["hidden"][2], 2)]
    if ring:
        s["got"] = dp_flip(s["sums"], data_count, 2)
    s = sync(s)

    s["attention_grad"].hop()
    s["hidden_got"] = [seq_swap(s["hidden"][1], 1)] + s["hidden_got"] + [seq_swap(s["hidden"][3], 3)]
    if ring:
        s["sums"] = s["sums"] + s.pop("got")
        s["got"] = dp_flip(s["sums"], data_count, 4)
    s["input_gradient"], s["y"] = kernel_call(
        last,
        (block, block),
        s["a_part"][0],
        s["a_got"][0],
        a_two,
        s["x"],
        s["mid_grad"],
        s["x_mid"],
        s["table"],
    )
    s = sync(s)

    s["attention_grad"].hop()
    if ring:
        s["sums"] = s["sums"] + s.pop("got")
    expand_weight_grad, reduce_weight_grad = place_hidden_grads(
        s["order"], s["hidden"][:1] + s["hidden_got"], expand_weight.shape, reduce_weight.shape, data_count
    )
    grads = lax.dynamic_slice_in_dim(s["sums"], place * each, each, 1)
    expand_bias_grad = lax.dynamic_slice(s["sums"][:, width:], bias_at, (1, bias_length))[0]
    attention_sum = sum(t.astype(F32) for t in s["attention_grad"].terms())
    return (
        s["y"][None],
        s["input_gradient"][None],
        grads[0],
        grads[1],
        attention_sum[:, :part],
        grads[2],
        attention_sum[:, part : 2 * part],
        attention_sum[:, 2 * part : 3 * part],
        grads[3],
        attention_sum[:, 3 * part :],
        grads[4],
        grads[5],
        grads[6],
        expand_weight_grad,
        expand_bias_grad,
        reduce_weight_grad,
        grads[7],
    )


def solution(mesh):
    vector = P(("dp", "seq"))
    matrix = P("dp", "seq")
    tokens = P("dp", "seq", None)
    return jax.shard_map(
        local,
        mesh=mesh,
        in_specs=(
            tokens,
            tokens,
            P("dp"),
            P(),
            vector,
            vector,
            matrix,
            vector,
            matrix,
            matrix,
            vector,
            matrix,
            vector,
            vector,
            vector,
            matrix,
            vector,
            matrix,
            vector,
        ),
        out_specs=(
            tokens,
            tokens,
            vector,
            vector,
            matrix,
            vector,
            matrix,
            matrix,
            vector,
            matrix,
            vector,
            vector,
            vector,
            matrix,
            vector,
            matrix,
            vector,
        ),
        check_vma=False,
    )
```

```python
import jax
import jax.numpy as jnp
from jax import lax
from jax.experimental import pallas as pl
from jax.experimental.pallas import tpu as pltpu
from jax.sharding import PartitionSpec as P

HEADS = 16
EPS = 1e-06
BF = jnp.bfloat16
F32 = jnp.float32
SEQ = 4
BLOCKS = 8
RING = 8
MIB = 1 << 20
VMEM = {
    "pack_columns": 60,
    "pack_hidden": 56,
    "join_hidden": 2,
    "stack_rows": 5,
    "norm_one": 8,
    "attend": 10,
    "middle": 14,
    "expand": 8,
    "reduce_part": 8,
    "mask_rows": 4,
    "feed_back": 6,
    "feed_grads": 6,
    "feed_grads_far": 4,
    "add_two": 2,
    "middle_back": 6,
    "attend_back": 12,
    "normed_back": 6,
    "attention_grads": 5,
    "part_hidden": 2,
    "place_hidden": 3,
    "last": 6,
    "finish": 3,
}
GAIN_ONE, SHIFT_ONE, BIAS_Q, BIAS_V, BIAS_O, GAIN_TWO, SHIFT_TWO, BIAS_R = (
    slice(i, i + 1) for i in range(8)
)


def mm(a, b):
    return lax.dot_general(a, b, (((1,), (0,)), ((), ())), preferred_element_type=F32)


def mm_nt(a, b):
    return lax.dot_general(a, b, (((1,), (1,)), ((), ())), preferred_element_type=F32)


def mm_tn(a, b):
    return lax.dot_general(a, b, (((0,), (0,)), ((), ())), preferred_element_type=F32)


def standardize(values):
    center = values - jnp.mean(values, axis=-1, keepdims=True)
    scale = lax.rsqrt(jnp.mean(center * center, axis=-1, keepdims=True) + EPS)
    return center * scale, scale


def rows_at(start, size):
    return pl.ds(pl.multiple_of(start, size), size)


def kernel_call(body, outs, *args, scratch=(), flops=0, far=()):
    specs = [
        pl.BlockSpec(memory_space=pltpu.SMEM if a.dtype == jnp.int32 else pltpu.VMEM) for a in args
    ]
    for i in far:
        specs[i] = pl.BlockSpec(memory_space=pl.ANY)
    moved = sum(a.size * a.dtype.itemsize for a in args)
    moved += sum(o.size * o.dtype.itemsize for o in outs)
    return pl.pallas_call(
        body,
        out_shape=tuple(outs),
        in_specs=specs,
        out_specs=tuple(pl.BlockSpec(memory_space=pltpu.VMEM) for _ in outs),
        scratch_shapes=list(scratch),
        compiler_params=pltpu.CompilerParams(vmem_limit_bytes=VMEM[body.__name__] * MIB),
        cost_estimate=pl.CostEstimate(flops=0, bytes_accessed=int(moved), transcendentals=0),
    )(*args)


def shape(dims, dtype):
    return jax.ShapeDtypeStruct(tuple(dims), dtype)


def norm_one(x0, x1, x2, x3, table, a_out, n_out, hold):
    rows, width = x0.shape
    for k, ref in enumerate((x0, x1, x2, x3)):
        normal, _ = standardize(ref[...].astype(F32))
        hold[k * rows : (k + 1) * rows, :] = normal
    normal = hold[...]
    n_out[...] = normal.astype(BF)
    a_out[...] = (normal * table[GAIN_ONE, :width] + table[SHIFT_ONE, :width]).astype(BF)


def mask_rows(c0, c1, c2, c3, factor, g_out, hold):
    rows = c0.shape[0]
    for k, ref in enumerate((c0, c1, c2, c3)):
        hold[k * rows : (k + 1) * rows, :] = ref[...].astype(F32)
    g_out[...] = (hold[...] * factor[...]).astype(BF)


def head_lanes(width, head, size):
    lane = lax.broadcasted_iota(jnp.int32, (1, width), 1)
    return (lane >= head * size) & (lane < (head + 1) * size)


def stack_rows(idx, order, *refs):
    w_qkv, w_low, w_high, table = refs[BLOCKS + 1 :]
    width, first = w_qkv.shape
    step = width // BLOCKS
    count = table.shape[0]
    wide = (table.shape[1] - width) // SEQ
    each = wide // SEQ
    table[...] = jnp.zeros_like(table)
    row = lax.broadcasted_iota(jnp.int32, (count, wide), 0)
    biases = jnp.zeros((count, wide), F32)
    for k in range(BLOCKS + 1):
        spot = idx[min(k, BLOCKS - 1)]
        at, size = spot * step, step
        if k >= BLOCKS - 1:
            size = step // 2
            at += size * (k - BLOCKS + 1)
        w_qkv[rows_at(at, size), :] = refs[k][:size, :first]

        @pl.when(at < width // 2)
        def _():
            w_low[rows_at(at, size), :] = refs[k][:size, first:]

        @pl.when(at >= width // 2)
        def _():
            w_high[rows_at(at - width // 2, size), :] = refs[k][:size, first:]

        if refs[k].shape[0] > size:
            below = refs[k][size:, :wide]
            placed = mm(below[:, :each], own_lanes(order, each, wide, each))
            table[:, rows_at(spot * wide, wide)] = placed[:count]
            biases = jnp.where(row == spot, below.astype(F32)[count : count + 1], biases)
    table[:, pl.ds(pl.multiple_of(width + order[0] * wide, wide), wide)] = biases


def copy_all(copies):
    for copy in copies:
        copy.start()
    for copy in copies:
        copy.wait()


def pack_columns(w0, w1, w2, w3, vectors, out, sems):
    high, wide = w0.shape
    copies = [
        pltpu.make_async_copy(w, out.at[:high, i * wide : (i + 1) * wide], sems.at[i])
        for i, w in enumerate((w0, w1, w2, w3))
    ]
    for copy in copies:
        copy.start()
    rows, each = vectors.shape
    out[high:, :each] = vectors[...].astype(BF)
    out[high:, each:] = jnp.zeros((rows, out.shape[1] - each), BF)
    for copy in copies:
        copy.wait()


def own_lanes(order, rows, wide, each):
    lane = lax.broadcasted_iota(jnp.int32, (rows, wide), 1)
    return (lane == order[0] * each + lax.broadcasted_iota(jnp.int32, (rows, wide), 0)).astype(BF)


def pack_hidden(order, w_expand, w_reduce, o0, o1, o2, o3, sems):
    step, part = w_expand.shape[0], w_reduce.shape[1]
    half = part // 2
    deep = w_expand.shape[1] // 2
    quarter = w_reduce.shape[0] // SEQ
    copies = []
    for m, out in enumerate((o0, o1, o2, o3)):
        one = rows_at(order[m] * half, half)
        two = pl.ds(pl.multiple_of(deep + order[m] * half, half), half)
        three = rows_at(order[m] * quarter, quarter)
        copies += [
            pltpu.make_async_copy(w_expand.at[:, one], out.at[:step, :half], sems.at[3 * m]),
            pltpu.make_async_copy(w_expand.at[:, two], out.at[:step, half:], sems.at[3 * m + 1]),
            pltpu.make_async_copy(w_reduce.at[three, :], out.at[step:, :], sems.at[3 * m + 2]),
        ]
    copy_all(copies)


def join_hidden(order, p0, p1, p2, p3, out):
    part = p0.shape[1]
    for m, ref in enumerate((p0, p1, p2, p3)):
        out[:, rows_at(order[m] * part, part)] = ref[...]


def part_hidden(order, e0, e1, e2, mine, *outs):
    part = mine.shape[1]
    for m in range(SEQ):
        lanes = rows_at(order[m] * part, part)
        e = e0[:, lanes].astype(F32) + e1[:, lanes].astype(F32) + e2[:, lanes].astype(F32)
        if m == 0:
            mine[...] = e
        else:
            outs[m - 1][...] = e.astype(BF)


def place_hidden(order, p0, p1, p2, p3, e_out, r_out):
    step, part = e_out.shape[0], p0.shape[1]
    half = part // 2
    deep = e_out.shape[1] // 2
    quarter = r_out.shape[0] // SEQ
    for m, ref in enumerate((p0, p1, p2, p3)):
        e_out[:, rows_at(order[m] * half, half)] = ref[:step, :half].astype(F32)
        e_out[:, pl.ds(pl.multiple_of(deep + order[m] * half, half), half)] = ref[:step, half:].astype(F32)
        r_out[rows_at(order[m] * quarter, quarter), :] = ref[step:, :].astype(F32)


def attend(order, a, w, table, key_mask, out, o_out, stat_out):
    width = o_out.shape[1]
    qkv = mm(a[...], w[...])
    mine = rows_at(order[0] * width, width)
    q = (qkv[:, :width] + table[BIAS_Q, mine]).astype(BF)
    key = qkv[:, width : 2 * width].astype(BF)
    value = (qkv[:, 2 * width :] + table[BIAS_V, mine]).astype(BF)
    out[:, :width] = q
    out[:, width : 2 * width] = key
    out[:, 2 * width :] = value
    size = width // (HEADS // SEQ)
    valid = key_mask[...] > 0
    total = None
    for h in range(HEADS // SEQ):
        lanes = head_lanes(width, h, size)
        logits = mm_nt(jnp.where(lanes, q, jnp.zeros_like(q)), key)
        scores = jnp.where(valid, logits * size ** (-0.5), -1000000000.0)
        top = jnp.max(scores, axis=-1, keepdims=True)
        weights = jnp.exp(scores - top)
        inverse = 1.0 / jnp.sum(weights, axis=-1, keepdims=True)
        probs = (weights * inverse).astype(BF)
        mixed = mm(probs, jnp.where(lanes, value, jnp.zeros_like(value)))
        total = mixed if total is None else total + mixed
        stat_out[:, h : h + 1] = top
        stat_out[:, HEADS // SEQ + h : HEADS // SEQ + h + 1] = inverse
    o_out[...] = total.astype(BF)


def middle(order, *refs):
    o = refs[:SEQ]
    w_low = refs[SEQ : 2 * SEQ]
    w_high = refs[2 * SEQ : 3 * SEQ]
    x = refs[3 * SEQ : 4 * SEQ]
    table, c_out, x_out, w_rows, hold, w = refs[4 * SEQ :]
    rows, full = x[0].shape
    width = o[0].shape[1]
    for m in range(SEQ):
        at = rows_at(order[m] * width, width)
        w[: full // 2, at] = w_low[m][...]
        w[full // 2 :, at] = w_high[m][...]
    w_rows[...] = w[rows_at(order[0] * width, width), :]
    for k in range(SEQ):
        hold[k * rows : (k + 1) * rows, :] = x[k][...].astype(F32) + table[BIAS_O, :full]
    for m in range(SEQ):
        part = mm(o[m][...], w[rows_at(order[m] * width, width), :])
        for k in range(SEQ):
            there = (k ^ m) * rows
            hold[there : there + rows, :] += part[k * rows : (k + 1) * rows, :]
    x_out[...] = hold[0:rows, :]
    normal, _ = standardize(hold[...])
    c_out[...] = (normal * table[GAIN_TWO, :full] + table[SHIFT_TWO, :full]).astype(BF)


def expand(idx, order, c, *refs):
    pieces = refs[:BLOCKS]
    table, h_out, p_out, w_out = refs[BLOCKS:]
    step = w_out.shape[0] // BLOCKS
    for k in range(BLOCKS):
        w_out[rows_at(idx[k] * step, step), :] = pieces[k][:step, :]
    width = h_out.shape[1]
    group = width // BLOCKS
    bias = table[:, pl.ds(pl.multiple_of(w_out.shape[0] + order[0] * group, group), group)]
    chunk = 2 * group
    for n in range(0, width, chunk):
        r = n // group
        row = jnp.concatenate([bias[r : r + 1], bias[r + 1 : r + 2]], axis=1)
        u = mm(c[...], w_out[:, n : n + chunk]) + row
        cdf = 0.5 * (1.0 + lax.erf(u * (0.5**0.5)))
        density = jnp.exp(-0.5 * u * u) * 0.3989422804014327
        h_out[:, n : n + chunk] = (u * cdf).astype(BF)
        p_out[:, n : n + chunk] = (cdf + u * density).astype(p_out.dtype)


def reduce_part(h, w, *outs):
    y = mm(h[...], w[...])
    rows = outs[0].shape[0]
    for k in range(SEQ):
        outs[k][...] = y[k * rows : (k + 1) * rows, :].astype(BF)


def feed_back(idx, g, w_expand, pull, *refs):
    pieces = refs[:BLOCKS]
    u_out, bias_out, w_out = refs[BLOCKS : BLOCKS + 3]
    outs = refs[BLOCKS + 3 :]
    step = w_out.shape[0] // BLOCKS
    for k in range(BLOCKS):
        w_out[rows_at(idx[k] * step, step), :] = pieces[k][pieces[k].shape[0] - step :, :]
    group = bias_out.shape[1]
    chunk = 2 * group
    for n in range(0, u_out.shape[1], chunk):
        part = mm_nt(g[...], w_out[n : n + chunk, :]) * pull[:, n : n + chunk].astype(F32)
        low = part.astype(BF)
        u_out[:, n : n + chunk] = low
        total = jnp.sum(low.astype(F32), axis=0, keepdims=True)
        bias_out[n // group : n // group + 1, :] = total[:, :group]
        bias_out[n // group + 1 : n // group + 2, :] = total[:, group:]
    rows = outs[0].shape[0]
    c = mm_nt(u_out[...], w_expand[...])
    for k in range(SEQ):
        outs[k][...] = c[k * rows : (k + 1) * rows, :].astype(BF)


def feed_grads(idx, c, du, h, g, *outs):
    step = outs[0].shape[0] // 2
    for k in range(BLOCKS - 1):
        at = rows_at(idx[k] * step, step)
        outs[k][:step, :] = mm_tn(c[:, at], du[...]).astype(BF)
        outs[k][step:, :] = mm_tn(h[:, at], g[...]).astype(BF)


def feed_grads_far(idx, c, du, h, g, e_out, r_out):
    at = rows_at(idx[BLOCKS - 1] * e_out.shape[0], e_out.shape[0])
    e_out[...] = mm_tn(c[:, at], du[...]).astype(BF)
    r_out[...] = mm_tn(h[:, at], g[...]).astype(BF)


def add_two(a, a_own, b, b_own, a_out, b_out):
    here = a.shape[0]
    rest = b_own.shape[0] - b.shape[0]
    a_out[:here, :] = (a[...].astype(F32) + a_own[:here, :].astype(F32)).astype(BF)
    b_out[rest:, :] = (b[...].astype(F32) + b_own[rest:, :].astype(F32)).astype(BF)
    if rest:
        a_out[here:, :] = a_own[here:, :]
        b_out[:rest, :] = b_own[:rest, :]


def norm_pull(upper, normal, scale, gain):
    inner = upper * gain
    return scale * (
        inner
        - jnp.mean(inner, axis=-1, keepdims=True)
        - normal * jnp.mean(inner * normal, axis=-1, keepdims=True)
    )


def middle_back(part0, part1, part2, x, cot, factor, table, grad_out, low_out, sums_out):
    upper = part0[...].astype(F32) + part1[...].astype(F32) + part2[...].astype(F32)
    normal, scale = standardize(x[...])
    upstream = cot[...].astype(F32) * factor[...]
    grad = upstream + norm_pull(upper, normal, scale, table[GAIN_TWO, : x.shape[1]])
    low = grad.astype(BF)
    grad_out[...] = grad
    low_out[...] = low
    sums_out[0:1, :] = jnp.sum(upper * normal, axis=0, keepdims=True)
    sums_out[1:2, :] = jnp.sum(upper, axis=0, keepdims=True)
    sums_out[2:3, :] = jnp.sum(low.astype(F32), axis=0, keepdims=True)
    sums_out[3:4, :] = jnp.sum(upstream, axis=0, keepdims=True)


def attend_back(order, *refs):
    grads = refs[:SEQ]
    w_rows, qkv, stat, key_mask, g_out, out, sums_out, hold = refs[SEQ:]
    rows = grads[0].shape[0]
    for k in range(SEQ):
        hold[k * rows : (k + 1) * rows, :] = grads[k][...].astype(F32)
    g_out[...] = hold[...].astype(BF)
    width = qkv.shape[1] // 3
    size = width // (HEADS // SEQ)
    d_out = mm_nt(g_out[...], w_rows[...]).astype(BF)
    q, key, value = (qkv[:, i * width : (i + 1) * width] for i in range(3))
    valid = key_mask[...] > 0
    dq = dk = dv = None
    for h in range(HEADS // SEQ):
        lanes = head_lanes(width, h, size)
        q_h = jnp.where(lanes, q, jnp.zeros_like(q))
        d_h = jnp.where(lanes, d_out, jnp.zeros_like(d_out))
        logits = mm_nt(q_h, key)
        scores = jnp.where(valid, logits * size ** (-0.5), -1000000000.0)
        top = stat[:, h : h + 1]
        inverse = stat[:, HEADS // SEQ + h : HEADS // SEQ + h + 1]
        probs = jnp.exp(scores - top) * inverse
        prob_grad = mm_nt(d_h, value)
        center = jnp.sum(probs * prob_grad, axis=-1, keepdims=True)
        low = jnp.where(valid, probs * (prob_grad - center) * size ** (-0.5), 0.0).astype(BF)
        dv_h = mm_tn(probs.astype(BF), d_h)
        dk_h = mm_tn(low, q_h)
        dq_h = mm(low, jnp.where(lanes, key, jnp.zeros_like(key)))
        dq = dq_h if dq is None else dq + dq_h
        dk = dk_h if dk is None else dk + dk_h
        dv = dv_h if dv is None else dv + dv_h
    dq, dk, dv = dq.astype(BF), dk.astype(BF), dv.astype(BF)
    out[:, :width] = dq
    out[:, width : 2 * width] = dk
    out[:, 2 * width :] = dv
    sums_out[0:1, :] = jnp.sum(dq.astype(F32), axis=0, keepdims=True)
    sums_out[1:2, :] = jnp.sum(dv.astype(F32), axis=0, keepdims=True)


def attention_grads(idx, order, a, d, g, sums, *refs):
    o = refs[:SEQ]
    outs = refs[SEQ : SEQ + BLOCKS + 1]
    hold, turned = refs[SEQ + BLOCKS + 1 :]
    rows = g.shape[0] // SEQ
    width = o[0].shape[1]
    full = hold.shape[0]
    step = full // BLOCKS
    mine = g[:, rows_at(order[0] * width, width)].astype(F32)
    for m in range(SEQ):
        for k in range(SEQ):
            there = (k ^ m) * rows
            turned[k * rows : (k + 1) * rows, :] = mine[there : there + rows, :]
        hold[rows_at(order[m] * width, width), :] = mm_tn(o[m][...], turned[...].astype(BF)).astype(BF)
    count, wide = sums.shape[0], step
    biases = sums[:, pl.ds(pl.multiple_of(full + order[0] * wide, wide), wide)]
    row = lax.broadcasted_iota(jnp.int32, biases.shape, 0)
    for k in range(BLOCKS):
        at = rows_at(idx[k] * step, step)
        value = mm_tn(a[:, at], d[...]).astype(BF)
        size = step if k < BLOCKS - 1 else step // 2
        outs[k][:size, : 3 * width] = value[:size]
        outs[k][:size, 3 * width :] = hold[rows_at(idx[k] * step, size), :]
        below = outs[k]
        if k == BLOCKS - 1:
            below = outs[k + 1]
            below[:size, : 3 * width] = value[size:]
            below[:size, 3 * width :] = hold[rows_at(idx[k] * step + size, size), :]
        if below.shape[0] > size:
            extra = below.shape[0] - size
            bias = jnp.sum(jnp.where(row == idx[k], biases, 0.0), axis=0, keepdims=True)
            bias = jnp.broadcast_to(bias, (extra - count, wide))
            block = jnp.concatenate([sums[:, rows_at(idx[k] * wide, wide)], bias], axis=0)
            below[size:, :wide] = block.astype(BF)
            below[size:, wide:] = jnp.zeros((extra, below.shape[1] - wide), BF)


def normed_back(order, d, w, normal, sums_qv, sums_mid, sum_e, sums, *outs):
    rows, width = outs[0].shape
    part, wide = sums_qv.shape[1], sum_e.shape[1]
    upper = mm_nt(d[...], w[...])
    for k in range(SEQ):
        outs[k][...] = upper[k * rows : (k + 1) * rows, :].astype(BF)
    sums[...] = jnp.zeros_like(sums)
    sums[GAIN_ONE, :width] = jnp.sum(upper * normal[...].astype(F32), axis=0, keepdims=True)
    sums[SHIFT_ONE, :width] = jnp.sum(upper, axis=0, keepdims=True)
    mine = rows_at(order[0] * part, part)
    sums[BIAS_Q, mine] = sums_qv[0:1, :]
    sums[BIAS_V, mine] = sums_qv[1:2, :]
    sums[BIAS_O, :width] = sums_mid[2:3, :]
    sums[GAIN_TWO, :width] = sums_mid[0:1, :]
    sums[SHIFT_TWO, :width] = sums_mid[1:2, :]
    sums[BIAS_R, :width] = sums_mid[3:4, :]
    sums[:, pl.ds(pl.multiple_of(width + order[0] * wide, wide), wide)] = sum_e[...]


def last(part0, part1, part2, x, grad, y0, y1, y2, x_mid, table, grad_out, y_out):
    width = x.shape[1]
    upper = part0[...].astype(F32) + part1[...].astype(F32) + part2[...].astype(F32)
    normal, scale = standardize(x[...].astype(F32))
    grad_out[...] = (grad[...] + norm_pull(upper, normal, scale, table[GAIN_ONE, :width])).astype(BF)
    y = x_mid[...] + table[BIAS_R, :width] + y0[...].astype(F32)
    y_out[...] = (y + y1[...].astype(F32) + y2[...].astype(F32)).astype(BF)


def finish(p0, p1, p2, w0, w1, w2, w3, sums, bias):
    high, part = w0.shape
    count, wide = sums.shape
    for i, out in enumerate((w0, w1, w2, w3)):
        at = slice(i * part, (i + 1) * part)
        out[...] = p0[:high, at].astype(F32) + p1[:high, at].astype(F32) + p2[:high, at].astype(F32)
    below = p0[high:, :wide].astype(F32) + p1[high:, :wide].astype(F32) + p2[high:, :wide].astype(F32)
    sums[...] = below[:count]
    bias[...] = below[count : count + 1]


def seq_swap(value, flip):
    return lax.ppermute(value, "seq", [(s, s ^ flip) for s in range(SEQ)])


def after(value, *others):
    return lax.optimization_barrier((value,) + others)[0]


def add(a, b):
    return (a.astype(F32) + b.astype(F32)).astype(BF)


def ring_order(data_count):
    return list(range(0, data_count, 2)) + list(range(data_count - 1, 0, -2))


def ring_hop(value, data_count, step):
    ring = ring_order(data_count)
    pairs = [(ring[r], ring[(r + step) % data_count]) for r in range(data_count)]
    return lax.ppermute(value, "dp", pairs)


RELATIVE = (0, -1, -2, -3, 1, 2, 3, 4)


def relative_order(data_count):
    if data_count != RING:
        return jnp.arange(BLOCKS, dtype=jnp.int32)
    me = lax.axis_index("dp")
    z, y = me // 2, me % 2
    place = jnp.where(y == 0, z, BLOCKS - 1 - z)
    there = (place + jnp.array(RELATIVE, dtype=jnp.int32) + BLOCKS) % BLOCKS
    half = BLOCKS // 2
    return jnp.where(there < half, 2 * there, 2 * (BLOCKS - 1 - there) + 1).astype(jnp.int32)


@jax.tree_util.register_pytree_node_class
class Gather:
    def __init__(self, value, data_count, parts, cut, back=(), front=()):
        self.value, self.data_count, self.parts, self.cut = value, data_count, parts, cut
        self.back, self.front = list(back), list(front)

    def tree_flatten(self):
        return (self.value, self.back, self.front), (self.data_count, self.parts, self.cut)

    @classmethod
    def tree_unflatten(cls, aux, parts):
        return cls(parts[0], *aux, *parts[1:])

    def hop(self):
        if self.data_count != RING:
            if not self.back:
                whole = lax.all_gather(self.value, "dp", axis=0, tiled=False)
                parts = [p.reshape((BLOCKS, -1) + p.shape[2:]) for p in jnp.split(whole, self.parts, axis=1)]
                self.back = list(jnp.concatenate(parts, axis=1))
            return
        back, front = (self.back or [self.value])[-1], (self.front or [self.value])[-1]
        if len(self.back) == BLOCKS // 2 - 1:
            back, front = back[: self.cut], front[self.cut :]
        self.back.append(ring_hop(back, self.data_count, 1))
        self.front.append(ring_hop(front, self.data_count, -1))

    def blocks(self, last=(0, 1)):
        if self.data_count != RING:
            halves = (self.back[-1][: self.cut], self.back[-1][self.cut :])
            return self.back[:-1] + [halves[i] for i in last]
        halves = (self.back[3], self.front[3])
        return [self.value] + self.back[:3] + self.front[:3] + [halves[i] for i in last]


@jax.tree_util.register_pytree_node_class
class Scatter:
    def __init__(self, pieces, data_count, parts, hops=0, left=None, right=None):
        self.pieces, self.data_count, self.parts = pieces, data_count, parts
        self.hops, self.left, self.right = hops, left, right

    def tree_flatten(self):
        return (self.pieces, self.left, self.right), (self.data_count, self.parts, self.hops)

    @classmethod
    def tree_unflatten(cls, aux, parts):
        return cls(parts[0], *aux, *parts[1:])

    def hop(self):
        n, self.hops = self.hops, self.hops + 1
        if self.data_count != RING:
            if n == 0:
                whole = jnp.concatenate(self.pieces, axis=0)
                wide = whole.shape[1]
                whole = whole.reshape(BLOCKS, self.parts, self.data_count // BLOCKS, -1, wide)
                whole = whole.transpose(0, 2, 1, 3, 4).reshape(-1, wide)
                self.left = lax.psum_scatter(whole, "dp", scatter_dimension=0, tiled=True)
            return self.left
        own = dict(zip(RELATIVE, self.pieces))
        left, right = self.left, self.right
        if n == 0:
            left, right = self.pieces[-2:]
        else:
            ahead, behind = own[4 - n], own[n - 4]
            outs = (shape(ahead.shape, BF),) * 2
            left, right = kernel_call(add_two, outs, left, ahead, right, behind)
        self.left = ring_hop(left, self.data_count, 1)
        self.right = ring_hop(right, self.data_count, -1)
        return left

    def terms(self):
        if self.data_count != RING:
            return [self.left, jnp.zeros_like(self.left), jnp.zeros_like(self.left)]
        return [self.pieces[0], self.left, self.right]


def sum_slot(value):
    one, two, three = (seq_swap(value, m) for m in range(1, SEQ))
    return value + one + two + three


def trade(parts, data_count):
    return [parts[0]] + [seq_swap(parts[m], m) for m in range(1, SEQ)]


def pack_hidden_weights(order, w_expand, w_reduce, data_count):
    high, low, part = w_expand.shape[0], w_reduce.shape[0] // SEQ, w_reduce.shape[1]
    if data_count == RING:
        piece = shape((high + low, part), BF)
        sems = [pltpu.SemaphoreType.DMA((3 * SEQ,))]
        return list(
            kernel_call(pack_hidden, (piece,) * SEQ, order, w_expand, w_reduce, far=(1, 2), scratch=sems)
        )
    e = w_expand.reshape(high, -1, SEQ, low).transpose(2, 0, 1, 3).reshape(SEQ, high, part)
    both = jnp.concatenate([e, w_reduce.reshape(SEQ, low, part)], axis=1)
    return [lax.dynamic_index_in_dim(both, order[m], 0, False) for m in range(SEQ)]


def join_hidden_weights(order, parts, data_count):
    rows, part = parts[0].shape
    if data_count == RING:
        return kernel_call(join_hidden, (shape((rows, SEQ * part), BF),), order, *parts)[0]
    both = jnp.zeros((rows, SEQ * part), BF)
    for m in range(SEQ):
        both = lax.dynamic_update_slice(both, parts[m], (0, order[m] * part))
    return both


def part_hidden_grads(order, terms, part, data_count):
    if data_count == RING:
        piece = (terms[0].shape[0], part)
        outs = (shape(piece, F32),) + (shape(piece, BF),) * (SEQ - 1)
        return list(kernel_call(part_hidden, outs, order, *terms))
    return [lax.dynamic_slice_in_dim(terms[0], order[m] * part, part, 1) for m in range(SEQ)]


def place_hidden_grads(order, parts, e_shape, r_shape, data_count):
    if data_count == RING:
        outs = (shape(e_shape, F32), shape(r_shape, F32))
        return kernel_call(place_hidden, outs, order, *parts)
    high, low = e_shape[0], r_shape[0] // SEQ
    both = jnp.zeros((SEQ,) + parts[0].shape, F32)
    for m in range(SEQ):
        both = lax.dynamic_update_slice(both, parts[m].astype(F32)[None], (order[m], 0, 0))
    e = both[:, :high].reshape(SEQ, high, -1, low).transpose(1, 2, 0, 3).reshape(e_shape)
    return e, both[:, high:].reshape(r_shape)


def eight(deep, wide):
    return (shape((deep, wide), BF),) * (BLOCKS - 1) + (shape((deep // 2, wide), BF),) * 2


def sync(state):
    return lax.optimization_barrier(state)


def local(
    block_input,
    cotangent,
    image_valid,
    token_valid,
    first_gain,
    first_shift,
    query_weight,
    query_bias,
    key_weight,
    value_weight,
    value_bias,
    output_weight,
    output_bias,
    second_gain,
    second_shift,
    expand_weight,
    expand_bias,
    reduce_weight,
    reduce_bias,
):
    data_count = lax.axis_size("dp")
    ring = data_count == RING
    me = lax.axis_index("seq")
    rows, width = block_input.shape[1:]
    tokens = rows * SEQ
    part = width // SEQ
    deep = expand_weight.shape[1]
    step = width // BLOCKS
    full = shape((tokens, width), BF)
    block = shape((rows, width), BF)
    s = {}
    s["idx"] = relative_order(data_count)
    dp = lax.axis_index("dp")
    s["order"] = jnp.stack([me ^ k for k in range(SEQ)] + [dp]).astype(jnp.int32)

    vectors = (
        first_gain,
        first_shift,
        query_bias,
        value_bias,
        output_bias,
        second_gain,
        second_shift,
        reduce_bias,
    )
    each = first_gain.shape[0]
    place = dp * SEQ + me
    count = len(vectors)
    group = deep // BLOCKS
    bias_row = expand_bias.astype(F32)[None]
    stacked = sum(
        jnp.pad(v.astype(F32)[None], ((i, 2 * count - 1 - i), (0, group - v.shape[0])))
        for i, v in enumerate(vectors + (expand_bias,))
    )
    bias_length = expand_bias.shape[0]
    bias_at = dp * bias_length
    bias_at = (bias_at // group, me * group + bias_at % group)
    table = shape((count, width + SEQ * group), F32)

    valid = token_valid.astype(F32).reshape(SEQ, rows)
    valid = jnp.concatenate([lax.dynamic_slice_in_dim(valid, s["order"][k], 1, 0) for k in range(SEQ)], axis=1)
    s["valid"] = valid
    s["factor"] = (valid * image_valid.astype(F32)[0]).reshape(tokens, 1)

    attention_weights = (query_weight, key_weight, value_weight, output_weight)
    extra = stacked.shape[0] if ring else 0
    if ring:
        sems = [pltpu.SemaphoreType.DMA((SEQ,))]
        outs = (shape((step + extra, width), BF),)
        args = attention_weights + (stacked,)
        (piece,) = kernel_call(pack_columns, outs, *args, far=(0, 1, 2, 3), scratch=sems)
    else:
        piece = jnp.concatenate(attention_weights, axis=1)
    s["attention"] = Gather(piece, data_count, 1, step // 2)
    s["attention"].hop()
    s["x"] = [block_input[0]]
    s["x"] += [seq_swap(s["x"][0], m) for m in (1, 2)]
    s["cot"] = [cotangent[0]]
    s["hidden"] = pack_hidden_weights(s["order"], expand_weight, reduce_weight, data_count)
    s = sync(s)

    s["attention"].hop()
    hidden = s.pop("hidden")
    s["hidden"] = [hidden[0]] + [seq_swap(hidden[m], m) for m in (1, 2)]
    s["hidden_last"] = hidden[3]
    s = sync(s)

    s["attention"].hop()
    s["hidden"].append(seq_swap(s.pop("hidden_last"), 3))
    s["x"].append(seq_swap(s["x"][2], 1))
    s = sync(s)

    s["attention"].hop()
    s["cot"].append(seq_swap(s["cot"][0], 1))
    feed = join_hidden_weights(s["order"], s.pop("hidden"), data_count)
    s["feed"] = Gather(feed, data_count, 2, step)
    s = sync(s)

    s["feed"].hop()
    half = shape((width // 2, part), BF)
    s["w_qkv"], w_low, w_high, s["table"] = kernel_call(
        stack_rows,
        (shape((width, 3 * part), BF), half, half, table),
        s["idx"],
        s["order"],
        *s.pop("attention").blocks(),
    )
    s["w_low"], s["w_high"] = [w_low], [w_high]
    s["w_low"] += [seq_swap(after(w_low, s["w_qkv"]), m) for m in (1, 2)]
    if ring:
        s["table"] = sum_slot(s["table"])
    else:
        every = lax.broadcasted_iota(jnp.int32, (each, width), 1)
        every = every == place * each + lax.broadcasted_iota(jnp.int32, (each, width), 0)
        placed = jnp.dot(stacked[:count, :each].astype(BF), every.astype(BF), preferred_element_type=F32)
        placed_bias = lax.dynamic_update_slice(
            jnp.zeros((count, table.shape[1] - width), F32), bias_row, bias_at
        )
        s["table"] = lax.psum(jnp.concatenate([placed, placed_bias], axis=1), ("dp", "seq"))
    s = sync(s)

    s["feed"].hop()
    s["w_high"] += [seq_swap(s["w_high"][0], m) for m in (1, 2)]
    s["a"], s["normal"] = kernel_call(
        norm_one, (full, full), *s["x"], s["table"], scratch=[pltpu.VMEM((tokens, width), F32)]
    )
    s["qkv"], o, s["stat"] = kernel_call(
        attend,
        (shape((tokens, 3 * part), BF), shape((tokens, part), BF), shape((tokens, 128), F32)),
        s["order"],
        s["a"],
        s["w_qkv"],
        s["table"],
        s["valid"],
        flops=2 * tokens * part * (3 * width + 8 * tokens),
    )
    s["o"] = [o]
    s = sync(s)

    s["feed"].hop()
    s["o"].append(seq_swap(s["o"][0], 2))
    s["w_low"].append(seq_swap(s["w_low"][2], 1))
    s = sync(s)

    s["feed"].hop()
    o_mine, o_two = s["o"]
    s["o"] = [o_mine, seq_swap(o_mine, 1), o_two, seq_swap(o_two, 1)]
    s["w_high"].append(seq_swap(s["w_high"][2], 1))
    s["cot"].append(seq_swap(s["cot"][0], 2))
    s["c"], s["x_mid"], s["w_rows"] = kernel_call(
        middle,
        (full, shape((rows, width), F32), shape((part, width), BF)),
        s["order"],
        *s["o"],
        *s.pop("w_low"),
        *s.pop("w_high"),
        *s["x"],
        s["table"],
        scratch=[pltpu.VMEM((tokens, width), F32), pltpu.VMEM((width, width), BF)],
        flops=2 * tokens * width * width,
    )
    s["x"] = s["x"][0]
    s = sync(s)

    s["cot"].append(seq_swap(s["cot"][2], 1))
    (s["g"],) = kernel_call(
        mask_rows, (full,), *s["cot"], s["factor"], scratch=[pltpu.VMEM((tokens, width), F32)]
    )
    s["cot"] = s["cot"][0]
    s["h"], s["pull"], w_e = kernel_call(
        expand,
        (shape((tokens, deep), BF), shape((tokens, deep), BF), shape((width, deep), BF)),
        s["idx"],
        s["order"],
        s["c"],
        *s["feed"].blocks((0,)),
        s["table"],
        flops=2 * tokens * width * deep,
    )

    s["du"], s["sum_e"], w_r, *s["c_part"] = kernel_call(
        feed_back,
        (shape((tokens, deep), BF), shape((BLOCKS, group), F32), shape((deep, width), BF), block, block, block, block),
        s["idx"],
        s["g"],
        w_e,
        s.pop("pull"),
        *s.pop("feed").blocks((1,)),
        flops=4 * tokens * width * deep,
    )
    s["c_got"] = [seq_swap(s["c_part"][m], 1) for m in (1, 3)]
    args = (s["idx"], s.pop("c"), s.pop("du"), s["h"], s.pop("g"))
    far = kernel_call(feed_grads_far, (shape((step, deep), BF),) * 2, *args, flops=tokens * width * deep // 2)
    s["c_two"] = seq_swap(add(after(s["c_part"][2], far[0], s["c_got"][0]), s["c_got"][1]), 2)
    pieces = kernel_call(
        feed_grads,
        (shape((2 * step, deep), BF),) * (BLOCKS - 1),
        after(args[0], far[0]),
        *args[1:],
        flops=3 * tokens * width * deep,
    )
    s["feed_grad"] = Scatter(list(pieces) + list(far), data_count, 2)
    s["feed_grad"].hop()
    s["y_part"] = kernel_call(
        reduce_part,
        (block, block, block, block),
        after(s.pop("h"), pieces[0]),
        w_r,
        flops=2 * tokens * width * deep,
    )
    s = sync(s)

    s["mid_grad"], branch, s["sums_mid"] = kernel_call(
        middle_back,
        (shape((rows, width), F32), block, shape((4, width), F32)),
        s.pop("c_part")[0],
        s.pop("c_got")[0],
        s.pop("c_two"),
        s["x_mid"],
        s["cot"],
        s["factor"][:rows],
        s["table"],
    )
    branch_two = seq_swap(branch, 2)
    s["feed_grad"].hop()
    s["y_got"] = [seq_swap(s["y_part"][1], 1)]
    s["branch"] = [branch, branch_two]
    s = sync(s)

    branch, branch_two = s.pop("branch")
    s["branch"] = [branch, seq_swap(branch, 1), branch_two, seq_swap(branch_two, 1)]
    s["feed_grad"].hop()
    s["y_got"].append(seq_swap(s["y_part"][3], 1))
    s["branch_full"], s["dqkv"], s["sums_qv"] = kernel_call(
        attend_back,
        (full, shape((tokens, 3 * part), BF), shape((2, part), F32)),
        s["order"],
        *s.pop("branch"),
        s.pop("w_rows"),
        s.pop("qkv"),
        s.pop("stat"),
        s["valid"],
        scratch=[pltpu.VMEM((tokens, width), F32)],
        flops=2 * tokens * part * (width + 20 * tokens),
    )
    s = sync(s)

    sent = s["feed_grad"].hop()
    s["sums"], *s["a_part"] = kernel_call(
        normed_back,
        (table, block, block, block, block),
        s["order"],
        after(s["dqkv"], sent),
        s.pop("w_qkv"),
        s.pop("normal"),
        s.pop("sums_qv"),
        s.pop("sums_mid"),
        s.pop("sum_e"),
        flops=6 * tokens * width * part,
    )
    if not ring:
        s["sums"] = lax.psum(s["sums"], ("dp", "seq"))
    s["a_got"] = [seq_swap(s["a_part"][m], 1) for m in (1, 3)]
    half = step // 2
    pieces = kernel_call(
        attention_grads,
        (shape((step + extra, width), BF),) * (BLOCKS - 1)
        + (shape((half, width), BF), shape((half + extra, width), BF)),
        s["idx"],
        s["order"],
        after(s.pop("a"), *s["a_got"]),
        s.pop("dqkv"),
        s.pop("branch_full"),
        s["sums"],
        *s.pop("o"),
        scratch=[pltpu.VMEM((width, part), BF), pltpu.VMEM((tokens, part), F32)],
        flops=8 * tokens * width * part,
    )
    s["attention_grad"] = Scatter(list(pieces), data_count, 1)
    s["attention_grad"].hop()
    s = sync(s)

    s["attention_grad"].hop()
    s["hidden"] = part_hidden_grads(s["order"], s.pop("feed_grad").terms(), part, data_count)
    s["hidden_got"] = [seq_swap(s["hidden"][1], 1)]
    s["a_two"] = seq_swap(add(s["a_part"][2], s["a_got"][1]), 2)
    s["y_two"] = add(s["y_part"][2], s["y_got"][1])
    s = sync(s)

    s["attention_grad"].hop()
    s["y_two"] = seq_swap(s["y_two"], 2)
    s = sync(s)

    s["attention_grad"].hop()
    s["hidden_got"] += [seq_swap(s["hidden"][m], m) for m in (2, 3)]
    s["input_gradient"], s["y"] = kernel_call(
        last,
        (block, block),
        s["a_part"][0],
        s["a_got"][0],
        s["a_two"],
        s["x"],
        s["mid_grad"],
        s["y_part"][0],
        s["y_got"][0],
        s["y_two"],
        s["x_mid"],
        s["table"],
    )
    s = sync(s)

    terms = s["attention_grad"].terms()
    high = attention_weights[0].shape[0]
    if ring:
        matrix = shape((high, part), F32)
        outs = (matrix,) * 4 + (shape((count, group), F32), shape((1, group), F32))
        *matrices, sums, bias_sum = kernel_call(finish, outs, *terms)
        grads = lax.dynamic_slice(sum_slot(sums), (0, me * each), (count, each))
        expand_bias_grad = bias_sum[0, :bias_length]
    else:
        grads = lax.dynamic_slice_in_dim(s["sums"], place * each, each, 1)
        expand_bias_grad = lax.dynamic_slice(s["sums"][:, width:], bias_at, (1, bias_length))[0]
        total = sum(t.astype(F32) for t in terms)
        matrices = [total[:, i * part : (i + 1) * part] for i in range(4)]
    expand_weight_grad, reduce_weight_grad = place_hidden_grads(
        s["order"], s["hidden"][:1] + s["hidden_got"], expand_weight.shape, reduce_weight.shape, data_count
    )
    return (
        s["y"][None],
        s["input_gradient"][None],
        grads[0],
        grads[1],
        matrices[0],
        grads[2],
        matrices[1],
        matrices[2],
        grads[3],
        matrices[3],
        grads[4],
        grads[5],
        grads[6],
        expand_weight_grad,
        expand_bias_grad,
        reduce_weight_grad,
        grads[7],
    )


def solution(mesh):
    vector = P(("dp", "seq"))
    matrix = P("dp", "seq")
    tokens = P("dp", "seq", None)
    return jax.shard_map(
        local,
        mesh=mesh,
        in_specs=(
            tokens,
            tokens,
            P("dp"),
            P(),
            vector,
            vector,
            matrix,
            vector,
            matrix,
            matrix,
            vector,
            matrix,
            vector,
            vector,
            vector,
            matrix,
            vector,
            matrix,
            vector,
        ),
        out_specs=(
            tokens,
            tokens,
            vector,
            vector,
            matrix,
            vector,
            matrix,
            matrix,
            vector,
            matrix,
            vector,
            vector,
            vector,
            matrix,
            vector,
            matrix,
            vector,
        ),
        check_vma=False,
    )
```

```python
import jax
import jax.numpy as jnp
from jax import lax
from jax.experimental import pallas as pl
from jax.experimental.pallas import tpu as pltpu
from jax.sharding import PartitionSpec as P

HEADS = 16
EPS = 1e-06
BF = jnp.bfloat16
F32 = jnp.float32
SEQ = 4
BLOCKS = 8
RING = 8
MIB = 1 << 20
VMEM = {
    "pack_columns": 60,
    "pack_hidden": 56,
    "join_hidden": 2,
    "stack_rows": 5,
    "norm_one": 8,
    "attend": 10,
    "middle": 14,
    "feed_forward": 12,
    "reduce_part": 8,
    "mask_rows": 4,
    "feed_grads": 6,
    "add_two": 2,
    "middle_back": 6,
    "attend_back": 12,
    "normed_back": 6,
    "attention_grads": 5,
    "part_hidden": 2,
    "place_hidden": 3,
    "last": 6,
    "finish": 3,
}
GAIN_ONE, SHIFT_ONE, BIAS_Q, BIAS_V, BIAS_O, GAIN_TWO, SHIFT_TWO, BIAS_R = (
    slice(i, i + 1) for i in range(8)
)


def mm(a, b):
    return lax.dot_general(a, b, (((1,), (0,)), ((), ())), preferred_element_type=F32)


def mm_nt(a, b):
    return lax.dot_general(a, b, (((1,), (1,)), ((), ())), preferred_element_type=F32)


def mm_tn(a, b):
    return lax.dot_general(a, b, (((0,), (0,)), ((), ())), preferred_element_type=F32)


def standardize(values):
    center = values - jnp.mean(values, axis=-1, keepdims=True)
    scale = lax.rsqrt(jnp.mean(center * center, axis=-1, keepdims=True) + EPS)
    return center * scale, scale


def rows_at(start, size):
    return pl.ds(pl.multiple_of(start, size), size)


def kernel_call(body, outs, *args, scratch=(), flops=0, far=()):
    specs = [
        pl.BlockSpec(memory_space=pltpu.SMEM if a.dtype == jnp.int32 else pltpu.VMEM) for a in args
    ]
    for i in far:
        specs[i] = pl.BlockSpec(memory_space=pl.ANY)
    moved = sum(a.size * a.dtype.itemsize for a in args)
    moved += sum(o.size * o.dtype.itemsize for o in outs)
    return pl.pallas_call(
        body,
        out_shape=tuple(outs),
        in_specs=specs,
        out_specs=tuple(pl.BlockSpec(memory_space=pltpu.VMEM) for _ in outs),
        scratch_shapes=list(scratch),
        compiler_params=pltpu.CompilerParams(vmem_limit_bytes=VMEM[body.__name__] * MIB),
        cost_estimate=pl.CostEstimate(flops=0, bytes_accessed=int(moved), transcendentals=0),
    )(*args)


def shape(dims, dtype):
    return jax.ShapeDtypeStruct(tuple(dims), dtype)


def norm_one(x0, x1, x2, x3, table, a_out, n_out, hold):
    rows, width = x0.shape
    for k, ref in enumerate((x0, x1, x2, x3)):
        normal, _ = standardize(ref[...].astype(F32))
        hold[k * rows : (k + 1) * rows, :] = normal
    normal = hold[...]
    n_out[...] = normal.astype(BF)
    a_out[...] = (normal * table[GAIN_ONE, :width] + table[SHIFT_ONE, :width]).astype(BF)


def mask_rows(c0, c1, c2, c3, factor, g_out, hold):
    rows = c0.shape[0]
    for k, ref in enumerate((c0, c1, c2, c3)):
        hold[k * rows : (k + 1) * rows, :] = ref[...].astype(F32)
    g_out[...] = (hold[...] * factor[...]).astype(BF)


def head_lanes(width, head, size):
    lane = lax.broadcasted_iota(jnp.int32, (1, width), 1)
    return (lane >= head * size) & (lane < (head + 1) * size)


def stack_rows(idx, order, *refs):
    w_qkv, w_low, w_high, table = refs[BLOCKS + 1 :]
    width, first = w_qkv.shape
    step = width // BLOCKS
    count = table.shape[0]
    wide = (table.shape[1] - width) // SEQ
    each = wide // SEQ
    table[...] = jnp.zeros_like(table)
    row = lax.broadcasted_iota(jnp.int32, (count, wide), 0)
    biases = jnp.zeros((count, wide), F32)
    for k in range(BLOCKS + 1):
        spot = idx[min(k, BLOCKS - 1)]
        at, size = spot * step, step
        if k >= BLOCKS - 1:
            size = step // 2
            at += size * (k - BLOCKS + 1)
        w_qkv[rows_at(at, size), :] = refs[k][:size, :first]

        @pl.when(at < width // 2)
        def _():
            w_low[rows_at(at, size), :] = refs[k][:size, first:]

        @pl.when(at >= width // 2)
        def _():
            w_high[rows_at(at - width // 2, size), :] = refs[k][:size, first:]

        if refs[k].shape[0] > size:
            below = refs[k][size:, :wide]
            placed = mm(below[:, :each], own_lanes(order, each, wide, each))
            table[:, rows_at(spot * wide, wide)] = placed[:count]
            biases = jnp.where(row == spot, below.astype(F32)[count : count + 1], biases)
    table[:, pl.ds(pl.multiple_of(width + order[0] * wide, wide), wide)] = biases


def copy_all(copies):
    for copy in copies:
        copy.start()
    for copy in copies:
        copy.wait()


def pack_columns(*refs):
    count = (len(refs) - 6) // 2
    weights, vectors = refs[:4], refs[4 : 4 + count]
    out, sems, hold = refs[4 + count : 7 + count]
    buffers = refs[7 + count :]
    high, wide = weights[0].shape
    copies = [
        pltpu.make_async_copy(w, out.at[:high, i * wide : (i + 1) * wide], sems.at[i])
        for i, w in enumerate(weights)
    ]
    small = [pltpu.make_async_copy(v, b, sems.at[4 + i]) for i, (v, b) in enumerate(zip(vectors, buffers))]
    for copy in small + copies:
        copy.start()
    hold[...] = jnp.zeros_like(hold)
    out[high:, :] = jnp.zeros((hold.shape[0], out.shape[1]), BF)
    for copy in small:
        copy.wait()
    for i, buffer in enumerate(buffers):
        size = buffer.shape[0]
        hold[i : i + 1, :size] = buffer[...].astype(F32).reshape(1, size)
    out[high:, : hold.shape[1]] = hold[...].astype(BF)
    for copy in copies:
        copy.wait()


def own_lanes(order, rows, wide, each):
    lane = lax.broadcasted_iota(jnp.int32, (rows, wide), 1)
    return (lane == order[0] * each + lax.broadcasted_iota(jnp.int32, (rows, wide), 0)).astype(BF)


def pack_hidden(order, w_expand, w_reduce, o0, o1, o2, o3, sems):
    step, part = w_expand.shape[0], w_reduce.shape[1]
    half = part // 2
    deep = w_expand.shape[1] // 2
    quarter = w_reduce.shape[0] // SEQ
    copies = []
    for m, out in enumerate((o0, o1, o2, o3)):
        one = rows_at(order[m] * half, half)
        two = pl.ds(pl.multiple_of(deep + order[m] * half, half), half)
        three = rows_at(order[m] * quarter, quarter)
        copies += [
            pltpu.make_async_copy(w_expand.at[:, one], out.at[:step, :half], sems.at[3 * m]),
            pltpu.make_async_copy(w_expand.at[:, two], out.at[:step, half:], sems.at[3 * m + 1]),
            pltpu.make_async_copy(w_reduce.at[three, :], out.at[step:, :], sems.at[3 * m + 2]),
        ]
    copy_all(copies)


def join_hidden(order, p0, p1, p2, p3, out):
    part = p0.shape[1]
    for m, ref in enumerate((p0, p1, p2, p3)):
        out[:, rows_at(order[m] * part, part)] = ref[...]


def part_hidden(order, e0, e1, e2, mine, *outs):
    part = mine.shape[1]
    for m in range(SEQ):
        lanes = rows_at(order[m] * part, part)
        e = e0[:, lanes].astype(F32) + e1[:, lanes].astype(F32) + e2[:, lanes].astype(F32)
        if m == 0:
            mine[...] = e
        else:
            outs[m - 1][...] = e.astype(BF)


def place_hidden(order, p0, p1, p2, p3, e_out, r_out):
    step, part = e_out.shape[0], p0.shape[1]
    half = part // 2
    deep = e_out.shape[1] // 2
    quarter = r_out.shape[0] // SEQ
    for m, ref in enumerate((p0, p1, p2, p3)):
        e_out[:, rows_at(order[m] * half, half)] = ref[:step, :half].astype(F32)
        e_out[:, pl.ds(pl.multiple_of(deep + order[m] * half, half), half)] = ref[:step, half:].astype(F32)
        r_out[rows_at(order[m] * quarter, quarter), :] = ref[step:, :].astype(F32)


def attend(order, a, w, table, key_mask, out, o_out, stat_out):
    width = o_out.shape[1]
    qkv = mm(a[...], w[...])
    mine = rows_at(order[0] * width, width)
    q = (qkv[:, :width] + table[BIAS_Q, mine]).astype(BF)
    key = qkv[:, width : 2 * width].astype(BF)
    value = (qkv[:, 2 * width :] + table[BIAS_V, mine]).astype(BF)
    out[:, :width] = q
    out[:, width : 2 * width] = key
    out[:, 2 * width :] = value
    size = width // (HEADS // SEQ)
    valid = key_mask[...] > 0
    total = None
    for h in range(HEADS // SEQ):
        lanes = head_lanes(width, h, size)
        logits = mm_nt(jnp.where(lanes, q, jnp.zeros_like(q)), key)
        scores = jnp.where(valid, logits * size ** (-0.5), -1000000000.0)
        top = jnp.max(scores, axis=-1, keepdims=True)
        weights = jnp.exp(scores - top)
        inverse = 1.0 / jnp.sum(weights, axis=-1, keepdims=True)
        probs = (weights * inverse).astype(BF)
        mixed = mm(probs, jnp.where(lanes, value, jnp.zeros_like(value)))
        total = mixed if total is None else total + mixed
        stat_out[:, h : h + 1] = top
        stat_out[:, HEADS // SEQ + h : HEADS // SEQ + h + 1] = inverse
    o_out[...] = total.astype(BF)


def middle(order, *refs):
    o = refs[:SEQ]
    w_low = refs[SEQ : 2 * SEQ]
    w_high = refs[2 * SEQ : 3 * SEQ]
    x = refs[3 * SEQ : 4 * SEQ]
    table, c_out, x_out, w_rows, hold, w = refs[4 * SEQ :]
    rows, full = x[0].shape
    width = o[0].shape[1]
    for m in range(SEQ):
        at = rows_at(order[m] * width, width)
        w[: full // 2, at] = w_low[m][...]
        w[full // 2 :, at] = w_high[m][...]
    w_rows[...] = w[rows_at(order[0] * width, width), :]
    for k in range(SEQ):
        hold[k * rows : (k + 1) * rows, :] = x[k][...].astype(F32) + table[BIAS_O, :full]
    for m in range(SEQ):
        part = mm(o[m][...], w[rows_at(order[m] * width, width), :])
        for k in range(SEQ):
            there = (k ^ m) * rows
            hold[there : there + rows, :] += part[k * rows : (k + 1) * rows, :]
    x_out[...] = hold[0:rows, :]
    normal, _ = standardize(hold[...])
    c_out[...] = (normal * table[GAIN_TWO, :full] + table[SHIFT_TWO, :full]).astype(BF)


def feed_forward(idx, order, c, g, table, *refs):
    pieces = refs[: BLOCKS + 1]
    h_out, u_out, bias_out, w_reduce, o0, o1, o2, o3, e_far, r_far, w_expand = refs[BLOCKS + 1 :]
    step = w_expand.shape[0] // BLOCKS
    for k in range(BLOCKS):
        at = rows_at(idx[k] * step, step)
        w_expand[at, :] = pieces[k][:step, :]
        last_piece = pieces[k] if k < BLOCKS - 1 else pieces[k + 1]
        w_reduce[at, :] = last_piece[last_piece.shape[0] - step :, :]
    width = h_out.shape[1]
    group = bias_out.shape[1]
    bias = table[:, pl.ds(pl.multiple_of(w_expand.shape[0] + order[0] * group, group), group)]
    chunk = 2 * group
    for n in range(0, width, chunk):
        r = n // group
        row = jnp.concatenate([bias[r : r + 1], bias[r + 1 : r + 2]], axis=1)
        u = mm(c[...], w_expand[:, n : n + chunk]) + row
        upper = mm_nt(g[...], w_reduce[n : n + chunk, :])
        cdf = 0.5 * (1.0 + lax.erf(u * (0.5**0.5)))
        density = jnp.exp(-0.5 * u * u) * 0.3989422804014327
        h_out[:, n : n + chunk] = (u * cdf).astype(BF)
        low = (upper * (cdf + u * density)).astype(BF)
        u_out[:, n : n + chunk] = low
        total = jnp.sum(low.astype(F32), axis=0, keepdims=True)
        bias_out[r : r + 1, :] = total[:, :group]
        bias_out[r + 1 : r + 2, :] = total[:, group:]
    lower = mm_nt(u_out[...], w_expand[...])
    rows = o0.shape[0]
    for k, out in enumerate((o0, o1, o2, o3)):
        out[...] = lower[k * rows : (k + 1) * rows, :].astype(BF)
    at = rows_at(idx[BLOCKS - 1] * step, step)
    e_far[...] = mm_tn(c[:, at], u_out[...]).astype(BF)
    r_far[...] = mm_tn(h_out[:, at], g[...]).astype(BF)


def reduce_part(h, w, *outs):
    y = mm(h[...], w[...])
    rows = outs[0].shape[0]
    for k in range(SEQ):
        outs[k][...] = y[k * rows : (k + 1) * rows, :].astype(BF)


def feed_grads(idx, c, du, h, g, *outs):
    step = outs[0].shape[0] // 2
    for k in range(BLOCKS - 1):
        at = rows_at(idx[k] * step, step)
        outs[k][:step, :] = mm_tn(c[:, at], du[...]).astype(BF)
        outs[k][step:, :] = mm_tn(h[:, at], g[...]).astype(BF)


def add_two(a, a_own, b, b_own, a_out, b_out):
    here = a.shape[0]
    rest = b_own.shape[0] - b.shape[0]
    a_out[:here, :] = (a[...].astype(F32) + a_own[:here, :].astype(F32)).astype(BF)
    b_out[rest:, :] = (b[...].astype(F32) + b_own[rest:, :].astype(F32)).astype(BF)
    if rest:
        a_out[here:, :] = a_own[here:, :]
        b_out[:rest, :] = b_own[:rest, :]


def norm_pull(upper, normal, scale, gain):
    inner = upper * gain
    return scale * (
        inner
        - jnp.mean(inner, axis=-1, keepdims=True)
        - normal * jnp.mean(inner * normal, axis=-1, keepdims=True)
    )


def middle_back(part0, part1, part2, x, cot, factor, table, grad_out, low_out, sums_out):
    upper = part0[...].astype(F32) + part1[...].astype(F32) + part2[...].astype(F32)
    normal, scale = standardize(x[...])
    upstream = cot[...].astype(F32) * factor[...]
    grad = upstream + norm_pull(upper, normal, scale, table[GAIN_TWO, : x.shape[1]])
    low = grad.astype(BF)
    grad_out[...] = grad
    low_out[...] = low
    sums_out[0:1, :] = jnp.sum(upper * normal, axis=0, keepdims=True)
    sums_out[1:2, :] = jnp.sum(upper, axis=0, keepdims=True)
    sums_out[2:3, :] = jnp.sum(low.astype(F32), axis=0, keepdims=True)
    sums_out[3:4, :] = jnp.sum(upstream, axis=0, keepdims=True)


def attend_back(order, *refs):
    grads = refs[:SEQ]
    w_rows, qkv, stat, key_mask, g_out, out, sums_out, hold = refs[SEQ:]
    rows = grads[0].shape[0]
    for k in range(SEQ):
        hold[k * rows : (k + 1) * rows, :] = grads[k][...].astype(F32)
    g_out[...] = hold[...].astype(BF)
    width = qkv.shape[1] // 3
    size = width // (HEADS // SEQ)
    d_out = mm_nt(g_out[...], w_rows[...]).astype(BF)
    q, key, value = (qkv[:, i * width : (i + 1) * width] for i in range(3))
    valid = key_mask[...] > 0
    dq = dk = dv = None
    for h in range(HEADS // SEQ):
        lanes = head_lanes(width, h, size)
        q_h = jnp.where(lanes, q, jnp.zeros_like(q))
        d_h = jnp.where(lanes, d_out, jnp.zeros_like(d_out))
        logits = mm_nt(q_h, key)
        scores = jnp.where(valid, logits * size ** (-0.5), -1000000000.0)
        top = stat[:, h : h + 1]
        inverse = stat[:, HEADS // SEQ + h : HEADS // SEQ + h + 1]
        probs = jnp.exp(scores - top) * inverse
        prob_grad = mm_nt(d_h, value)
        center = jnp.sum(probs * prob_grad, axis=-1, keepdims=True)
        low = jnp.where(valid, probs * (prob_grad - center) * size ** (-0.5), 0.0).astype(BF)
        dv_h = mm_tn(probs.astype(BF), d_h)
        dk_h = mm_tn(low, q_h)
        dq_h = mm(low, jnp.where(lanes, key, jnp.zeros_like(key)))
        dq = dq_h if dq is None else dq + dq_h
        dk = dk_h if dk is None else dk + dk_h
        dv = dv_h if dv is None else dv + dv_h
    dq, dk, dv = dq.astype(BF), dk.astype(BF), dv.astype(BF)
    out[:, :width] = dq
    out[:, width : 2 * width] = dk
    out[:, 2 * width :] = dv
    sums_out[0:1, :] = jnp.sum(dq.astype(F32), axis=0, keepdims=True)
    sums_out[1:2, :] = jnp.sum(dv.astype(F32), axis=0, keepdims=True)


def attention_grads(idx, order, a, d, g, sums, *refs):
    o = refs[:SEQ]
    outs = refs[SEQ : SEQ + BLOCKS + 1]
    hold, turned = refs[SEQ + BLOCKS + 1 :]
    rows = g.shape[0] // SEQ
    width = o[0].shape[1]
    full = hold.shape[0]
    step = full // BLOCKS
    mine = g[:, rows_at(order[0] * width, width)].astype(F32)
    for m in range(SEQ):
        for k in range(SEQ):
            there = (k ^ m) * rows
            turned[k * rows : (k + 1) * rows, :] = mine[there : there + rows, :]
        hold[rows_at(order[m] * width, width), :] = mm_tn(o[m][...], turned[...].astype(BF)).astype(BF)
    count, wide = sums.shape[0], step
    biases = sums[:, pl.ds(pl.multiple_of(full + order[0] * wide, wide), wide)]
    row = lax.broadcasted_iota(jnp.int32, biases.shape, 0)
    for k in range(BLOCKS):
        at = rows_at(idx[k] * step, step)
        value = mm_tn(a[:, at], d[...]).astype(BF)
        size = step if k < BLOCKS - 1 else step // 2
        outs[k][:size, : 3 * width] = value[:size]
        outs[k][:size, 3 * width :] = hold[rows_at(idx[k] * step, size), :]
        below = outs[k]
        if k == BLOCKS - 1:
            below = outs[k + 1]
            below[:size, : 3 * width] = value[size:]
            below[:size, 3 * width :] = hold[rows_at(idx[k] * step + size, size), :]
        if below.shape[0] > size:
            extra = below.shape[0] - size
            bias = jnp.sum(jnp.where(row == idx[k], biases, 0.0), axis=0, keepdims=True)
            bias = jnp.broadcast_to(bias, (extra - count, wide))
            block = jnp.concatenate([sums[:, rows_at(idx[k] * wide, wide)], bias], axis=0)
            below[size:, :wide] = block.astype(BF)
            below[size:, wide:] = jnp.zeros((extra, below.shape[1] - wide), BF)


def normed_back(order, d, w, normal, sums_qv, sums_mid, sum_e, sums, *outs):
    rows, width = outs[0].shape
    part, wide = sums_qv.shape[1], sum_e.shape[1]
    upper = mm_nt(d[...], w[...])
    for k in range(SEQ):
        outs[k][...] = upper[k * rows : (k + 1) * rows, :].astype(BF)
    sums[...] = jnp.zeros_like(sums)
    sums[GAIN_ONE, :width] = jnp.sum(upper * normal[...].astype(F32), axis=0, keepdims=True)
    sums[SHIFT_ONE, :width] = jnp.sum(upper, axis=0, keepdims=True)
    mine = rows_at(order[0] * part, part)
    sums[BIAS_Q, mine] = sums_qv[0:1, :]
    sums[BIAS_V, mine] = sums_qv[1:2, :]
    sums[BIAS_O, :width] = sums_mid[2:3, :]
    sums[GAIN_TWO, :width] = sums_mid[0:1, :]
    sums[SHIFT_TWO, :width] = sums_mid[1:2, :]
    sums[BIAS_R, :width] = sums_mid[3:4, :]
    sums[:, pl.ds(pl.multiple_of(width + order[0] * wide, wide), wide)] = sum_e[...]


def last(part0, part1, part2, x, grad, y0, y1, y2, x_mid, table, grad_out, y_out):
    width = x.shape[1]
    upper = part0[...].astype(F32) + part1[...].astype(F32) + part2[...].astype(F32)
    normal, scale = standardize(x[...].astype(F32))
    grad_out[...] = (grad[...] + norm_pull(upper, normal, scale, table[GAIN_ONE, :width])).astype(BF)
    y = x_mid[...] + table[BIAS_R, :width] + y0[...].astype(F32)
    y_out[...] = (y + y1[...].astype(F32) + y2[...].astype(F32)).astype(BF)


def finish(p0, p1, p2, w0, w1, w2, w3, sums, bias):
    high, part = w0.shape
    count, wide = sums.shape
    for i, out in enumerate((w0, w1, w2, w3)):
        at = slice(i * part, (i + 1) * part)
        out[...] = p0[:high, at].astype(F32) + p1[:high, at].astype(F32) + p2[:high, at].astype(F32)
    below = p0[high:, :wide].astype(F32) + p1[high:, :wide].astype(F32) + p2[high:, :wide].astype(F32)
    sums[...] = below[:count]
    bias[...] = below[count : count + 1]


def seq_swap(value, flip):
    return lax.ppermute(value, "seq", [(s, s ^ flip) for s in range(SEQ)])


def after(value, *others):
    return lax.optimization_barrier((value,) + others)[0]


def add(a, b):
    return (a.astype(F32) + b.astype(F32)).astype(BF)


def ring_order(data_count):
    return list(range(0, data_count, 2)) + list(range(data_count - 1, 0, -2))


def ring_hop(value, data_count, step):
    ring = ring_order(data_count)
    pairs = [(ring[r], ring[(r + step) % data_count]) for r in range(data_count)]
    return lax.ppermute(value, "dp", pairs)


RELATIVE = (0, -1, -2, -3, 1, 2, 3, 4)


def relative_order(data_count):
    if data_count != RING:
        return jnp.arange(BLOCKS, dtype=jnp.int32)
    me = lax.axis_index("dp")
    z, y = me // 2, me % 2
    place = jnp.where(y == 0, z, BLOCKS - 1 - z)
    there = (place + jnp.array(RELATIVE, dtype=jnp.int32) + BLOCKS) % BLOCKS
    half = BLOCKS // 2
    return jnp.where(there < half, 2 * there, 2 * (BLOCKS - 1 - there) + 1).astype(jnp.int32)


@jax.tree_util.register_pytree_node_class
class Gather:
    def __init__(self, value, data_count, parts, cut, back=(), front=()):
        self.value, self.data_count, self.parts, self.cut = value, data_count, parts, cut
        self.back, self.front = list(back), list(front)

    def tree_flatten(self):
        return (self.value, self.back, self.front), (self.data_count, self.parts, self.cut)

    @classmethod
    def tree_unflatten(cls, aux, parts):
        return cls(parts[0], *aux, *parts[1:])

    def hop(self):
        if self.data_count != RING:
            if not self.back:
                whole = lax.all_gather(self.value, "dp", axis=0, tiled=False)
                parts = [p.reshape((BLOCKS, -1) + p.shape[2:]) for p in jnp.split(whole, self.parts, axis=1)]
                self.back = list(jnp.concatenate(parts, axis=1))
            return
        back, front = (self.back or [self.value])[-1], (self.front or [self.value])[-1]
        if len(self.back) == BLOCKS // 2 - 1:
            back, front = back[: self.cut], front[self.cut :]
        self.back.append(ring_hop(back, self.data_count, 1))
        self.front.append(ring_hop(front, self.data_count, -1))

    def blocks(self, last=(0, 1)):
        if self.data_count != RING:
            halves = (self.back[-1][: self.cut], self.back[-1][self.cut :])
            return self.back[:-1] + [halves[i] for i in last]
        halves = (self.back[3], self.front[3])
        return [self.value] + self.back[:3] + self.front[:3] + [halves[i] for i in last]


@jax.tree_util.register_pytree_node_class
class Scatter:
    def __init__(self, pieces, data_count, parts, hops=0, left=None, right=None):
        self.pieces, self.data_count, self.parts = pieces, data_count, parts
        self.hops, self.left, self.right = hops, left, right

    def tree_flatten(self):
        return (self.pieces, self.left, self.right), (self.data_count, self.parts, self.hops)

    @classmethod
    def tree_unflatten(cls, aux, parts):
        return cls(parts[0], *aux, *parts[1:])

    def hop(self):
        n, self.hops = self.hops, self.hops + 1
        if self.data_count != RING:
            if n == 0:
                whole = jnp.concatenate(self.pieces, axis=0)
                wide = whole.shape[1]
                whole = whole.reshape(BLOCKS, self.parts, self.data_count // BLOCKS, -1, wide)
                whole = whole.transpose(0, 2, 1, 3, 4).reshape(-1, wide)
                self.left = lax.psum_scatter(whole, "dp", scatter_dimension=0, tiled=True)
            return self.left
        own = dict(zip(RELATIVE, self.pieces))
        left, right = self.left, self.right
        if n == 0:
            left, right = self.pieces[-2:]
        else:
            ahead, behind = own[4 - n], own[n - 4]
            outs = (shape(ahead.shape, BF),) * 2
            left, right = kernel_call(add_two, outs, left, ahead, right, behind)
        self.left = ring_hop(left, self.data_count, 1)
        self.right = ring_hop(right, self.data_count, -1)
        return left

    def terms(self):
        if self.data_count != RING:
            return [self.left, jnp.zeros_like(self.left), jnp.zeros_like(self.left)]
        return [self.pieces[0], self.left, self.right]


def sum_slot(value):
    one, two, three = (seq_swap(value, m) for m in range(1, SEQ))
    return value + one + two + three


def trade(parts, data_count):
    return [parts[0]] + [seq_swap(parts[m], m) for m in range(1, SEQ)]


def pack_hidden_weights(order, w_expand, w_reduce, data_count):
    high, low, part = w_expand.shape[0], w_reduce.shape[0] // SEQ, w_reduce.shape[1]
    if data_count == RING:
        piece = shape((high + low, part), BF)
        sems = [pltpu.SemaphoreType.DMA((3 * SEQ,))]
        return list(
            kernel_call(pack_hidden, (piece,) * SEQ, order, w_expand, w_reduce, far=(1, 2), scratch=sems)
        )
    e = w_expand.reshape(high, -1, SEQ, low).transpose(2, 0, 1, 3).reshape(SEQ, high, part)
    both = jnp.concatenate([e, w_reduce.reshape(SEQ, low, part)], axis=1)
    return [lax.dynamic_index_in_dim(both, order[m], 0, False) for m in range(SEQ)]


def join_hidden_weights(order, parts, data_count):
    rows, part = parts[0].shape
    if data_count == RING:
        return kernel_call(join_hidden, (shape((rows, SEQ * part), BF),), order, *parts)[0]
    both = jnp.zeros((rows, SEQ * part), BF)
    for m in range(SEQ):
        both = lax.dynamic_update_slice(both, parts[m], (0, order[m] * part))
    return both


def part_hidden_grads(order, terms, part, data_count):
    if data_count == RING:
        piece = (terms[0].shape[0], part)
        outs = (shape(piece, F32),) + (shape(piece, BF),) * (SEQ - 1)
        return list(kernel_call(part_hidden, outs, order, *terms))
    return [lax.dynamic_slice_in_dim(terms[0], order[m] * part, part, 1) for m in range(SEQ)]


def place_hidden_grads(order, parts, e_shape, r_shape, data_count):
    if data_count == RING:
        outs = (shape(e_shape, F32), shape(r_shape, F32))
        return kernel_call(place_hidden, outs, order, *parts)
    high, low = e_shape[0], r_shape[0] // SEQ
    both = jnp.zeros((SEQ,) + parts[0].shape, F32)
    for m in range(SEQ):
        both = lax.dynamic_update_slice(both, parts[m].astype(F32)[None], (order[m], 0, 0))
    e = both[:, :high].reshape(SEQ, high, -1, low).transpose(1, 2, 0, 3).reshape(e_shape)
    return e, both[:, high:].reshape(r_shape)


def eight(deep, wide):
    return (shape((deep, wide), BF),) * (BLOCKS - 1) + (shape((deep // 2, wide), BF),) * 2


def sync(state):
    return lax.optimization_barrier(state)


def local(
    block_input,
    cotangent,
    image_valid,
    token_valid,
    first_gain,
    first_shift,
    query_weight,
    query_bias,
    key_weight,
    value_weight,
    value_bias,
    output_weight,
    output_bias,
    second_gain,
    second_shift,
    expand_weight,
    expand_bias,
    reduce_weight,
    reduce_bias,
):
    data_count = lax.axis_size("dp")
    ring = data_count == RING
    me = lax.axis_index("seq")
    rows, width = block_input.shape[1:]
    tokens = rows * SEQ
    part = width // SEQ
    deep = expand_weight.shape[1]
    step = width // BLOCKS
    full = shape((tokens, width), BF)
    block = shape((rows, width), BF)
    s = {}
    s["idx"] = relative_order(data_count)
    dp = lax.axis_index("dp")
    s["order"] = jnp.stack([me ^ k for k in range(SEQ)] + [dp]).astype(jnp.int32)

    vectors = (
        first_gain,
        first_shift,
        query_bias,
        value_bias,
        output_bias,
        second_gain,
        second_shift,
        reduce_bias,
    )
    each = first_gain.shape[0]
    place = dp * SEQ + me
    count = len(vectors)
    group = deep // BLOCKS
    bias_row = expand_bias.astype(F32)[None]
    bias_length = expand_bias.shape[0]
    bias_at = dp * bias_length
    bias_at = (bias_at // group, me * group + bias_at % group)
    table = shape((count, width + SEQ * group), F32)

    valid = token_valid.astype(F32).reshape(SEQ, rows)
    valid = jnp.concatenate([lax.dynamic_slice_in_dim(valid, s["order"][k], 1, 0) for k in range(SEQ)], axis=1)
    s["valid"] = valid
    s["factor"] = (valid * image_valid.astype(F32)[0]).reshape(tokens, 1)

    attention_weights = (query_weight, key_weight, value_weight, output_weight)
    extra = 2 * count if ring else 0
    if ring:
        args = attention_weights + vectors + (expand_bias,)
        scratch = [pltpu.SemaphoreType.DMA((len(args),)), pltpu.VMEM((extra, group), F32)]
        scratch += [pltpu.VMEM(v.shape, BF) for v in args[4:]]
        outs = (shape((step + extra, width), BF),)
        (piece,) = kernel_call(pack_columns, outs, *args, far=range(len(args)), scratch=scratch)
    else:
        piece = jnp.concatenate(attention_weights, axis=1)
    s["attention"] = Gather(piece, data_count, 1, step // 2)
    s["attention"].hop()
    s["x"] = [block_input[0]]
    s["x"] += [seq_swap(s["x"][0], m) for m in (1, 2)]
    s["cot"] = [cotangent[0]]
    s["hidden"] = pack_hidden_weights(s["order"], expand_weight, reduce_weight, data_count)
    s = sync(s)

    s["attention"].hop()
    hidden = s.pop("hidden")
    s["hidden"] = [hidden[0]] + [seq_swap(hidden[m], m) for m in (1, 2)]
    s["hidden_last"] = hidden[3]
    s = sync(s)

    s["attention"].hop()
    s["hidden"].append(seq_swap(s.pop("hidden_last"), 3))
    s["x"].append(seq_swap(s["x"][2], 1))
    s["cot"].append(seq_swap(s["cot"][0], 2))
    s = sync(s)

    s["attention"].hop()
    s["cot"] = [s["cot"][0], seq_swap(s["cot"][0], 1), s["cot"][1], seq_swap(s["cot"][1], 1)]
    feed = join_hidden_weights(s["order"], s.pop("hidden"), data_count)
    s["feed"] = Gather(feed, data_count, 2, step)
    s = sync(s)

    s["feed"].hop()
    half = shape((width // 2, part), BF)
    s["w_qkv"], w_low, w_high, s["table"] = kernel_call(
        stack_rows,
        (shape((width, 3 * part), BF), half, half, table),
        s["idx"],
        s["order"],
        *s.pop("attention").blocks(),
    )
    s["w_low"], s["w_high"] = [w_low], [w_high]
    s["w_low"] += [seq_swap(after(w_low, s["w_qkv"]), m) for m in (1, 2)]
    if ring:
        s["table"] = sum_slot(s["table"])
    else:
        every = lax.broadcasted_iota(jnp.int32, (each, width), 1)
        every = every == place * each + lax.broadcasted_iota(jnp.int32, (each, width), 0)
        stacked = sum(
            jnp.pad(v[None], ((i, count - 1 - i), (0, 0))) for i, v in enumerate(vectors)
        )
        placed = jnp.dot(stacked, every.astype(BF), preferred_element_type=F32)
        placed_bias = lax.dynamic_update_slice(
            jnp.zeros((count, table.shape[1] - width), F32), bias_row, bias_at
        )
        s["table"] = lax.psum(jnp.concatenate([placed, placed_bias], axis=1), ("dp", "seq"))
    s = sync(s)

    s["feed"].hop()
    s["w_high"] += [seq_swap(s["w_high"][0], m) for m in (1, 2)]
    s["a"], s["normal"] = kernel_call(
        norm_one, (full, full), *s["x"], s["table"], scratch=[pltpu.VMEM((tokens, width), F32)]
    )
    s["qkv"], o, s["stat"] = kernel_call(
        attend,
        (shape((tokens, 3 * part), BF), shape((tokens, part), BF), shape((tokens, 128), F32)),
        s["order"],
        s["a"],
        s["w_qkv"],
        s["table"],
        s["valid"],
        flops=2 * tokens * part * (3 * width + 8 * tokens),
    )
    s["o"] = [o]
    s = sync(s)

    s["feed"].hop()
    s["o"].append(seq_swap(s["o"][0], 2))
    (s["g"],) = kernel_call(
        mask_rows, (full,), *s["cot"], s["factor"], scratch=[pltpu.VMEM((tokens, width), F32)]
    )
    s["cot"] = s["cot"][0]
    s["w_low"].append(seq_swap(s["w_low"][2], 1))
    s = sync(s)

    s["feed"].hop()
    o_mine, o_two = s["o"]
    s["o"] = [o_mine, seq_swap(o_mine, 1), o_two, seq_swap(o_two, 1)]
    s["w_high"].append(seq_swap(s["w_high"][2], 1))
    s["c"], s["x_mid"], s["w_rows"] = kernel_call(
        middle,
        (full, shape((rows, width), F32), shape((part, width), BF)),
        s["order"],
        *s["o"],
        *s.pop("w_low"),
        *s.pop("w_high"),
        *s["x"],
        s["table"],
        scratch=[pltpu.VMEM((tokens, width), F32), pltpu.VMEM((width, width), BF)],
        flops=2 * tokens * width * width,
    )
    s["x"] = s["x"][0]
    s = sync(s)

    h, du, s["sum_e"], w_r, *c_part, e_far, r_far = kernel_call(
        feed_forward,
        (
            shape((tokens, deep), BF),
            shape((tokens, deep), BF),
            shape((BLOCKS, group), F32),
            shape((deep, width), BF),
            block,
            block,
            block,
            block,
            shape((step, deep), BF),
            shape((step, width), BF),
        ),
        s["idx"],
        s["order"],
        s["c"],
        s["g"],
        s["table"],
        *s.pop("feed").blocks(),
        scratch=[pltpu.VMEM((width, deep), BF)],
        flops=7 * tokens * width * deep,
    )
    s["c_part"] = c_part
    s["c_got"] = [seq_swap(c_part[m], 1) for m in (1, 3)]
    far = [e_far, r_far]
    args = (s["idx"], s.pop("c"), du, h, s.pop("g"))
    s["c_two"] = seq_swap(add(after(s["c_part"][2], s["c_got"][0]), s["c_got"][1]), 2)
    pieces = kernel_call(
        feed_grads,
        (shape((2 * step, deep), BF),) * (BLOCKS - 1),
        after(args[0], far[0]),
        *args[1:],
        flops=3 * tokens * width * deep,
    )
    s["feed_grad"] = Scatter(list(pieces) + list(far), data_count, 2)
    s["feed_grad"].hop()
    s["y_part"] = kernel_call(
        reduce_part,
        (block, block, block, block),
        after(h, pieces[0]),
        w_r,
        flops=2 * tokens * width * deep,
    )
    s = sync(s)

    s["mid_grad"], branch, s["sums_mid"] = kernel_call(
        middle_back,
        (shape((rows, width), F32), block, shape((4, width), F32)),
        s.pop("c_part")[0],
        s.pop("c_got")[0],
        s.pop("c_two"),
        s["x_mid"],
        s["cot"],
        s["factor"][:rows],
        s["table"],
    )
    branch_two = seq_swap(branch, 2)
    s["feed_grad"].hop()
    s["y_got"] = [seq_swap(s["y_part"][1], 1)]
    s["branch"] = [branch, branch_two]
    s = sync(s)

    branch, branch_two = s.pop("branch")
    s["branch"] = [branch, seq_swap(branch, 1), branch_two, seq_swap(branch_two, 1)]
    s["feed_grad"].hop()
    s["y_got"].append(seq_swap(s["y_part"][3], 1))
    s["branch_full"], s["dqkv"], s["sums_qv"] = kernel_call(
        attend_back,
        (full, shape((tokens, 3 * part), BF), shape((2, part), F32)),
        s["order"],
        *s.pop("branch"),
        s.pop("w_rows"),
        s.pop("qkv"),
        s.pop("stat"),
        s["valid"],
        scratch=[pltpu.VMEM((tokens, width), F32)],
        flops=2 * tokens * part * (width + 20 * tokens),
    )
    s = sync(s)

    sent = s["feed_grad"].hop()
    s["sums"], *s["a_part"] = kernel_call(
        normed_back,
        (table, block, block, block, block),
        s["order"],
        after(s["dqkv"], sent),
        s.pop("w_qkv"),
        s.pop("normal"),
        s.pop("sums_qv"),
        s.pop("sums_mid"),
        s.pop("sum_e"),
        flops=6 * tokens * width * part,
    )
    if not ring:
        s["sums"] = lax.psum(s["sums"], ("dp", "seq"))
    s["a_got"] = [seq_swap(s["a_part"][m], 1) for m in (1, 3)]
    half = step // 2
    pieces = kernel_call(
        attention_grads,
        (shape((step + extra, width), BF),) * (BLOCKS - 1)
        + (shape((half, width), BF), shape((half + extra, width), BF)),
        s["idx"],
        s["order"],
        after(s.pop("a"), *s["a_got"]),
        s.pop("dqkv"),
        s.pop("branch_full"),
        s["sums"],
        *s.pop("o"),
        scratch=[pltpu.VMEM((width, part), BF), pltpu.VMEM((tokens, part), F32)],
        flops=8 * tokens * width * part,
    )
    s["attention_grad"] = Scatter(list(pieces), data_count, 1)
    s["attention_grad"].hop()
    s = sync(s)

    s["attention_grad"].hop()
    s["hidden"] = part_hidden_grads(s["order"], s.pop("feed_grad").terms(), part, data_count)
    s["hidden_got"] = [seq_swap(s["hidden"][1], 1)]
    s["a_two"] = seq_swap(add(s["a_part"][2], s["a_got"][1]), 2)
    s["y_two"] = add(s["y_part"][2], s["y_got"][1])
    s = sync(s)

    s["attention_grad"].hop()
    s["y_two"] = seq_swap(s["y_two"], 2)
    s = sync(s)

    s["attention_grad"].hop()
    s["hidden_got"] += [seq_swap(s["hidden"][m], m) for m in (2, 3)]
    s["input_gradient"], s["y"] = kernel_call(
        last,
        (block, block),
        s["a_part"][0],
        s["a_got"][0],
        s["a_two"],
        s["x"],
        s["mid_grad"],
        s["y_part"][0],
        s["y_got"][0],
        s["y_two"],
        s["x_mid"],
        s["table"],
    )
    s = sync(s)

    terms = s["attention_grad"].terms()
    high = attention_weights[0].shape[0]
    if ring:
        matrix = shape((high, part), F32)
        outs = (matrix,) * 4 + (shape((count, group), F32), shape((1, group), F32))
        *matrices, sums, bias_sum = kernel_call(finish, outs, *terms)
        grads = lax.dynamic_slice(sum_slot(sums), (0, me * each), (count, each))
        expand_bias_grad = bias_sum[0, :bias_length]
    else:
        grads = lax.dynamic_slice_in_dim(s["sums"], place * each, each, 1)
        expand_bias_grad = lax.dynamic_slice(s["sums"][:, width:], bias_at, (1, bias_length))[0]
        total = sum(t.astype(F32) for t in terms)
        matrices = [total[:, i * part : (i + 1) * part] for i in range(4)]
    expand_weight_grad, reduce_weight_grad = place_hidden_grads(
        s["order"], s["hidden"][:1] + s["hidden_got"], expand_weight.shape, reduce_weight.shape, data_count
    )
    return (
        s["y"][None],
        s["input_gradient"][None],
        grads[0],
        grads[1],
        matrices[0],
        grads[2],
        matrices[1],
        matrices[2],
        grads[3],
        matrices[3],
        grads[4],
        grads[5],
        grads[6],
        expand_weight_grad,
        expand_bias_grad,
        reduce_weight_grad,
        grads[7],
    )


def solution(mesh):
    vector = P(("dp", "seq"))
    matrix = P("dp", "seq")
    tokens = P("dp", "seq", None)
    return jax.shard_map(
        local,
        mesh=mesh,
        in_specs=(
            tokens,
            tokens,
            P("dp"),
            P(),
            vector,
            vector,
            matrix,
            vector,
            matrix,
            matrix,
            vector,
            matrix,
            vector,
            vector,
            vector,
            matrix,
            vector,
            matrix,
            vector,
        ),
        out_specs=(
            tokens,
            tokens,
            vector,
            vector,
            matrix,
            vector,
            matrix,
            matrix,
            vector,
            matrix,
            vector,
            vector,
            vector,
            matrix,
            vector,
            matrix,
            vector,
        ),
        check_vma=False,
    )
```

```python
import jax
import jax.numpy as jnp
from jax import lax
from jax.experimental import pallas as pl
from jax.experimental.pallas import tpu as pltpu
from jax.sharding import PartitionSpec as P

HEADS = 16
EPS = 1e-06
BF = jnp.bfloat16
F32 = jnp.float32
SEQ = 4
BLOCKS = 8
RING = 8
MIB = 1 << 20
VMEM = {
    "pack_columns": 60,
    "pack_hidden": 56,
    "join_hidden": 2,
    "stack_rows": 5,
    "norm_one": 8,
    "attend": 10,
    "middle": 14,
    "feed_forward": 12,
    "reduce_part": 8,
    "mask_rows": 4,
    "feed_grads": 6,
    "add_two": 2,
    "middle_back": 6,
    "attend_back": 12,
    "normed_back": 6,
    "attention_grads": 5,
    "part_hidden": 2,
    "place_hidden": 3,
    "last": 6,
    "finish": 3,
}
GAIN_ONE, SHIFT_ONE, BIAS_Q, BIAS_V, BIAS_O, GAIN_TWO, SHIFT_TWO, BIAS_R = (
    slice(i, i + 1) for i in range(8)
)


def mm(a, b):
    return lax.dot_general(a, b, (((1,), (0,)), ((), ())), preferred_element_type=F32)


def mm_nt(a, b):
    return lax.dot_general(a, b, (((1,), (1,)), ((), ())), preferred_element_type=F32)


def mm_tn(a, b):
    return lax.dot_general(a, b, (((0,), (0,)), ((), ())), preferred_element_type=F32)


def standardize(values):
    center = values - jnp.mean(values, axis=-1, keepdims=True)
    scale = lax.rsqrt(jnp.mean(center * center, axis=-1, keepdims=True) + EPS)
    return center * scale, scale


def rows_at(start, size):
    return pl.ds(pl.multiple_of(start, size), size)


def kernel_call(body, outs, *args, scratch=(), flops=0, far=()):
    specs = [
        pl.BlockSpec(memory_space=pltpu.SMEM if a.dtype == jnp.int32 else pltpu.VMEM) for a in args
    ]
    for i in far:
        specs[i] = pl.BlockSpec(memory_space=pl.ANY)
    moved = sum(a.size * a.dtype.itemsize for a in args)
    moved += sum(o.size * o.dtype.itemsize for o in outs)
    return pl.pallas_call(
        body,
        out_shape=tuple(outs),
        in_specs=specs,
        out_specs=tuple(pl.BlockSpec(memory_space=pltpu.VMEM) for _ in outs),
        scratch_shapes=list(scratch),
        compiler_params=pltpu.CompilerParams(vmem_limit_bytes=VMEM[body.__name__] * MIB),
        cost_estimate=pl.CostEstimate(flops=0, bytes_accessed=int(moved), transcendentals=0),
    )(*args)


def shape(dims, dtype):
    return jax.ShapeDtypeStruct(tuple(dims), dtype)


def norm_one(x0, x1, x2, x3, table, a_out, n_out, hold):
    rows, width = x0.shape
    for k, ref in enumerate((x0, x1, x2, x3)):
        normal, _ = standardize(ref[...].astype(F32))
        hold[k * rows : (k + 1) * rows, :] = normal
    normal = hold[...]
    n_out[...] = normal.astype(BF)
    a_out[...] = (normal * table[GAIN_ONE, :width] + table[SHIFT_ONE, :width]).astype(BF)


def mask_rows(c0, c1, c2, c3, factor, g_out, hold):
    rows = c0.shape[0]
    for k, ref in enumerate((c0, c1, c2, c3)):
        hold[k * rows : (k + 1) * rows, :] = ref[...].astype(F32)
    g_out[...] = (hold[...] * factor[...]).astype(BF)


def head_lanes(width, head, size):
    lane = lax.broadcasted_iota(jnp.int32, (1, width), 1)
    return (lane >= head * size) & (lane < (head + 1) * size)


def stack_rows(idx, order, *refs):
    w_qkv, w_low, w_high, table = refs[BLOCKS + 1 :]
    width, first = w_qkv.shape
    step = width // BLOCKS
    count = table.shape[0]
    wide = (table.shape[1] - width) // SEQ
    each = wide // SEQ
    table[...] = jnp.zeros_like(table)
    row = lax.broadcasted_iota(jnp.int32, (count, wide), 0)
    biases = jnp.zeros((count, wide), F32)
    for k in range(BLOCKS + 1):
        spot = idx[min(k, BLOCKS - 1)]
        at, size = spot * step, step
        if k >= BLOCKS - 1:
            size = step // 2
            at += size * (k - BLOCKS + 1)
        w_qkv[rows_at(at, size), :] = refs[k][:size, :first]

        @pl.when(at < width // 2)
        def _():
            w_low[rows_at(at, size), :] = refs[k][:size, first:]

        @pl.when(at >= width // 2)
        def _():
            w_high[rows_at(at - width // 2, size), :] = refs[k][:size, first:]

        if refs[k].shape[0] > size:
            below = refs[k][size:, :wide]
            placed = mm(below[:, :each], own_lanes(order, each, wide, each))
            table[:, rows_at(spot * wide, wide)] = placed[:count]
            biases = jnp.where(row == spot, below.astype(F32)[count : count + 1], biases)
    table[:, pl.ds(pl.multiple_of(width + order[0] * wide, wide), wide)] = biases


def copy_all(copies):
    for copy in copies:
        copy.start()
    for copy in copies:
        copy.wait()


def pack_columns(*refs):
    count = (len(refs) - 6) // 2
    weights, vectors = refs[:4], refs[4 : 4 + count]
    out, sems, hold = refs[4 + count : 7 + count]
    buffers = refs[7 + count :]
    high, wide = weights[0].shape
    copies = [
        pltpu.make_async_copy(w, out.at[:high, i * wide : (i + 1) * wide], sems.at[i])
        for i, w in enumerate(weights)
    ]
    small = [pltpu.make_async_copy(v, b, sems.at[4 + i]) for i, (v, b) in enumerate(zip(vectors, buffers))]
    for copy in small + copies:
        copy.start()
    hold[...] = jnp.zeros_like(hold)
    out[high:, :] = jnp.zeros((hold.shape[0], out.shape[1]), BF)
    for copy in small:
        copy.wait()
    for i, buffer in enumerate(buffers):
        size = buffer.shape[0]
        hold[i : i + 1, :size] = buffer[...].astype(F32).reshape(1, size)
    out[high:, : hold.shape[1]] = hold[...].astype(BF)
    for copy in copies:
        copy.wait()


def own_lanes(order, rows, wide, each):
    lane = lax.broadcasted_iota(jnp.int32, (rows, wide), 1)
    return (lane == order[0] * each + lax.broadcasted_iota(jnp.int32, (rows, wide), 0)).astype(BF)


def pack_hidden(order, w_expand, w_reduce, o0, o1, o2, o3, sems):
    step, part = w_expand.shape[0], w_reduce.shape[1]
    half = part // 2
    deep = w_expand.shape[1] // 2
    quarter = w_reduce.shape[0] // SEQ
    copies = []
    for m, out in enumerate((o0, o1, o2, o3)):
        one = rows_at(order[m] * half, half)
        two = pl.ds(pl.multiple_of(deep + order[m] * half, half), half)
        three = rows_at(order[m] * quarter, quarter)
        copies += [
            pltpu.make_async_copy(w_expand.at[:, one], out.at[:step, :half], sems.at[3 * m]),
            pltpu.make_async_copy(w_expand.at[:, two], out.at[:step, half:], sems.at[3 * m + 1]),
            pltpu.make_async_copy(w_reduce.at[three, :], out.at[step:, :], sems.at[3 * m + 2]),
        ]
    copy_all(copies)


def join_hidden(order, p0, p1, p2, p3, out):
    part = p0.shape[1]
    for m, ref in enumerate((p0, p1, p2, p3)):
        out[:, rows_at(order[m] * part, part)] = ref[...]


def part_hidden(order, e0, e1, e2, mine, *outs):
    part = mine.shape[1]
    for m in range(SEQ):
        lanes = rows_at(order[m] * part, part)
        e = e0[:, lanes].astype(F32) + e1[:, lanes].astype(F32) + e2[:, lanes].astype(F32)
        if m == 0:
            mine[...] = e
        else:
            outs[m - 1][...] = e.astype(BF)


def place_hidden(order, p0, p1, p2, p3, e_out, r_out):
    step, part = e_out.shape[0], p0.shape[1]
    half = part // 2
    deep = e_out.shape[1] // 2
    quarter = r_out.shape[0] // SEQ
    for m, ref in enumerate((p0, p1, p2, p3)):
        e_out[:, rows_at(order[m] * half, half)] = ref[:step, :half].astype(F32)
        e_out[:, pl.ds(pl.multiple_of(deep + order[m] * half, half), half)] = ref[:step, half:].astype(F32)
        r_out[rows_at(order[m] * quarter, quarter), :] = ref[step:, :].astype(F32)


def attend(order, a, w, table, key_mask, out, o_out, stat_out):
    width = o_out.shape[1]
    qkv = mm(a[...], w[...])
    mine = rows_at(order[0] * width, width)
    q = (qkv[:, :width] + table[BIAS_Q, mine]).astype(BF)
    key = qkv[:, width : 2 * width].astype(BF)
    value = (qkv[:, 2 * width :] + table[BIAS_V, mine]).astype(BF)
    out[:, :width] = q
    out[:, width : 2 * width] = key
    out[:, 2 * width :] = value
    size = width // (HEADS // SEQ)
    valid = key_mask[...] > 0
    total = None
    for h in range(HEADS // SEQ):
        lanes = head_lanes(width, h, size)
        logits = mm_nt(jnp.where(lanes, q, jnp.zeros_like(q)), key)
        scores = jnp.where(valid, logits * size ** (-0.5), -1000000000.0)
        top = jnp.max(scores, axis=-1, keepdims=True)
        weights = jnp.exp(scores - top)
        inverse = 1.0 / jnp.sum(weights, axis=-1, keepdims=True)
        probs = (weights * inverse).astype(BF)
        mixed = mm(probs, jnp.where(lanes, value, jnp.zeros_like(value)))
        total = mixed if total is None else total + mixed
        stat_out[:, h : h + 1] = top
        stat_out[:, HEADS // SEQ + h : HEADS // SEQ + h + 1] = inverse
    o_out[...] = total.astype(BF)


def middle(order, *refs):
    o = refs[:SEQ]
    w_low = refs[SEQ : 2 * SEQ]
    w_high = refs[2 * SEQ : 3 * SEQ]
    x = refs[3 * SEQ : 4 * SEQ]
    table, c_out, x_out, w_rows, hold, w = refs[4 * SEQ :]
    rows, full = x[0].shape
    width = o[0].shape[1]
    for m in range(SEQ):
        at = rows_at(order[m] * width, width)
        w[: full // 2, at] = w_low[m][...]
        w[full // 2 :, at] = w_high[m][...]
    w_rows[...] = w[rows_at(order[0] * width, width), :]
    for k in range(SEQ):
        hold[k * rows : (k + 1) * rows, :] = x[k][...].astype(F32) + table[BIAS_O, :full]
    for m in range(SEQ):
        part = mm(o[m][...], w[rows_at(order[m] * width, width), :])
        for k in range(SEQ):
            there = (k ^ m) * rows
            hold[there : there + rows, :] += part[k * rows : (k + 1) * rows, :]
    x_out[...] = hold[0:rows, :]
    normal, _ = standardize(hold[...])
    c_out[...] = (normal * table[GAIN_TWO, :full] + table[SHIFT_TWO, :full]).astype(BF)


def feed_forward(idx, order, c, g, table, *refs):
    pieces = refs[: BLOCKS + 1]
    h_out, u_out, bias_out, w_reduce, o0, o1, o2, o3, e_far, r_far, w_expand = refs[BLOCKS + 1 :]
    step = w_expand.shape[0] // BLOCKS
    for k in range(BLOCKS):
        at = rows_at(idx[k] * step, step)
        w_expand[at, :] = pieces[k][:step, :]
        last_piece = pieces[k] if k < BLOCKS - 1 else pieces[k + 1]
        w_reduce[at, :] = last_piece[last_piece.shape[0] - step :, :]
    width = h_out.shape[1]
    group = bias_out.shape[1]
    bias = table[:, pl.ds(pl.multiple_of(w_expand.shape[0] + order[0] * group, group), group)]
    chunk = 2 * group
    for n in range(0, width, chunk):
        r = n // group
        row = jnp.concatenate([bias[r : r + 1], bias[r + 1 : r + 2]], axis=1)
        u = mm(c[...], w_expand[:, n : n + chunk]) + row
        upper = mm_nt(g[...], w_reduce[n : n + chunk, :])
        cdf = 0.5 * (1.0 + lax.erf(u * (0.5**0.5)))
        density = jnp.exp(-0.5 * u * u) * 0.3989422804014327
        h_out[:, n : n + chunk] = (u * cdf).astype(BF)
        low = (upper * (cdf + u * density)).astype(BF)
        u_out[:, n : n + chunk] = low
        total = jnp.sum(low.astype(F32), axis=0, keepdims=True)
        bias_out[r : r + 1, :] = total[:, :group]
        bias_out[r + 1 : r + 2, :] = total[:, group:]
    lower = mm_nt(u_out[...], w_expand[...])
    rows = o0.shape[0]
    for k, out in enumerate((o0, o1, o2, o3)):
        out[...] = lower[k * rows : (k + 1) * rows, :].astype(BF)
    at = rows_at(idx[BLOCKS - 1] * step, step)
    e_far[...] = mm_tn(c[:, at], u_out[...]).astype(BF)
    r_far[...] = mm_tn(h_out[:, at], g[...]).astype(BF)


def reduce_part(h, w, *outs):
    y = mm(h[...], w[...])
    rows = outs[0].shape[0]
    for k in range(SEQ):
        outs[k][...] = y[k * rows : (k + 1) * rows, :].astype(BF)


def feed_grads(idx, c, du, h, g, *outs):
    step = outs[0].shape[0] // 2
    for k in range(BLOCKS - 1):
        at = rows_at(idx[k] * step, step)
        outs[k][:step, :] = mm_tn(c[:, at], du[...]).astype(BF)
        outs[k][step:, :] = mm_tn(h[:, at], g[...]).astype(BF)


def add_two(a, a_own, b, b_own, a_out, b_out):
    here = a.shape[0]
    rest = b_own.shape[0] - b.shape[0]
    a_out[:here, :] = (a[...].astype(F32) + a_own[:here, :].astype(F32)).astype(BF)
    b_out[rest:, :] = (b[...].astype(F32) + b_own[rest:, :].astype(F32)).astype(BF)
    if rest:
        a_out[here:, :] = a_own[here:, :]
        b_out[:rest, :] = b_own[:rest, :]


def norm_pull(upper, normal, scale, gain):
    inner = upper * gain
    return scale * (
        inner
        - jnp.mean(inner, axis=-1, keepdims=True)
        - normal * jnp.mean(inner * normal, axis=-1, keepdims=True)
    )


def middle_back(part0, part1, part2, x, cot, factor, table, grad_out, low_out, sums_out):
    upper = part0[...].astype(F32) + part1[...].astype(F32) + part2[...].astype(F32)
    normal, scale = standardize(x[...])
    upstream = cot[...].astype(F32) * factor[...]
    grad = upstream + norm_pull(upper, normal, scale, table[GAIN_TWO, : x.shape[1]])
    low = grad.astype(BF)
    grad_out[...] = grad
    low_out[...] = low
    sums_out[0:1, :] = jnp.sum(upper * normal, axis=0, keepdims=True)
    sums_out[1:2, :] = jnp.sum(upper, axis=0, keepdims=True)
    sums_out[2:3, :] = jnp.sum(low.astype(F32), axis=0, keepdims=True)
    sums_out[3:4, :] = jnp.sum(upstream, axis=0, keepdims=True)


def attend_back(order, *refs):
    grads = refs[:SEQ]
    w_rows, qkv, stat, key_mask, g_out, out, sums_out, hold = refs[SEQ:]
    rows = grads[0].shape[0]
    for k in range(SEQ):
        hold[k * rows : (k + 1) * rows, :] = grads[k][...].astype(F32)
    g_out[...] = hold[...].astype(BF)
    width = qkv.shape[1] // 3
    size = width // (HEADS // SEQ)
    d_out = mm_nt(g_out[...], w_rows[...]).astype(BF)
    q, key, value = (qkv[:, i * width : (i + 1) * width] for i in range(3))
    valid = key_mask[...] > 0
    dq = dk = dv = None
    for h in range(HEADS // SEQ):
        lanes = head_lanes(width, h, size)
        q_h = jnp.where(lanes, q, jnp.zeros_like(q))
        d_h = jnp.where(lanes, d_out, jnp.zeros_like(d_out))
        logits = mm_nt(q_h, key)
        scores = jnp.where(valid, logits * size ** (-0.5), -1000000000.0)
        top = stat[:, h : h + 1]
        inverse = stat[:, HEADS // SEQ + h : HEADS // SEQ + h + 1]
        probs = jnp.exp(scores - top) * inverse
        prob_grad = mm_nt(d_h, value)
        center = jnp.sum(probs * prob_grad, axis=-1, keepdims=True)
        low = jnp.where(valid, probs * (prob_grad - center) * size ** (-0.5), 0.0).astype(BF)
        dv_h = mm_tn(probs.astype(BF), d_h)
        dk_h = mm_tn(low, q_h)
        dq_h = mm(low, jnp.where(lanes, key, jnp.zeros_like(key)))
        dq = dq_h if dq is None else dq + dq_h
        dk = dk_h if dk is None else dk + dk_h
        dv = dv_h if dv is None else dv + dv_h
    dq, dk, dv = dq.astype(BF), dk.astype(BF), dv.astype(BF)
    out[:, :width] = dq
    out[:, width : 2 * width] = dk
    out[:, 2 * width :] = dv
    sums_out[0:1, :] = jnp.sum(dq.astype(F32), axis=0, keepdims=True)
    sums_out[1:2, :] = jnp.sum(dv.astype(F32), axis=0, keepdims=True)


def attention_grads(idx, order, a, d, g, sums, *refs):
    o = refs[:SEQ]
    outs = refs[SEQ : SEQ + BLOCKS + 1]
    hold, turned = refs[SEQ + BLOCKS + 1 :]
    rows = g.shape[0] // SEQ
    width = o[0].shape[1]
    full = hold.shape[0]
    step = full // BLOCKS
    mine = g[:, rows_at(order[0] * width, width)].astype(F32)
    for m in range(SEQ):
        for k in range(SEQ):
            there = (k ^ m) * rows
            turned[k * rows : (k + 1) * rows, :] = mine[there : there + rows, :]
        hold[rows_at(order[m] * width, width), :] = mm_tn(o[m][...], turned[...].astype(BF)).astype(BF)
    count, wide = sums.shape[0], step
    biases = sums[:, pl.ds(pl.multiple_of(full + order[0] * wide, wide), wide)]
    row = lax.broadcasted_iota(jnp.int32, biases.shape, 0)
    for k in range(BLOCKS):
        at = rows_at(idx[k] * step, step)
        value = mm_tn(a[:, at], d[...]).astype(BF)
        size = step if k < BLOCKS - 1 else step // 2
        outs[k][:size, : 3 * width] = value[:size]
        outs[k][:size, 3 * width :] = hold[rows_at(idx[k] * step, size), :]
        below = outs[k]
        if k == BLOCKS - 1:
            below = outs[k + 1]
            below[:size, : 3 * width] = value[size:]
            below[:size, 3 * width :] = hold[rows_at(idx[k] * step + size, size), :]
        if below.shape[0] > size:
            extra = below.shape[0] - size
            bias = jnp.sum(jnp.where(row == idx[k], biases, 0.0), axis=0, keepdims=True)
            bias = jnp.broadcast_to(bias, (extra - count, wide))
            block = jnp.concatenate([sums[:, rows_at(idx[k] * wide, wide)], bias], axis=0)
            below[size:, :wide] = block.astype(BF)
            below[size:, wide:] = jnp.zeros((extra, below.shape[1] - wide), BF)


def normed_back(order, d, w, normal, sums_qv, sums_mid, sum_e, sums, *outs):
    rows, width = outs[0].shape
    part, wide = sums_qv.shape[1], sum_e.shape[1]
    upper = mm_nt(d[...], w[...])
    for k in range(SEQ):
        outs[k][...] = upper[k * rows : (k + 1) * rows, :].astype(BF)
    sums[...] = jnp.zeros_like(sums)
    sums[GAIN_ONE, :width] = jnp.sum(upper * normal[...].astype(F32), axis=0, keepdims=True)
    sums[SHIFT_ONE, :width] = jnp.sum(upper, axis=0, keepdims=True)
    mine = rows_at(order[0] * part, part)
    sums[BIAS_Q, mine] = sums_qv[0:1, :]
    sums[BIAS_V, mine] = sums_qv[1:2, :]
    sums[BIAS_O, :width] = sums_mid[2:3, :]
    sums[GAIN_TWO, :width] = sums_mid[0:1, :]
    sums[SHIFT_TWO, :width] = sums_mid[1:2, :]
    sums[BIAS_R, :width] = sums_mid[3:4, :]
    sums[:, pl.ds(pl.multiple_of(width + order[0] * wide, wide), wide)] = sum_e[...]


def last(part0, part1, part2, x, grad, y0, y1, y2, x_mid, table, grad_out, y_out):
    width = x.shape[1]
    upper = part0[...].astype(F32) + part1[...].astype(F32) + part2[...].astype(F32)
    normal, scale = standardize(x[...].astype(F32))
    grad_out[...] = (grad[...] + norm_pull(upper, normal, scale, table[GAIN_ONE, :width])).astype(BF)
    y = x_mid[...] + table[BIAS_R, :width] + y0[...].astype(F32)
    y_out[...] = (y + y1[...].astype(F32) + y2[...].astype(F32)).astype(BF)


def finish(p0, p1, p2, w0, w1, w2, w3, sums, bias):
    high, part = w0.shape
    count, wide = sums.shape
    for i, out in enumerate((w0, w1, w2, w3)):
        at = slice(i * part, (i + 1) * part)
        out[...] = p0[:high, at].astype(F32) + p1[:high, at].astype(F32) + p2[:high, at].astype(F32)
    below = p0[high:, :wide].astype(F32) + p1[high:, :wide].astype(F32) + p2[high:, :wide].astype(F32)
    sums[...] = below[:count]
    bias[...] = below[count : count + 1]


def seq_swap(value, flip):
    return lax.ppermute(value, "seq", [(s, s ^ flip) for s in range(SEQ)])


def after(value, *others):
    return lax.optimization_barrier((value,) + others)[0]


def add(a, b):
    return (a.astype(F32) + b.astype(F32)).astype(BF)


def ring_order(data_count):
    return list(range(0, data_count, 2)) + list(range(data_count - 1, 0, -2))


def ring_hop(value, data_count, step):
    ring = ring_order(data_count)
    pairs = [(ring[r], ring[(r + step) % data_count]) for r in range(data_count)]
    return lax.ppermute(value, "dp", pairs)


RELATIVE = (0, -1, -2, -3, 1, 2, 3, 4)


def relative_order(data_count):
    if data_count != RING:
        return jnp.arange(BLOCKS, dtype=jnp.int32)
    me = lax.axis_index("dp")
    z, y = me // 2, me % 2
    place = jnp.where(y == 0, z, BLOCKS - 1 - z)
    there = (place + jnp.array(RELATIVE, dtype=jnp.int32) + BLOCKS) % BLOCKS
    half = BLOCKS // 2
    return jnp.where(there < half, 2 * there, 2 * (BLOCKS - 1 - there) + 1).astype(jnp.int32)


@jax.tree_util.register_pytree_node_class
class Gather:
    def __init__(self, value, data_count, parts, cut, back=(), front=()):
        self.value, self.data_count, self.parts, self.cut = value, data_count, parts, cut
        self.back, self.front = list(back), list(front)

    def tree_flatten(self):
        return (self.value, self.back, self.front), (self.data_count, self.parts, self.cut)

    @classmethod
    def tree_unflatten(cls, aux, parts):
        return cls(parts[0], *aux, *parts[1:])

    def hop(self):
        if self.data_count != RING:
            if not self.back:
                whole = lax.all_gather(self.value, "dp", axis=0, tiled=False)
                parts = [p.reshape((BLOCKS, -1) + p.shape[2:]) for p in jnp.split(whole, self.parts, axis=1)]
                self.back = list(jnp.concatenate(parts, axis=1))
            return
        back, front = (self.back or [self.value])[-1], (self.front or [self.value])[-1]
        if len(self.back) == BLOCKS // 2 - 1:
            back, front = back[: self.cut], front[self.cut :]
        self.back.append(ring_hop(back, self.data_count, 1))
        self.front.append(ring_hop(front, self.data_count, -1))

    def blocks(self, last=(0, 1)):
        if self.data_count != RING:
            halves = (self.back[-1][: self.cut], self.back[-1][self.cut :])
            return self.back[:-1] + [halves[i] for i in last]
        halves = (self.back[3], self.front[3])
        return [self.value] + self.back[:3] + self.front[:3] + [halves[i] for i in last]


@jax.tree_util.register_pytree_node_class
class Scatter:
    def __init__(self, pieces, data_count, parts, hops=0, left=None, right=None):
        self.pieces, self.data_count, self.parts = pieces, data_count, parts
        self.hops, self.left, self.right = hops, left, right

    def tree_flatten(self):
        return (self.pieces, self.left, self.right), (self.data_count, self.parts, self.hops)

    @classmethod
    def tree_unflatten(cls, aux, parts):
        return cls(parts[0], *aux, *parts[1:])

    def hop(self):
        n, self.hops = self.hops, self.hops + 1
        if self.data_count != RING:
            if n == 0:
                whole = jnp.concatenate(self.pieces, axis=0)
                wide = whole.shape[1]
                whole = whole.reshape(BLOCKS, self.parts, self.data_count // BLOCKS, -1, wide)
                whole = whole.transpose(0, 2, 1, 3, 4).reshape(-1, wide)
                self.left = lax.psum_scatter(whole, "dp", scatter_dimension=0, tiled=True)
            return self.left
        own = dict(zip(RELATIVE, self.pieces))
        left, right = self.left, self.right
        if n == 0:
            left, right = self.pieces[-2:]
        else:
            ahead, behind = own[4 - n], own[n - 4]
            outs = (shape(ahead.shape, BF),) * 2
            left, right = kernel_call(add_two, outs, left, ahead, right, behind)
        self.left = ring_hop(left, self.data_count, 1)
        self.right = ring_hop(right, self.data_count, -1)
        return left

    def terms(self):
        if self.data_count != RING:
            return [self.left, jnp.zeros_like(self.left), jnp.zeros_like(self.left)]
        return [self.pieces[0], self.left, self.right]


def sum_slot(value):
    value = value + seq_swap(value, 1)
    return value + seq_swap(value, 2)


def trade(parts, data_count):
    return [parts[0]] + [seq_swap(parts[m], m) for m in range(1, SEQ)]


def pack_hidden_weights(order, w_expand, w_reduce, data_count):
    high, low, part = w_expand.shape[0], w_reduce.shape[0] // SEQ, w_reduce.shape[1]
    if data_count == RING:
        piece = shape((high + low, part), BF)
        sems = [pltpu.SemaphoreType.DMA((3 * SEQ,))]
        return list(
            kernel_call(pack_hidden, (piece,) * SEQ, order, w_expand, w_reduce, far=(1, 2), scratch=sems)
        )
    e = w_expand.reshape(high, -1, SEQ, low).transpose(2, 0, 1, 3).reshape(SEQ, high, part)
    both = jnp.concatenate([e, w_reduce.reshape(SEQ, low, part)], axis=1)
    return [lax.dynamic_index_in_dim(both, order[m], 0, False) for m in range(SEQ)]


def join_hidden_weights(order, parts, data_count):
    rows, part = parts[0].shape
    if data_count == RING:
        return kernel_call(join_hidden, (shape((rows, SEQ * part), BF),), order, *parts)[0]
    both = jnp.zeros((rows, SEQ * part), BF)
    for m in range(SEQ):
        both = lax.dynamic_update_slice(both, parts[m], (0, order[m] * part))
    return both


def part_hidden_grads(order, terms, part, data_count):
    if data_count == RING:
        piece = (terms[0].shape[0], part)
        outs = (shape(piece, F32),) + (shape(piece, BF),) * (SEQ - 1)
        return list(kernel_call(part_hidden, outs, order, *terms))
    return [lax.dynamic_slice_in_dim(terms[0], order[m] * part, part, 1) for m in range(SEQ)]


def place_hidden_grads(order, parts, e_shape, r_shape, data_count):
    if data_count == RING:
        outs = (shape(e_shape, F32), shape(r_shape, F32))
        return kernel_call(place_hidden, outs, order, *parts)
    high, low = e_shape[0], r_shape[0] // SEQ
    both = jnp.zeros((SEQ,) + parts[0].shape, F32)
    for m in range(SEQ):
        both = lax.dynamic_update_slice(both, parts[m].astype(F32)[None], (order[m], 0, 0))
    e = both[:, :high].reshape(SEQ, high, -1, low).transpose(1, 2, 0, 3).reshape(e_shape)
    return e, both[:, high:].reshape(r_shape)


def eight(deep, wide):
    return (shape((deep, wide), BF),) * (BLOCKS - 1) + (shape((deep // 2, wide), BF),) * 2


def sync(state):
    return lax.optimization_barrier(state)


def local(
    block_input,
    cotangent,
    image_valid,
    token_valid,
    first_gain,
    first_shift,
    query_weight,
    query_bias,
    key_weight,
    value_weight,
    value_bias,
    output_weight,
    output_bias,
    second_gain,
    second_shift,
    expand_weight,
    expand_bias,
    reduce_weight,
    reduce_bias,
):
    data_count = lax.axis_size("dp")
    ring = data_count == RING
    me = lax.axis_index("seq")
    rows, width = block_input.shape[1:]
    tokens = rows * SEQ
    part = width // SEQ
    deep = expand_weight.shape[1]
    step = width // BLOCKS
    full = shape((tokens, width), BF)
    block = shape((rows, width), BF)
    s = {}
    s["idx"] = relative_order(data_count)
    dp = lax.axis_index("dp")
    s["order"] = jnp.stack([me ^ k for k in range(SEQ)] + [dp]).astype(jnp.int32)

    vectors = (
        first_gain,
        first_shift,
        query_bias,
        value_bias,
        output_bias,
        second_gain,
        second_shift,
        reduce_bias,
    )
    each = first_gain.shape[0]
    place = dp * SEQ + me
    count = len(vectors)
    group = deep // BLOCKS
    bias_row = expand_bias.astype(F32)[None]
    bias_length = expand_bias.shape[0]
    bias_at = dp * bias_length
    bias_at = (bias_at // group, me * group + bias_at % group)
    table = shape((count, width + SEQ * group), F32)

    valid = token_valid.astype(F32).reshape(SEQ, rows)
    valid = jnp.concatenate([lax.dynamic_slice_in_dim(valid, s["order"][k], 1, 0) for k in range(SEQ)], axis=1)
    s["valid"] = valid
    s["factor"] = (valid * image_valid.astype(F32)[0]).reshape(tokens, 1)

    attention_weights = (query_weight, key_weight, value_weight, output_weight)
    extra = 2 * count if ring else 0
    if ring:
        args = attention_weights + vectors + (expand_bias,)
        scratch = [pltpu.SemaphoreType.DMA((len(args),)), pltpu.VMEM((extra, group), F32)]
        scratch += [pltpu.VMEM(v.shape, BF) for v in args[4:]]
        outs = (shape((step + extra, width), BF),)
        (piece,) = kernel_call(pack_columns, outs, *args, far=range(len(args)), scratch=scratch)
    else:
        piece = jnp.concatenate(attention_weights, axis=1)
    s["attention"] = Gather(piece, data_count, 1, step // 2)
    s["attention"].hop()
    s["x"] = [block_input[0]]
    s["x"] += [seq_swap(s["x"][0], m) for m in (1, 2)]
    s["cot"] = [cotangent[0]]
    s["hidden"] = pack_hidden_weights(s["order"], expand_weight, reduce_weight, data_count)
    s = sync(s)

    s["attention"].hop()
    hidden = s.pop("hidden")
    s["hidden"] = [hidden[0]] + [seq_swap(hidden[m], m) for m in (1, 2)]
    s["hidden_last"] = hidden[3]
    s = sync(s)

    s["attention"].hop()
    s["hidden"].append(seq_swap(s.pop("hidden_last"), 3))
    s["x"].append(seq_swap(s["x"][2], 1))
    s["cot"].append(seq_swap(s["cot"][0], 2))
    s = sync(s)

    s["attention"].hop()
    s["cot"] = [s["cot"][0], seq_swap(s["cot"][0], 1), s["cot"][1], seq_swap(s["cot"][1], 1)]
    feed = join_hidden_weights(s["order"], s.pop("hidden"), data_count)
    s["feed"] = Gather(feed, data_count, 2, step)
    s = sync(s)

    s["feed"].hop()
    half = shape((width // 2, part), BF)
    s["w_qkv"], w_low, w_high, s["table"] = kernel_call(
        stack_rows,
        (shape((width, 3 * part), BF), half, half, table),
        s["idx"],
        s["order"],
        *s.pop("attention").blocks(),
    )
    s["w_low"], s["w_high"] = [w_low], [w_high]
    s["w_low"].append(seq_swap(after(w_low, s["w_qkv"]), 2))
    if ring:
        s["table"] = sum_slot(s["table"])
    else:
        every = lax.broadcasted_iota(jnp.int32, (each, width), 1)
        every = every == place * each + lax.broadcasted_iota(jnp.int32, (each, width), 0)
        stacked = sum(
            jnp.pad(v[None], ((i, count - 1 - i), (0, 0))) for i, v in enumerate(vectors)
        )
        placed = jnp.dot(stacked, every.astype(BF), preferred_element_type=F32)
        placed_bias = lax.dynamic_update_slice(
            jnp.zeros((count, table.shape[1] - width), F32), bias_row, bias_at
        )
        s["table"] = lax.psum(jnp.concatenate([placed, placed_bias], axis=1), ("dp", "seq"))
    s = sync(s)

    s["feed"].hop()
    s["w_high"] += [seq_swap(s["w_high"][0], m) for m in (1, 2)]
    s["a"], s["normal"] = kernel_call(
        norm_one, (full, full), *s["x"], s["table"], scratch=[pltpu.VMEM((tokens, width), F32)]
    )
    s["qkv"], o, s["stat"] = kernel_call(
        attend,
        (shape((tokens, 3 * part), BF), shape((tokens, part), BF), shape((tokens, 128), F32)),
        s["order"],
        s["a"],
        s["w_qkv"],
        s["table"],
        s["valid"],
        flops=2 * tokens * part * (3 * width + 8 * tokens),
    )
    s["o"] = [o]
    s = sync(s)

    s["feed"].hop()
    s["o"].append(seq_swap(s["o"][0], 2))
    (s["g"],) = kernel_call(
        mask_rows, (full,), *s["cot"], s["factor"], scratch=[pltpu.VMEM((tokens, width), F32)]
    )
    s["cot"] = s["cot"][0]
    s["w_low"].append(seq_swap(s["w_low"][1], 1))
    s = sync(s)

    s["feed"].hop()
    o_mine, o_two = s["o"]
    s["o"] = [o_mine, seq_swap(o_mine, 1), o_two, seq_swap(o_two, 1)]
    s["w_high"].append(seq_swap(s["w_high"][2], 1))
    s["w_low"].insert(1, seq_swap(s["w_low"][0], 1))
    s["c"], s["x_mid"], s["w_rows"] = kernel_call(
        middle,
        (full, shape((rows, width), F32), shape((part, width), BF)),
        s["order"],
        *s["o"],
        *s.pop("w_low"),
        *s.pop("w_high"),
        *s["x"],
        s["table"],
        scratch=[pltpu.VMEM((tokens, width), F32), pltpu.VMEM((width, width), BF)],
        flops=2 * tokens * width * width,
    )
    s["x"] = s["x"][0]
    s = sync(s)

    h, du, s["sum_e"], w_r, *c_part, e_far, r_far = kernel_call(
        feed_forward,
        (
            shape((tokens, deep), BF),
            shape((tokens, deep), BF),
            shape((BLOCKS, group), F32),
            shape((deep, width), BF),
            block,
            block,
            block,
            block,
            shape((step, deep), BF),
            shape((step, width), BF),
        ),
        s["idx"],
        s["order"],
        s["c"],
        s["g"],
        s["table"],
        *s.pop("feed").blocks(),
        scratch=[pltpu.VMEM((width, deep), BF)],
        flops=7 * tokens * width * deep,
    )
    s["c_part"] = c_part
    s["c_got"] = [seq_swap(c_part[m], 1) for m in (1, 3)]
    far = [e_far, r_far]
    args = (s["idx"], s.pop("c"), du, h, s.pop("g"))
    s["c_two"] = seq_swap(add(after(s["c_part"][2], s["c_got"][0]), s["c_got"][1]), 2)
    pieces = kernel_call(
        feed_grads,
        (shape((2 * step, deep), BF),) * (BLOCKS - 1),
        after(args[0], far[0]),
        *args[1:],
        flops=3 * tokens * width * deep,
    )
    s["feed_grad"] = Scatter(list(pieces) + list(far), data_count, 2)
    s["feed_grad"].hop()
    s["y_part"] = kernel_call(
        reduce_part,
        (block, block, block, block),
        after(h, pieces[0]),
        w_r,
        flops=2 * tokens * width * deep,
    )
    s = sync(s)

    s["mid_grad"], branch, s["sums_mid"] = kernel_call(
        middle_back,
        (shape((rows, width), F32), block, shape((4, width), F32)),
        s.pop("c_part")[0],
        s.pop("c_got")[0],
        s.pop("c_two"),
        s["x_mid"],
        s["cot"],
        s["factor"][:rows],
        s["table"],
    )
    branch_two = seq_swap(branch, 2)
    s["feed_grad"].hop()
    s["y_got"] = [seq_swap(s["y_part"][1], 1)]
    s["branch"] = [branch, branch_two]
    s = sync(s)

    branch, branch_two = s.pop("branch")
    s["branch"] = [branch, seq_swap(branch, 1), branch_two, seq_swap(branch_two, 1)]
    s["feed_grad"].hop()
    s["y_got"].append(seq_swap(s["y_part"][3], 1))
    s["branch_full"], s["dqkv"], s["sums_qv"] = kernel_call(
        attend_back,
        (full, shape((tokens, 3 * part), BF), shape((2, part), F32)),
        s["order"],
        *s.pop("branch"),
        s.pop("w_rows"),
        s.pop("qkv"),
        s.pop("stat"),
        s["valid"],
        scratch=[pltpu.VMEM((tokens, width), F32)],
        flops=2 * tokens * part * (width + 20 * tokens),
    )
    s = sync(s)

    sent = s["feed_grad"].hop()
    s["sums"], *s["a_part"] = kernel_call(
        normed_back,
        (table, block, block, block, block),
        s["order"],
        after(s["dqkv"], sent),
        s.pop("w_qkv"),
        s.pop("normal"),
        s.pop("sums_qv"),
        s.pop("sums_mid"),
        s.pop("sum_e"),
        flops=6 * tokens * width * part,
    )
    if not ring:
        s["sums"] = lax.psum(s["sums"], ("dp", "seq"))
    s["a_got"] = [seq_swap(s["a_part"][m], 1) for m in (1, 3)]
    half = step // 2
    pieces = kernel_call(
        attention_grads,
        (shape((step + extra, width), BF),) * (BLOCKS - 1)
        + (shape((half, width), BF), shape((half + extra, width), BF)),
        s["idx"],
        s["order"],
        after(s.pop("a"), *s["a_got"]),
        s.pop("dqkv"),
        s.pop("branch_full"),
        s["sums"],
        *s.pop("o"),
        scratch=[pltpu.VMEM((width, part), BF), pltpu.VMEM((tokens, part), F32)],
        flops=8 * tokens * width * part,
    )
    s["attention_grad"] = Scatter(list(pieces), data_count, 1)
    s["attention_grad"].hop()
    s = sync(s)

    s["attention_grad"].hop()
    s["hidden"] = part_hidden_grads(s["order"], s.pop("feed_grad").terms(), part, data_count)
    s["hidden_got"] = [seq_swap(s["hidden"][1], 1)]
    s["a_two"] = seq_swap(add(s["a_part"][2], s["a_got"][1]), 2)
    s["y_two"] = add(s["y_part"][2], s["y_got"][1])
    s = sync(s)

    s["attention_grad"].hop()
    s["y_two"] = seq_swap(s["y_two"], 2)
    s = sync(s)

    s["attention_grad"].hop()
    s["hidden_got"] += [seq_swap(s["hidden"][m], m) for m in (2, 3)]
    s["input_gradient"], s["y"] = kernel_call(
        last,
        (block, block),
        s["a_part"][0],
        s["a_got"][0],
        s["a_two"],
        s["x"],
        s["mid_grad"],
        s["y_part"][0],
        s["y_got"][0],
        s["y_two"],
        s["x_mid"],
        s["table"],
    )
    s = sync(s)

    terms = s["attention_grad"].terms()
    high = attention_weights[0].shape[0]
    if ring:
        matrix = shape((high, part), F32)
        outs = (matrix,) * 4 + (shape((count, group), F32), shape((1, group), F32))
        *matrices, sums, bias_sum = kernel_call(finish, outs, *terms)
        grads = lax.dynamic_slice(sum_slot(sums), (0, me * each), (count, each))
        expand_bias_grad = bias_sum[0, :bias_length]
    else:
        grads = lax.dynamic_slice_in_dim(s["sums"], place * each, each, 1)
        expand_bias_grad = lax.dynamic_slice(s["sums"][:, width:], bias_at, (1, bias_length))[0]
        total = sum(t.astype(F32) for t in terms)
        matrices = [total[:, i * part : (i + 1) * part] for i in range(4)]
    expand_weight_grad, reduce_weight_grad = place_hidden_grads(
        s["order"], s["hidden"][:1] + s["hidden_got"], expand_weight.shape, reduce_weight.shape, data_count
    )
    return (
        s["y"][None],
        s["input_gradient"][None],
        grads[0],
        grads[1],
        matrices[0],
        grads[2],
        matrices[1],
        matrices[2],
        grads[3],
        matrices[3],
        grads[4],
        grads[5],
        grads[6],
        expand_weight_grad,
        expand_bias_grad,
        reduce_weight_grad,
        grads[7],
    )


def solution(mesh):
    vector = P(("dp", "seq"))
    matrix = P("dp", "seq")
    tokens = P("dp", "seq", None)
    return jax.shard_map(
        local,
        mesh=mesh,
        in_specs=(
            tokens,
            tokens,
            P("dp"),
            P(),
            vector,
            vector,
            matrix,
            vector,
            matrix,
            matrix,
            vector,
            matrix,
            vector,
            vector,
            vector,
            matrix,
            vector,
            matrix,
            vector,
        ),
        out_specs=(
            tokens,
            tokens,
            vector,
            vector,
            matrix,
            vector,
            matrix,
            matrix,
            vector,
            matrix,
            vector,
            vector,
            vector,
            matrix,
            vector,
            matrix,
            vector,
        ),
        check_vma=False,
    )
```

```python
import jax
import jax.numpy as jnp
from jax import lax
from jax.experimental import pallas as pl
from jax.experimental.pallas import tpu as pltpu
from jax.sharding import PartitionSpec as P

HEADS = 16
EPS = 1e-06
BF = jnp.bfloat16
F32 = jnp.float32
SEQ = 4
BLOCKS = 8
RING = 8
MIB = 1 << 20
VMEM = {
    "pack_columns": 60,
    "pack_hidden": 56,
    "join_hidden": 2,
    "stack_rows": 5,
    "norm_one": 8,
    "attend": 10,
    "middle": 14,
    "feed_forward": 12,
    "reduce_part": 8,
    "mask_rows": 4,
    "feed_grads": 6,
    "add_two": 2,
    "middle_back": 6,
    "attend_back": 12,
    "normed_back": 6,
    "attention_grads": 5,
    "part_hidden": 2,
    "place_hidden": 3,
    "last": 6,
    "finish": 3,
}
GAIN_ONE, SHIFT_ONE, BIAS_Q, BIAS_V, BIAS_O, GAIN_TWO, SHIFT_TWO, BIAS_R = (
    slice(i, i + 1) for i in range(8)
)


def mm(a, b):
    return lax.dot_general(a, b, (((1,), (0,)), ((), ())), preferred_element_type=F32)


def mm_nt(a, b):
    return lax.dot_general(a, b, (((1,), (1,)), ((), ())), preferred_element_type=F32)


def mm_tn(a, b):
    return lax.dot_general(a, b, (((0,), (0,)), ((), ())), preferred_element_type=F32)


def standardize(values):
    center = values - jnp.mean(values, axis=-1, keepdims=True)
    scale = lax.rsqrt(jnp.mean(center * center, axis=-1, keepdims=True) + EPS)
    return center * scale, scale


def rows_at(start, size):
    return pl.ds(pl.multiple_of(start, size), size)


def kernel_call(body, outs, *args, scratch=(), flops=0, far=()):
    specs = [
        pl.BlockSpec(memory_space=pltpu.SMEM if a.dtype == jnp.int32 else pltpu.VMEM) for a in args
    ]
    for i in far:
        specs[i] = pl.BlockSpec(memory_space=pl.ANY)
    moved = sum(a.size * a.dtype.itemsize for a in args)
    moved += sum(o.size * o.dtype.itemsize for o in outs)
    return pl.pallas_call(
        body,
        out_shape=tuple(outs),
        in_specs=specs,
        out_specs=tuple(pl.BlockSpec(memory_space=pltpu.VMEM) for _ in outs),
        scratch_shapes=list(scratch),
        compiler_params=pltpu.CompilerParams(vmem_limit_bytes=VMEM[body.__name__] * MIB),
        cost_estimate=pl.CostEstimate(flops=0, bytes_accessed=int(moved), transcendentals=0),
    )(*args)


def shape(dims, dtype):
    return jax.ShapeDtypeStruct(tuple(dims), dtype)


def norm_one(x0, x1, x2, x3, table, a_out, n_out, hold):
    rows, width = x0.shape
    for k, ref in enumerate((x0, x1, x2, x3)):
        normal, _ = standardize(ref[...].astype(F32))
        hold[k * rows : (k + 1) * rows, :] = normal
    normal = hold[...]
    n_out[...] = normal.astype(BF)
    a_out[...] = (normal * table[GAIN_ONE, :width] + table[SHIFT_ONE, :width]).astype(BF)


def mask_rows(c0, c1, c2, c3, factor, g_out, hold):
    rows = c0.shape[0]
    for k, ref in enumerate((c0, c1, c2, c3)):
        hold[k * rows : (k + 1) * rows, :] = ref[...].astype(F32)
    g_out[...] = (hold[...] * factor[...]).astype(BF)


def head_lanes(width, head, size):
    lane = lax.broadcasted_iota(jnp.int32, (1, width), 1)
    return (lane >= head * size) & (lane < (head + 1) * size)


def stack_rows(idx, order, *refs):
    w_qkv, w_low, w_high, table = refs[BLOCKS + 1 :]
    width, first = w_qkv.shape
    step = width // BLOCKS
    count = table.shape[0]
    wide = (table.shape[1] - width) // SEQ
    each = wide // SEQ
    table[...] = jnp.zeros_like(table)
    row = lax.broadcasted_iota(jnp.int32, (count, wide), 0)
    biases = jnp.zeros((count, wide), F32)
    for k in range(BLOCKS + 1):
        spot = idx[min(k, BLOCKS - 1)]
        at, size = spot * step, step
        if k >= BLOCKS - 1:
            size = step // 2
            at += size * (k - BLOCKS + 1)
        w_qkv[rows_at(at, size), :] = refs[k][:size, :first]

        @pl.when(at < width // 2)
        def _():
            w_low[rows_at(at, size), :] = refs[k][:size, first:]

        @pl.when(at >= width // 2)
        def _():
            w_high[rows_at(at - width // 2, size), :] = refs[k][:size, first:]

        if refs[k].shape[0] > size:
            below = refs[k][size:, :wide]
            placed = mm(below[:, :each], own_lanes(order, each, wide, each))
            table[:, rows_at(spot * wide, wide)] = placed[:count]
            biases = jnp.where(row == spot, below.astype(F32)[count : count + 1], biases)
    table[:, pl.ds(pl.multiple_of(width + order[0] * wide, wide), wide)] = biases


def copy_all(copies):
    for copy in copies:
        copy.start()
    for copy in copies:
        copy.wait()


def pack_columns(*refs):
    count = (len(refs) - 6) // 2
    weights, vectors = refs[:4], refs[4 : 4 + count]
    out, sems, hold = refs[4 + count : 7 + count]
    buffers = refs[7 + count :]
    high, wide = weights[0].shape
    copies = [
        pltpu.make_async_copy(w, out.at[:high, i * wide : (i + 1) * wide], sems.at[i])
        for i, w in enumerate(weights)
    ]
    small = [pltpu.make_async_copy(v, b, sems.at[4 + i]) for i, (v, b) in enumerate(zip(vectors, buffers))]
    for copy in small + copies:
        copy.start()
    hold[...] = jnp.zeros_like(hold)
    out[high:, :] = jnp.zeros((hold.shape[0], out.shape[1]), BF)
    for copy in small:
        copy.wait()
    for i, buffer in enumerate(buffers):
        size = buffer.shape[0]
        hold[i : i + 1, :size] = buffer[...].astype(F32).reshape(1, size)
    out[high:, : hold.shape[1]] = hold[...].astype(BF)
    for copy in copies:
        copy.wait()


def own_lanes(order, rows, wide, each):
    lane = lax.broadcasted_iota(jnp.int32, (rows, wide), 1)
    return (lane == order[0] * each + lax.broadcasted_iota(jnp.int32, (rows, wide), 0)).astype(BF)


def pack_hidden(order, w_expand, w_reduce, o0, o1, o2, o3, sems):
    step, part = w_expand.shape[0], w_reduce.shape[1]
    half = part // 2
    deep = w_expand.shape[1] // 2
    quarter = w_reduce.shape[0] // SEQ
    copies = []
    for m, out in enumerate((o0, o1, o2, o3)):
        one = rows_at(order[m] * half, half)
        two = pl.ds(pl.multiple_of(deep + order[m] * half, half), half)
        three = rows_at(order[m] * quarter, quarter)
        copies += [
            pltpu.make_async_copy(w_expand.at[:, one], out.at[:step, :half], sems.at[3 * m]),
            pltpu.make_async_copy(w_expand.at[:, two], out.at[:step, half:], sems.at[3 * m + 1]),
            pltpu.make_async_copy(w_reduce.at[three, :], out.at[step:, :], sems.at[3 * m + 2]),
        ]
    copy_all(copies)


def join_hidden(order, p0, p1, p2, p3, out):
    part = p0.shape[1]
    for m, ref in enumerate((p0, p1, p2, p3)):
        out[:, rows_at(order[m] * part, part)] = ref[...]


def part_hidden(order, e0, e1, e2, mine, *outs):
    part = mine.shape[1]
    for m in range(SEQ):
        lanes = rows_at(order[m] * part, part)
        e = e0[:, lanes].astype(F32) + e1[:, lanes].astype(F32) + e2[:, lanes].astype(F32)
        if m == 0:
            mine[...] = e
        else:
            outs[m - 1][...] = e.astype(BF)


def place_hidden(order, p0, p1, p2, p3, e_out, r_out):
    step, part = e_out.shape[0], p0.shape[1]
    half = part // 2
    deep = e_out.shape[1] // 2
    quarter = r_out.shape[0] // SEQ
    for m, ref in enumerate((p0, p1, p2, p3)):
        e_out[:, rows_at(order[m] * half, half)] = ref[:step, :half].astype(F32)
        e_out[:, pl.ds(pl.multiple_of(deep + order[m] * half, half), half)] = ref[:step, half:].astype(F32)
        r_out[rows_at(order[m] * quarter, quarter), :] = ref[step:, :].astype(F32)


def attend(order, a, w, table, key_mask, out, o_out, stat_out):
    width = o_out.shape[1]
    qkv = mm(a[...], w[...])
    mine = rows_at(order[0] * width, width)
    q = (qkv[:, :width] + table[BIAS_Q, mine]).astype(BF)
    key = qkv[:, width : 2 * width].astype(BF)
    value = (qkv[:, 2 * width :] + table[BIAS_V, mine]).astype(BF)
    out[:, :width] = q
    out[:, width : 2 * width] = key
    out[:, 2 * width :] = value
    size = width // (HEADS // SEQ)
    valid = key_mask[...] > 0
    total = None
    for h in range(HEADS // SEQ):
        lanes = head_lanes(width, h, size)
        logits = mm_nt(jnp.where(lanes, q, jnp.zeros_like(q)), key)
        scores = jnp.where(valid, logits * size ** (-0.5), -1000000000.0)
        top = jnp.max(scores, axis=-1, keepdims=True)
        weights = jnp.exp(scores - top)
        inverse = 1.0 / jnp.sum(weights, axis=-1, keepdims=True)
        probs = (weights * inverse).astype(BF)
        mixed = mm(probs, jnp.where(lanes, value, jnp.zeros_like(value)))
        total = mixed if total is None else total + mixed
        stat_out[:, h : h + 1] = top
        stat_out[:, HEADS // SEQ + h : HEADS // SEQ + h + 1] = inverse
    o_out[...] = total.astype(BF)


def middle(order, *refs):
    o = refs[:SEQ]
    w_low = refs[SEQ : 2 * SEQ]
    w_high = refs[2 * SEQ : 3 * SEQ]
    x = refs[3 * SEQ : 4 * SEQ]
    table, c_out, x_out, w_rows, hold, w = refs[4 * SEQ :]
    rows, full = x[0].shape
    width = o[0].shape[1]
    for m in range(SEQ):
        at = rows_at(order[m] * width, width)
        w[: full // 2, at] = w_low[m][...]
        w[full // 2 :, at] = w_high[m][...]
    w_rows[...] = w[rows_at(order[0] * width, width), :]
    for k in range(SEQ):
        hold[k * rows : (k + 1) * rows, :] = x[k][...].astype(F32) + table[BIAS_O, :full]
    for m in range(SEQ):
        part = mm(o[m][...], w[rows_at(order[m] * width, width), :])
        for k in range(SEQ):
            there = (k ^ m) * rows
            hold[there : there + rows, :] += part[k * rows : (k + 1) * rows, :]
    x_out[...] = hold[0:rows, :]
    normal, _ = standardize(hold[...])
    c_out[...] = (normal * table[GAIN_TWO, :full] + table[SHIFT_TWO, :full]).astype(BF)


def feed_forward(idx, order, c, g, table, *refs):
    pieces = refs[: BLOCKS + 1]
    h_out, u_out, bias_out, w_reduce, o0, o1, o2, o3, e_far, r_far, w_expand = refs[BLOCKS + 1 :]
    step = w_expand.shape[0] // BLOCKS
    for k in range(BLOCKS):
        at = rows_at(idx[k] * step, step)
        w_expand[at, :] = pieces[k][:step, :]
        last_piece = pieces[k] if k < BLOCKS - 1 else pieces[k + 1]
        w_reduce[at, :] = last_piece[last_piece.shape[0] - step :, :]
    width = h_out.shape[1]
    group = bias_out.shape[1]
    bias = table[:, pl.ds(pl.multiple_of(w_expand.shape[0] + order[0] * group, group), group)]
    chunk = 2 * group
    for n in range(0, width, chunk):
        r = n // group
        row = jnp.concatenate([bias[r : r + 1], bias[r + 1 : r + 2]], axis=1)
        u = mm(c[...], w_expand[:, n : n + chunk]) + row
        upper = mm_nt(g[...], w_reduce[n : n + chunk, :])
        cdf = 0.5 * (1.0 + lax.erf(u * (0.5**0.5)))
        density = jnp.exp(-0.5 * u * u) * 0.3989422804014327
        h_out[:, n : n + chunk] = (u * cdf).astype(BF)
        low = (upper * (cdf + u * density)).astype(BF)
        u_out[:, n : n + chunk] = low
        total = jnp.sum(low.astype(F32), axis=0, keepdims=True)
        bias_out[r : r + 1, :] = total[:, :group]
        bias_out[r + 1 : r + 2, :] = total[:, group:]
    lower = mm_nt(u_out[...], w_expand[...])
    rows = o0.shape[0]
    for k, out in enumerate((o0, o1, o2, o3)):
        out[...] = lower[k * rows : (k + 1) * rows, :].astype(BF)
    at = rows_at(idx[BLOCKS - 1] * step, step)
    e_far[...] = mm_tn(c[:, at], u_out[...]).astype(BF)
    r_far[...] = mm_tn(h_out[:, at], g[...]).astype(BF)


def reduce_part(h, w, *outs):
    y = mm(h[...], w[...])
    rows = outs[0].shape[0]
    for k in range(SEQ):
        outs[k][...] = y[k * rows : (k + 1) * rows, :].astype(BF)


def feed_grads(idx, c, du, h, g, *outs):
    step = outs[0].shape[0] // 2
    for k in range(BLOCKS - 1):
        at = rows_at(idx[k] * step, step)
        outs[k][:step, :] = mm_tn(c[:, at], du[...]).astype(BF)
        outs[k][step:, :] = mm_tn(h[:, at], g[...]).astype(BF)


def add_two(a, a_own, b, b_own, a_out, b_out):
    here = a.shape[0]
    rest = b_own.shape[0] - b.shape[0]
    a_out[:here, :] = (a[...].astype(F32) + a_own[:here, :].astype(F32)).astype(BF)
    b_out[rest:, :] = (b[...].astype(F32) + b_own[rest:, :].astype(F32)).astype(BF)
    if rest:
        a_out[here:, :] = a_own[here:, :]
        b_out[:rest, :] = b_own[:rest, :]


def norm_pull(upper, normal, scale, gain):
    inner = upper * gain
    return scale * (
        inner
        - jnp.mean(inner, axis=-1, keepdims=True)
        - normal * jnp.mean(inner * normal, axis=-1, keepdims=True)
    )


def middle_back(part0, part1, part2, x, cot, factor, table, grad_out, low_out, sums_out):
    upper = part0[...].astype(F32) + part1[...].astype(F32) + part2[...].astype(F32)
    normal, scale = standardize(x[...])
    upstream = cot[...].astype(F32) * factor[...]
    grad = upstream + norm_pull(upper, normal, scale, table[GAIN_TWO, : x.shape[1]])
    low = grad.astype(BF)
    grad_out[...] = grad
    low_out[...] = low
    sums_out[0:1, :] = jnp.sum(upper * normal, axis=0, keepdims=True)
    sums_out[1:2, :] = jnp.sum(upper, axis=0, keepdims=True)
    sums_out[2:3, :] = jnp.sum(low.astype(F32), axis=0, keepdims=True)
    sums_out[3:4, :] = jnp.sum(upstream, axis=0, keepdims=True)


def attend_back(order, *refs):
    grads = refs[:SEQ]
    w_rows, qkv, stat, key_mask, g_out, out, sums_out, hold = refs[SEQ:]
    rows = grads[0].shape[0]
    for k in range(SEQ):
        hold[k * rows : (k + 1) * rows, :] = grads[k][...].astype(F32)
    g_out[...] = hold[...].astype(BF)
    width = qkv.shape[1] // 3
    size = width // (HEADS // SEQ)
    d_out = mm_nt(g_out[...], w_rows[...]).astype(BF)
    q, key, value = (qkv[:, i * width : (i + 1) * width] for i in range(3))
    valid = key_mask[...] > 0
    dq = dk = dv = None
    for h in range(HEADS // SEQ):
        lanes = head_lanes(width, h, size)
        q_h = jnp.where(lanes, q, jnp.zeros_like(q))
        d_h = jnp.where(lanes, d_out, jnp.zeros_like(d_out))
        logits = mm_nt(q_h, key)
        scores = jnp.where(valid, logits * size ** (-0.5), -1000000000.0)
        top = stat[:, h : h + 1]
        inverse = stat[:, HEADS // SEQ + h : HEADS // SEQ + h + 1]
        probs = jnp.exp(scores - top) * inverse
        prob_grad = mm_nt(d_h, value)
        center = jnp.sum(probs * prob_grad, axis=-1, keepdims=True)
        low = jnp.where(valid, probs * (prob_grad - center) * size ** (-0.5), 0.0).astype(BF)
        dv_h = mm_tn(probs.astype(BF), d_h)
        dk_h = mm_tn(low, q_h)
        dq_h = mm(low, jnp.where(lanes, key, jnp.zeros_like(key)))
        dq = dq_h if dq is None else dq + dq_h
        dk = dk_h if dk is None else dk + dk_h
        dv = dv_h if dv is None else dv + dv_h
    dq, dk, dv = dq.astype(BF), dk.astype(BF), dv.astype(BF)
    out[:, :width] = dq
    out[:, width : 2 * width] = dk
    out[:, 2 * width :] = dv
    sums_out[0:1, :] = jnp.sum(dq.astype(F32), axis=0, keepdims=True)
    sums_out[1:2, :] = jnp.sum(dv.astype(F32), axis=0, keepdims=True)


def attention_grads(idx, order, a, d, g, sums, *refs):
    o = refs[:SEQ]
    outs = refs[SEQ : SEQ + BLOCKS + 1]
    hold, turned = refs[SEQ + BLOCKS + 1 :]
    rows = g.shape[0] // SEQ
    width = o[0].shape[1]
    full = hold.shape[0]
    step = full // BLOCKS
    mine = g[:, rows_at(order[0] * width, width)].astype(F32)
    for m in range(SEQ):
        for k in range(SEQ):
            there = (k ^ m) * rows
            turned[k * rows : (k + 1) * rows, :] = mine[there : there + rows, :]
        hold[rows_at(order[m] * width, width), :] = mm_tn(o[m][...], turned[...].astype(BF)).astype(BF)
    count, wide = sums.shape[0], step
    biases = sums[:, pl.ds(pl.multiple_of(full + order[0] * wide, wide), wide)]
    row = lax.broadcasted_iota(jnp.int32, biases.shape, 0)
    for k in range(BLOCKS):
        at = rows_at(idx[k] * step, step)
        value = mm_tn(a[:, at], d[...]).astype(BF)
        size = step if k < BLOCKS - 1 else step // 2
        outs[k][:size, : 3 * width] = value[:size]
        outs[k][:size, 3 * width :] = hold[rows_at(idx[k] * step, size), :]
        below = outs[k]
        if k == BLOCKS - 1:
            below = outs[k + 1]
            below[:size, : 3 * width] = value[size:]
            below[:size, 3 * width :] = hold[rows_at(idx[k] * step + size, size), :]
        if below.shape[0] > size:
            extra = below.shape[0] - size
            bias = jnp.sum(jnp.where(row == idx[k], biases, 0.0), axis=0, keepdims=True)
            bias = jnp.broadcast_to(bias, (extra - count, wide))
            block = jnp.concatenate([sums[:, rows_at(idx[k] * wide, wide)], bias], axis=0)
            below[size:, :wide] = block.astype(BF)
            below[size:, wide:] = jnp.zeros((extra, below.shape[1] - wide), BF)


def normed_back(order, d, w, normal, sums_qv, sums_mid, sum_e, sums, *outs):
    rows, width = outs[0].shape
    part, wide = sums_qv.shape[1], sum_e.shape[1]
    upper = mm_nt(d[...], w[...])
    for k in range(SEQ):
        outs[k][...] = upper[k * rows : (k + 1) * rows, :].astype(BF)
    sums[...] = jnp.zeros_like(sums)
    sums[GAIN_ONE, :width] = jnp.sum(upper * normal[...].astype(F32), axis=0, keepdims=True)
    sums[SHIFT_ONE, :width] = jnp.sum(upper, axis=0, keepdims=True)
    mine = rows_at(order[0] * part, part)
    sums[BIAS_Q, mine] = sums_qv[0:1, :]
    sums[BIAS_V, mine] = sums_qv[1:2, :]
    sums[BIAS_O, :width] = sums_mid[2:3, :]
    sums[GAIN_TWO, :width] = sums_mid[0:1, :]
    sums[SHIFT_TWO, :width] = sums_mid[1:2, :]
    sums[BIAS_R, :width] = sums_mid[3:4, :]
    sums[:, pl.ds(pl.multiple_of(width + order[0] * wide, wide), wide)] = sum_e[...]


def last(part0, part1, part2, x, grad, y0, y1, y2, x_mid, table, grad_out, y_out):
    width = x.shape[1]
    upper = part0[...].astype(F32) + part1[...].astype(F32) + part2[...].astype(F32)
    normal, scale = standardize(x[...].astype(F32))
    grad_out[...] = (grad[...] + norm_pull(upper, normal, scale, table[GAIN_ONE, :width])).astype(BF)
    y = x_mid[...] + table[BIAS_R, :width] + y0[...].astype(F32)
    y_out[...] = (y + y1[...].astype(F32) + y2[...].astype(F32)).astype(BF)


def finish(p0, p1, p2, w0, w1, w2, w3, sums, bias):
    high, part = w0.shape
    count, wide = sums.shape
    for i, out in enumerate((w0, w1, w2, w3)):
        at = slice(i * part, (i + 1) * part)
        out[...] = p0[:high, at].astype(F32) + p1[:high, at].astype(F32) + p2[:high, at].astype(F32)
    below = p0[high:, :wide].astype(F32) + p1[high:, :wide].astype(F32) + p2[high:, :wide].astype(F32)
    sums[...] = below[:count]
    bias[...] = below[count : count + 1]


def seq_swap(value, flip):
    return lax.ppermute(value, "seq", [(s, s ^ flip) for s in range(SEQ)])


def after(value, *others):
    return lax.optimization_barrier((value,) + others)[0]


def add(a, b):
    return (a.astype(F32) + b.astype(F32)).astype(BF)


def ring_order(data_count):
    return list(range(0, data_count, 2)) + list(range(data_count - 1, 0, -2))


def ring_hop(value, data_count, step):
    ring = ring_order(data_count)
    pairs = [(ring[r], ring[(r + step) % data_count]) for r in range(data_count)]
    return lax.ppermute(value, "dp", pairs)


RELATIVE = (0, -1, -2, -3, 1, 2, 3, 4)


def relative_order(data_count):
    if data_count != RING:
        return jnp.arange(BLOCKS, dtype=jnp.int32)
    me = lax.axis_index("dp")
    z, y = me // 2, me % 2
    place = jnp.where(y == 0, z, BLOCKS - 1 - z)
    there = (place + jnp.array(RELATIVE, dtype=jnp.int32) + BLOCKS) % BLOCKS
    half = BLOCKS // 2
    return jnp.where(there < half, 2 * there, 2 * (BLOCKS - 1 - there) + 1).astype(jnp.int32)


@jax.tree_util.register_pytree_node_class
class Gather:
    def __init__(self, value, data_count, parts, cut, back=(), front=()):
        self.value, self.data_count, self.parts, self.cut = value, data_count, parts, cut
        self.back, self.front = list(back), list(front)

    def tree_flatten(self):
        return (self.value, self.back, self.front), (self.data_count, self.parts, self.cut)

    @classmethod
    def tree_unflatten(cls, aux, parts):
        return cls(parts[0], *aux, *parts[1:])

    def hop(self):
        if self.data_count != RING:
            if not self.back:
                whole = lax.all_gather(self.value, "dp", axis=0, tiled=False)
                parts = [p.reshape((BLOCKS, -1) + p.shape[2:]) for p in jnp.split(whole, self.parts, axis=1)]
                self.back = list(jnp.concatenate(parts, axis=1))
            return
        back, front = (self.back or [self.value])[-1], (self.front or [self.value])[-1]
        if len(self.back) == BLOCKS // 2 - 1:
            back, front = back[: self.cut], front[self.cut :]
        self.back.append(ring_hop(back, self.data_count, 1))
        self.front.append(ring_hop(front, self.data_count, -1))

    def blocks(self, last=(0, 1)):
        if self.data_count != RING:
            halves = (self.back[-1][: self.cut], self.back[-1][self.cut :])
            return self.back[:-1] + [halves[i] for i in last]
        halves = (self.back[3], self.front[3])
        return [self.value] + self.back[:3] + self.front[:3] + [halves[i] for i in last]


@jax.tree_util.register_pytree_node_class
class Scatter:
    def __init__(self, pieces, data_count, parts, hops=0, left=None, right=None):
        self.pieces, self.data_count, self.parts = pieces, data_count, parts
        self.hops, self.left, self.right = hops, left, right

    def tree_flatten(self):
        return (self.pieces, self.left, self.right), (self.data_count, self.parts, self.hops)

    @classmethod
    def tree_unflatten(cls, aux, parts):
        return cls(parts[0], *aux, *parts[1:])

    def hop(self):
        n, self.hops = self.hops, self.hops + 1
        if self.data_count != RING:
            if n == 0:
                whole = jnp.concatenate(self.pieces, axis=0)
                wide = whole.shape[1]
                whole = whole.reshape(BLOCKS, self.parts, self.data_count // BLOCKS, -1, wide)
                whole = whole.transpose(0, 2, 1, 3, 4).reshape(-1, wide)
                self.left = lax.psum_scatter(whole, "dp", scatter_dimension=0, tiled=True)
            return self.left
        own = dict(zip(RELATIVE, self.pieces))
        left, right = self.left, self.right
        if n == 0:
            left, right = self.pieces[-2:]
        else:
            ahead, behind = own[4 - n], own[n - 4]
            outs = (shape(ahead.shape, BF),) * 2
            left, right = kernel_call(add_two, outs, left, ahead, right, behind)
        self.left = ring_hop(left, self.data_count, 1)
        self.right = ring_hop(right, self.data_count, -1)
        return left

    def terms(self):
        if self.data_count != RING:
            return [self.left, jnp.zeros_like(self.left), jnp.zeros_like(self.left)]
        return [self.pieces[0], self.left, self.right]


def sum_slot(value):
    value = value + seq_swap(value, 1)
    return value + seq_swap(value, 2)


def trade(parts, data_count):
    return [parts[0]] + [seq_swap(parts[m], m) for m in range(1, SEQ)]


def pack_hidden_weights(order, w_expand, w_reduce, data_count):
    high, low, part = w_expand.shape[0], w_reduce.shape[0] // SEQ, w_reduce.shape[1]
    if data_count == RING:
        piece = shape((high + low, part), BF)
        sems = [pltpu.SemaphoreType.DMA((3 * SEQ,))]
        return list(
            kernel_call(pack_hidden, (piece,) * SEQ, order, w_expand, w_reduce, far=(1, 2), scratch=sems)
        )
    e = w_expand.reshape(high, -1, SEQ, low).transpose(2, 0, 1, 3).reshape(SEQ, high, part)
    both = jnp.concatenate([e, w_reduce.reshape(SEQ, low, part)], axis=1)
    return [lax.dynamic_index_in_dim(both, order[m], 0, False) for m in range(SEQ)]


def join_hidden_weights(order, parts, data_count):
    rows, part = parts[0].shape
    if data_count == RING:
        return kernel_call(join_hidden, (shape((rows, SEQ * part), BF),), order, *parts)[0]
    both = jnp.zeros((rows, SEQ * part), BF)
    for m in range(SEQ):
        both = lax.dynamic_update_slice(both, parts[m], (0, order[m] * part))
    return both


def part_hidden_grads(order, terms, part, data_count):
    if data_count == RING:
        piece = (terms[0].shape[0], part)
        outs = (shape(piece, F32),) + (shape(piece, BF),) * (SEQ - 1)
        return list(kernel_call(part_hidden, outs, order, *terms))
    return [lax.dynamic_slice_in_dim(terms[0], order[m] * part, part, 1) for m in range(SEQ)]


def place_hidden_grads(order, parts, e_shape, r_shape, data_count):
    if data_count == RING:
        outs = (shape(e_shape, F32), shape(r_shape, F32))
        return kernel_call(place_hidden, outs, order, *parts)
    high, low = e_shape[0], r_shape[0] // SEQ
    both = jnp.zeros((SEQ,) + parts[0].shape, F32)
    for m in range(SEQ):
        both = lax.dynamic_update_slice(both, parts[m].astype(F32)[None], (order[m], 0, 0))
    e = both[:, :high].reshape(SEQ, high, -1, low).transpose(1, 2, 0, 3).reshape(e_shape)
    return e, both[:, high:].reshape(r_shape)


def eight(deep, wide):
    return (shape((deep, wide), BF),) * (BLOCKS - 1) + (shape((deep // 2, wide), BF),) * 2


def sync(state):
    return lax.optimization_barrier(state)


def local(
    block_input,
    cotangent,
    image_valid,
    token_valid,
    first_gain,
    first_shift,
    query_weight,
    query_bias,
    key_weight,
    value_weight,
    value_bias,
    output_weight,
    output_bias,
    second_gain,
    second_shift,
    expand_weight,
    expand_bias,
    reduce_weight,
    reduce_bias,
):
    data_count = lax.axis_size("dp")
    ring = data_count == RING
    me = lax.axis_index("seq")
    rows, width = block_input.shape[1:]
    tokens = rows * SEQ
    part = width // SEQ
    deep = expand_weight.shape[1]
    step = width // BLOCKS
    full = shape((tokens, width), BF)
    block = shape((rows, width), BF)
    s = {}
    s["idx"] = relative_order(data_count)
    dp = lax.axis_index("dp")
    s["order"] = jnp.stack([me ^ k for k in range(SEQ)] + [dp]).astype(jnp.int32)

    vectors = (
        first_gain,
        first_shift,
        query_bias,
        value_bias,
        output_bias,
        second_gain,
        second_shift,
        reduce_bias,
    )
    each = first_gain.shape[0]
    place = dp * SEQ + me
    count = len(vectors)
    group = deep // BLOCKS
    bias_row = expand_bias.astype(F32)[None]
    bias_length = expand_bias.shape[0]
    bias_at = dp * bias_length
    bias_at = (bias_at // group, me * group + bias_at % group)
    table = shape((count, width + SEQ * group), F32)

    valid = token_valid.astype(F32).reshape(SEQ, rows)
    valid = jnp.concatenate([lax.dynamic_slice_in_dim(valid, s["order"][k], 1, 0) for k in range(SEQ)], axis=1)
    s["valid"] = valid
    s["factor"] = (valid * image_valid.astype(F32)[0]).reshape(tokens, 1)

    attention_weights = (query_weight, key_weight, value_weight, output_weight)
    extra = 2 * count if ring else 0
    if ring:
        args = attention_weights + vectors + (expand_bias,)
        scratch = [pltpu.SemaphoreType.DMA((len(args),)), pltpu.VMEM((extra, group), F32)]
        scratch += [pltpu.VMEM(v.shape, BF) for v in args[4:]]
        outs = (shape((step + extra, width), BF),)
        (piece,) = kernel_call(pack_columns, outs, *args, far=range(len(args)), scratch=scratch)
    else:
        piece = jnp.concatenate(attention_weights, axis=1)
    s["attention"] = Gather(piece, data_count, 1, step // 2)
    s["attention"].hop()
    s["x"] = [block_input[0]]
    s["x"] += [seq_swap(s["x"][0], m) for m in (1, 2)]
    s["cot"] = [cotangent[0]]
    s["hidden"] = pack_hidden_weights(s["order"], expand_weight, reduce_weight, data_count)
    s = sync(s)

    s["attention"].hop()
    hidden = s.pop("hidden")
    s["hidden"] = [hidden[0]] + [seq_swap(hidden[m], m) for m in (1, 2)]
    s["hidden_last"] = hidden[3]
    s = sync(s)

    s["attention"].hop()
    s["hidden"].append(seq_swap(s.pop("hidden_last"), 3))
    s["x"].append(seq_swap(s["x"][2], 1))
    s["cot"].append(seq_swap(s["cot"][0], 2))
    s = sync(s)

    s["attention"].hop()
    s["cot"] = [s["cot"][0], seq_swap(s["cot"][0], 1), s["cot"][1], seq_swap(s["cot"][1], 1)]
    feed = join_hidden_weights(s["order"], s.pop("hidden"), data_count)
    s["feed"] = Gather(feed, data_count, 2, step)
    s = sync(s)

    s["feed"].hop()
    half = shape((width // 2, part), BF)
    s["w_qkv"], w_low, w_high, s["table"] = kernel_call(
        stack_rows,
        (shape((width, 3 * part), BF), half, half, table),
        s["idx"],
        s["order"],
        *s.pop("attention").blocks(),
    )
    s["w_low"], s["w_high"] = [w_low], [w_high]
    s["w_low"].append(seq_swap(after(w_low, s["w_qkv"]), 2))
    if ring:
        s["table"] = sum_slot(s["table"])
    else:
        every = lax.broadcasted_iota(jnp.int32, (each, width), 1)
        every = every == place * each + lax.broadcasted_iota(jnp.int32, (each, width), 0)
        stacked = sum(
            jnp.pad(v[None], ((i, count - 1 - i), (0, 0))) for i, v in enumerate(vectors)
        )
        placed = jnp.dot(stacked, every.astype(BF), preferred_element_type=F32)
        placed_bias = lax.dynamic_update_slice(
            jnp.zeros((count, table.shape[1] - width), F32), bias_row, bias_at
        )
        s["table"] = lax.psum(jnp.concatenate([placed, placed_bias], axis=1), ("dp", "seq"))
    s = sync(s)

    s["feed"].hop()
    s["w_high"] += [seq_swap(s["w_high"][0], m) for m in (1, 2)]
    s["a"], s["normal"] = kernel_call(
        norm_one, (full, full), *s["x"], s["table"], scratch=[pltpu.VMEM((tokens, width), F32)]
    )
    s["qkv"], o, s["stat"] = kernel_call(
        attend,
        (shape((tokens, 3 * part), BF), shape((tokens, part), BF), shape((tokens, 128), F32)),
        s["order"],
        s["a"],
        s["w_qkv"],
        s["table"],
        s["valid"],
        flops=2 * tokens * part * (3 * width + 8 * tokens),
    )
    s["o"] = [o]
    s = sync(s)

    s["feed"].hop()
    s["o"].append(seq_swap(s["o"][0], 2))
    (s["g"],) = kernel_call(
        mask_rows, (full,), *s["cot"], s["factor"], scratch=[pltpu.VMEM((tokens, width), F32)]
    )
    s["cot"] = s["cot"][0]
    s["w_low"].append(seq_swap(s["w_low"][1], 1))
    s = sync(s)

    s["feed"].hop()
    o_mine, o_two = s["o"]
    s["o"] = [o_mine, seq_swap(o_mine, 1), o_two, seq_swap(o_two, 1)]
    s["w_high"].append(seq_swap(s["w_high"][2], 1))
    s["w_low"].insert(1, seq_swap(s["w_low"][0], 1))
    s["c"], s["x_mid"], s["w_rows"] = kernel_call(
        middle,
        (full, shape((rows, width), F32), shape((part, width), BF)),
        s["order"],
        *s["o"],
        *s.pop("w_low"),
        *s.pop("w_high"),
        *s["x"],
        s["table"],
        scratch=[pltpu.VMEM((tokens, width), F32), pltpu.VMEM((width, width), BF)],
        flops=2 * tokens * width * width,
    )
    s["x"] = s["x"][0]
    s = sync(s)

    h, du, s["sum_e"], w_r, *c_part, e_far, r_far = kernel_call(
        feed_forward,
        (
            shape((tokens, deep), BF),
            shape((tokens, deep), BF),
            shape((BLOCKS, group), F32),
            shape((deep, width), BF),
            block,
            block,
            block,
            block,
            shape((step, deep), BF),
            shape((step, width), BF),
        ),
        s["idx"],
        s["order"],
        s["c"],
        s["g"],
        s["table"],
        *s.pop("feed").blocks(),
        scratch=[pltpu.VMEM((width, deep), BF)],
        flops=7 * tokens * width * deep,
    )
    s["c_part"] = c_part
    s["c_got"] = [seq_swap(c_part[m], 1) for m in (1, 3)]
    far = [e_far, r_far]
    args = (s["idx"], s.pop("c"), du, h, s.pop("g"))
    s["c_two"] = seq_swap(add(after(s["c_part"][2], s["c_got"][0]), s["c_got"][1]), 2)
    pieces = kernel_call(
        feed_grads,
        (shape((2 * step, deep), BF),) * (BLOCKS - 1),
        after(args[0], far[0]),
        *args[1:],
        flops=3 * tokens * width * deep,
    )
    s["feed_grad"] = Scatter(list(pieces) + list(far), data_count, 2)
    s["feed_grad"].hop()
    s["y_part"] = kernel_call(
        reduce_part,
        (block, block, block, block),
        after(h, pieces[0]),
        w_r,
        flops=2 * tokens * width * deep,
    )
    s = sync(s)

    s["mid_grad"], branch, s["sums_mid"] = kernel_call(
        middle_back,
        (shape((rows, width), F32), block, shape((4, width), F32)),
        s.pop("c_part")[0],
        s.pop("c_got")[0],
        s.pop("c_two"),
        s["x_mid"],
        s["cot"],
        s["factor"][:rows],
        s["table"],
    )
    branch_two = seq_swap(branch, 2)
    s["feed_grad"].hop()
    s["y_got"] = [seq_swap(s["y_part"][1], 1)]
    s["branch"] = [branch, branch_two]
    s = sync(s)

    branch, branch_two = s.pop("branch")
    s["branch"] = [branch, seq_swap(branch, 1), branch_two, seq_swap(branch_two, 1)]
    s["feed_grad"].hop()
    s["y_got"].append(seq_swap(s["y_part"][3], 1))
    s["branch_full"], s["dqkv"], s["sums_qv"] = kernel_call(
        attend_back,
        (full, shape((tokens, 3 * part), BF), shape((2, part), F32)),
        s["order"],
        *s.pop("branch"),
        s.pop("w_rows"),
        s.pop("qkv"),
        s.pop("stat"),
        s["valid"],
        scratch=[pltpu.VMEM((tokens, width), F32)],
        flops=2 * tokens * part * (width + 20 * tokens),
    )
    s = sync(s)

    sent = s["feed_grad"].hop()
    s["sums"], *s["a_part"] = kernel_call(
        normed_back,
        (table, block, block, block, block),
        s["order"],
        after(s["dqkv"], sent),
        s.pop("w_qkv"),
        s.pop("normal"),
        s.pop("sums_qv"),
        s.pop("sums_mid"),
        s.pop("sum_e"),
        flops=6 * tokens * width * part,
    )
    if not ring:
        s["sums"] = lax.psum(s["sums"], ("dp", "seq"))
    s["a_got"] = [seq_swap(s["a_part"][m], 1) for m in (1, 3)]
    half = step // 2
    pieces = kernel_call(
        attention_grads,
        (shape((step + extra, width), BF),) * (BLOCKS - 1)
        + (shape((half, width), BF), shape((half + extra, width), BF)),
        s["idx"],
        s["order"],
        after(s.pop("a"), *s["a_got"]),
        s.pop("dqkv"),
        s.pop("branch_full"),
        s["sums"],
        *s.pop("o"),
        scratch=[pltpu.VMEM((width, part), BF), pltpu.VMEM((tokens, part), F32)],
        flops=8 * tokens * width * part,
    )
    s["attention_grad"] = Scatter(list(pieces), data_count, 1)
    s["attention_grad"].hop()
    s = sync(s)

    sent = s["attention_grad"].hop()
    s["hidden"] = part_hidden_grads(s["order"], s.pop("feed_grad").terms(), part, data_count)
    s["hidden_got"] = [seq_swap(s["hidden"][1], 1)]
    s["a_two"] = seq_swap(add(after(s["a_part"][2], sent), s["a_got"][1]), 2)
    s["y_two"] = add(after(s["y_part"][2], sent), s["y_got"][1])
    s = sync(s)

    s["attention_grad"].hop()
    s["y_two"] = seq_swap(s["y_two"], 2)
    s = sync(s)

    s["attention_grad"].hop()
    s["hidden_got"] += [seq_swap(s["hidden"][m], m) for m in (2, 3)]
    s["input_gradient"], s["y"] = kernel_call(
        last,
        (block, block),
        s["a_part"][0],
        s["a_got"][0],
        s["a_two"],
        s["x"],
        s["mid_grad"],
        s["y_part"][0],
        s["y_got"][0],
        s["y_two"],
        s["x_mid"],
        s["table"],
    )
    s = sync(s)

    terms = s["attention_grad"].terms()
    high = attention_weights[0].shape[0]
    if ring:
        matrix = shape((high, part), F32)
        outs = (matrix,) * 4 + (shape((count, group), F32), shape((1, group), F32))
        *matrices, sums, bias_sum = kernel_call(finish, outs, *terms)
        grads = lax.dynamic_slice(sum_slot(sums), (0, me * each), (count, each))
        expand_bias_grad = bias_sum[0, :bias_length]
    else:
        grads = lax.dynamic_slice_in_dim(s["sums"], place * each, each, 1)
        expand_bias_grad = lax.dynamic_slice(s["sums"][:, width:], bias_at, (1, bias_length))[0]
        total = sum(t.astype(F32) for t in terms)
        matrices = [total[:, i * part : (i + 1) * part] for i in range(4)]
    expand_weight_grad, reduce_weight_grad = place_hidden_grads(
        s["order"], s["hidden"][:1] + s["hidden_got"], expand_weight.shape, reduce_weight.shape, data_count
    )
    return (
        s["y"][None],
        s["input_gradient"][None],
        grads[0],
        grads[1],
        matrices[0],
        grads[2],
        matrices[1],
        matrices[2],
        grads[3],
        matrices[3],
        grads[4],
        grads[5],
        grads[6],
        expand_weight_grad,
        expand_bias_grad,
        reduce_weight_grad,
        grads[7],
    )


def solution(mesh):
    vector = P(("dp", "seq"))
    matrix = P("dp", "seq")
    tokens = P("dp", "seq", None)
    return jax.shard_map(
        local,
        mesh=mesh,
        in_specs=(
            tokens,
            tokens,
            P("dp"),
            P(),
            vector,
            vector,
            matrix,
            vector,
            matrix,
            matrix,
            vector,
            matrix,
            vector,
            vector,
            vector,
            matrix,
            vector,
            matrix,
            vector,
        ),
        out_specs=(
            tokens,
            tokens,
            vector,
            vector,
            matrix,
            vector,
            matrix,
            matrix,
            vector,
            matrix,
            vector,
            vector,
            vector,
            matrix,
            vector,
            matrix,
            vector,
        ),
        check_vma=False,
    )
```

```python
import jax
import jax.numpy as jnp
from jax import lax
from jax.experimental import pallas as pl
from jax.experimental.pallas import tpu as pltpu
from jax.sharding import PartitionSpec as P

HEADS = 16
EPS = 1e-06
BF = jnp.bfloat16
F32 = jnp.float32
SEQ = 4
BLOCKS = 8
RING = 8
MIB = 1 << 20
VMEM = {
    "pack_columns": 60,
    "pack_hidden": 56,
    "join_hidden": 2,
    "stack_rows": 5,
    "norm_one": 8,
    "attend": 10,
    "middle": 14,
    "feed_forward": 12,
    "reduce_part": 8,
    "mask_rows": 4,
    "feed_grads": 6,
    "add_two": 2,
    "middle_back": 6,
    "attend_back": 12,
    "normed_back": 6,
    "attention_grads": 5,
    "part_hidden": 2,
    "place_hidden": 3,
    "last": 6,
    "finish": 3,
}
GAIN_ONE, SHIFT_ONE, BIAS_Q, BIAS_V, BIAS_O, GAIN_TWO, SHIFT_TWO, BIAS_R = (
    slice(i, i + 1) for i in range(8)
)


def mm(a, b):
    return lax.dot_general(a, b, (((1,), (0,)), ((), ())), preferred_element_type=F32)


def mm_nt(a, b):
    return lax.dot_general(a, b, (((1,), (1,)), ((), ())), preferred_element_type=F32)


def mm_tn(a, b):
    return lax.dot_general(a, b, (((0,), (0,)), ((), ())), preferred_element_type=F32)


def standardize(values):
    center = values - jnp.mean(values, axis=-1, keepdims=True)
    scale = lax.rsqrt(jnp.mean(center * center, axis=-1, keepdims=True) + EPS)
    return center * scale, scale


def rows_at(start, size):
    return pl.ds(pl.multiple_of(start, size), size)


def kernel_call(body, outs, *args, scratch=(), flops=0, far=()):
    specs = [
        pl.BlockSpec(memory_space=pltpu.SMEM if a.dtype == jnp.int32 else pltpu.VMEM) for a in args
    ]
    for i in far:
        specs[i] = pl.BlockSpec(memory_space=pl.ANY)
    moved = sum(a.size * a.dtype.itemsize for a in args)
    moved += sum(o.size * o.dtype.itemsize for o in outs)
    return pl.pallas_call(
        body,
        out_shape=tuple(outs),
        in_specs=specs,
        out_specs=tuple(pl.BlockSpec(memory_space=pltpu.VMEM) for _ in outs),
        scratch_shapes=list(scratch),
        compiler_params=pltpu.CompilerParams(vmem_limit_bytes=VMEM[body.__name__] * MIB),
        cost_estimate=pl.CostEstimate(flops=0, bytes_accessed=int(moved), transcendentals=0),
    )(*args)


def shape(dims, dtype):
    return jax.ShapeDtypeStruct(tuple(dims), dtype)


def norm_one(x0, x1, x2, x3, table, a_out, n_out, hold):
    rows, width = x0.shape
    for k, ref in enumerate((x0, x1, x2, x3)):
        normal, _ = standardize(ref[...].astype(F32))
        hold[k * rows : (k + 1) * rows, :] = normal
    normal = hold[...]
    n_out[...] = normal.astype(BF)
    a_out[...] = (normal * table[GAIN_ONE, :width] + table[SHIFT_ONE, :width]).astype(BF)


def mask_rows(c0, c1, c2, c3, factor, g_out, hold):
    rows = c0.shape[0]
    for k, ref in enumerate((c0, c1, c2, c3)):
        hold[k * rows : (k + 1) * rows, :] = ref[...].astype(F32)
    g_out[...] = (hold[...] * factor[...]).astype(BF)


def head_lanes(width, head, size):
    lane = lax.broadcasted_iota(jnp.int32, (1, width), 1)
    return (lane >= head * size) & (lane < (head + 1) * size)


def stack_rows(idx, order, *refs):
    w_qkv, w_low, w_high, table = refs[BLOCKS + 1 :]
    width, first = w_qkv.shape
    step = width // BLOCKS
    count = table.shape[0]
    wide = (table.shape[1] - width) // SEQ
    each = wide // SEQ
    table[...] = jnp.zeros_like(table)
    row = lax.broadcasted_iota(jnp.int32, (count, wide), 0)
    biases = jnp.zeros((count, wide), F32)
    for k in range(BLOCKS + 1):
        spot = idx[min(k, BLOCKS - 1)]
        at, size = spot * step, step
        if k >= BLOCKS - 1:
            size = step // 2
            at += size * (k - BLOCKS + 1)
        w_qkv[rows_at(at, size), :] = refs[k][:size, :first]

        @pl.when(at < width // 2)
        def _():
            w_low[rows_at(at, size), :] = refs[k][:size, first:]

        @pl.when(at >= width // 2)
        def _():
            w_high[rows_at(at - width // 2, size), :] = refs[k][:size, first:]

        if refs[k].shape[0] > size:
            below = refs[k][size:, : 2 * wide]
            placed = mm(below[:, :each], own_lanes(order, each, wide, each))
            table[:, rows_at(spot * wide, wide)] = placed[:count]
            biases = jnp.where(row == spot, below.astype(F32)[:1, wide:], biases)
    table[:, pl.ds(pl.multiple_of(width + order[0] * wide, wide), wide)] = biases


def copy_all(copies):
    for copy in copies:
        copy.start()
    for copy in copies:
        copy.wait()


def pack_columns(*refs):
    count = (len(refs) - 6) // 2
    weights, vectors = refs[:4], refs[4 : 4 + count]
    out, sems, hold = refs[4 + count : 7 + count]
    buffers = refs[7 + count :]
    high, wide = weights[0].shape
    copies = [
        pltpu.make_async_copy(w, out.at[:high, i * wide : (i + 1) * wide], sems.at[i])
        for i, w in enumerate(weights)
    ]
    small = [pltpu.make_async_copy(v, b, sems.at[4 + i]) for i, (v, b) in enumerate(zip(vectors, buffers))]
    for copy in small + copies:
        copy.start()
    hold[...] = jnp.zeros_like(hold)
    out[high:, :] = jnp.zeros((hold.shape[0], out.shape[1]), BF)
    for copy in small:
        copy.wait()
    for i, buffer in enumerate(buffers):
        size = buffer.shape[0]
        row, first = (i, 0) if i < count - 1 else (0, hold.shape[1] - size)
        hold[row : row + 1, first : first + size] = buffer[...].astype(F32).reshape(1, size)
    out[high:, : hold.shape[1]] = hold[...].astype(BF)
    for copy in copies:
        copy.wait()


def own_lanes(order, rows, wide, each):
    lane = lax.broadcasted_iota(jnp.int32, (rows, wide), 1)
    return (lane == order[0] * each + lax.broadcasted_iota(jnp.int32, (rows, wide), 0)).astype(BF)


def pack_hidden(order, w_expand, w_reduce, o0, o1, o2, o3, sems):
    step, part = w_expand.shape[0], w_reduce.shape[1]
    half = part // 2
    deep = w_expand.shape[1] // 2
    quarter = w_reduce.shape[0] // SEQ
    copies = []
    for m, out in enumerate((o0, o1, o2, o3)):
        one = rows_at(order[m] * half, half)
        two = pl.ds(pl.multiple_of(deep + order[m] * half, half), half)
        three = rows_at(order[m] * quarter, quarter)
        copies += [
            pltpu.make_async_copy(w_expand.at[:, one], out.at[:step, :half], sems.at[3 * m]),
            pltpu.make_async_copy(w_expand.at[:, two], out.at[:step, half:], sems.at[3 * m + 1]),
            pltpu.make_async_copy(w_reduce.at[three, :], out.at[step:, :], sems.at[3 * m + 2]),
        ]
    copy_all(copies)


def join_hidden(order, p0, p1, p2, p3, out):
    part = p0.shape[1]
    for m, ref in enumerate((p0, p1, p2, p3)):
        out[:, rows_at(order[m] * part, part)] = ref[...]


def part_hidden(order, e0, e1, e2, mine, *outs):
    part = mine.shape[1]
    for m in range(SEQ):
        lanes = rows_at(order[m] * part, part)
        e = e0[:, lanes].astype(F32) + e1[:, lanes].astype(F32) + e2[:, lanes].astype(F32)
        if m == 0:
            mine[...] = e
        else:
            outs[m - 1][...] = e.astype(BF)


def place_hidden(order, p0, p1, p2, p3, e_out, r_out):
    step, part = e_out.shape[0], p0.shape[1]
    half = part // 2
    deep = e_out.shape[1] // 2
    quarter = r_out.shape[0] // SEQ
    for m, ref in enumerate((p0, p1, p2, p3)):
        e_out[:, rows_at(order[m] * half, half)] = ref[:step, :half].astype(F32)
        e_out[:, pl.ds(pl.multiple_of(deep + order[m] * half, half), half)] = ref[:step, half:].astype(F32)
        r_out[rows_at(order[m] * quarter, quarter), :] = ref[step:, :].astype(F32)


def attend(order, a, w, table, key_mask, out, o_out, stat_out):
    width = o_out.shape[1]
    qkv = mm(a[...], w[...])
    mine = rows_at(order[0] * width, width)
    q = (qkv[:, :width] + table[BIAS_Q, mine]).astype(BF)
    key = qkv[:, width : 2 * width].astype(BF)
    value = (qkv[:, 2 * width :] + table[BIAS_V, mine]).astype(BF)
    out[:, :width] = q
    out[:, width : 2 * width] = key
    out[:, 2 * width :] = value
    size = width // (HEADS // SEQ)
    valid = key_mask[...] > 0
    total = None
    for h in range(HEADS // SEQ):
        lanes = head_lanes(width, h, size)
        logits = mm_nt(jnp.where(lanes, q, jnp.zeros_like(q)), key)
        scores = jnp.where(valid, logits * size ** (-0.5), -1000000000.0)
        top = jnp.max(scores, axis=-1, keepdims=True)
        weights = jnp.exp(scores - top)
        inverse = 1.0 / jnp.sum(weights, axis=-1, keepdims=True)
        probs = (weights * inverse).astype(BF)
        mixed = mm(probs, jnp.where(lanes, value, jnp.zeros_like(value)))
        total = mixed if total is None else total + mixed
        stat_out[:, h : h + 1] = top
        stat_out[:, HEADS // SEQ + h : HEADS // SEQ + h + 1] = inverse
    o_out[...] = total.astype(BF)


def middle(order, *refs):
    o = refs[:SEQ]
    w_low = refs[SEQ : 2 * SEQ]
    w_high = refs[2 * SEQ : 3 * SEQ]
    x = refs[3 * SEQ : 4 * SEQ]
    table, c_out, x_out, w_rows, hold, w = refs[4 * SEQ :]
    rows, full = x[0].shape
    width = o[0].shape[1]
    for m in range(SEQ):
        at = rows_at(order[m] * width, width)
        w[: full // 2, at] = w_low[m][...]
        w[full // 2 :, at] = w_high[m][...]
    w_rows[...] = w[rows_at(order[0] * width, width), :]
    for k in range(SEQ):
        hold[k * rows : (k + 1) * rows, :] = x[k][...].astype(F32) + table[BIAS_O, :full]
    for m in range(SEQ):
        part = mm(o[m][...], w[rows_at(order[m] * width, width), :])
        for k in range(SEQ):
            there = (k ^ m) * rows
            hold[there : there + rows, :] += part[k * rows : (k + 1) * rows, :]
    x_out[...] = hold[0:rows, :]
    normal, _ = standardize(hold[...])
    c_out[...] = (normal * table[GAIN_TWO, :full] + table[SHIFT_TWO, :full]).astype(BF)


def feed_forward(idx, order, c, g, table, *refs):
    pieces = refs[: BLOCKS + 1]
    h_out, u_out, bias_out, w_reduce, o0, o1, o2, o3, e_far, r_far, w_expand = refs[BLOCKS + 1 :]
    step = w_expand.shape[0] // BLOCKS
    for k in range(BLOCKS):
        at = rows_at(idx[k] * step, step)
        w_expand[at, :] = pieces[k][:step, :]
        last_piece = pieces[k] if k < BLOCKS - 1 else pieces[k + 1]
        w_reduce[at, :] = last_piece[last_piece.shape[0] - step :, :]
    width = h_out.shape[1]
    group = bias_out.shape[1]
    bias = table[:, pl.ds(pl.multiple_of(w_expand.shape[0] + order[0] * group, group), group)]
    chunk = 2 * group
    for n in range(0, width, chunk):
        r = n // group
        row = jnp.concatenate([bias[r : r + 1], bias[r + 1 : r + 2]], axis=1)
        u = mm(c[...], w_expand[:, n : n + chunk]) + row
        upper = mm_nt(g[...], w_reduce[n : n + chunk, :])
        cdf = 0.5 * (1.0 + lax.erf(u * (0.5**0.5)))
        density = jnp.exp(-0.5 * u * u) * 0.3989422804014327
        h_out[:, n : n + chunk] = (u * cdf).astype(BF)
        low = (upper * (cdf + u * density)).astype(BF)
        u_out[:, n : n + chunk] = low
        total = jnp.sum(low.astype(F32), axis=0, keepdims=True)
        bias_out[r : r + 1, :] = total[:, :group]
        bias_out[r + 1 : r + 2, :] = total[:, group:]
    lower = mm_nt(u_out[...], w_expand[...])
    rows = o0.shape[0]
    for k, out in enumerate((o0, o1, o2, o3)):
        out[...] = lower[k * rows : (k + 1) * rows, :].astype(BF)
    at = rows_at(idx[BLOCKS - 1] * step, step)
    e_far[...] = mm_tn(c[:, at], u_out[...]).astype(BF)
    r_far[...] = mm_tn(h_out[:, at], g[...]).astype(BF)


def reduce_part(h, w, *outs):
    y = mm(h[...], w[...])
    rows = outs[0].shape[0]
    for k in range(SEQ):
        outs[k][...] = y[k * rows : (k + 1) * rows, :].astype(BF)


def feed_grads(idx, c, du, h, g, *outs):
    step = outs[0].shape[0] // 2
    for k in range(BLOCKS - 1):
        at = rows_at(idx[k] * step, step)
        outs[k][:step, :] = mm_tn(c[:, at], du[...]).astype(BF)
        outs[k][step:, :] = mm_tn(h[:, at], g[...]).astype(BF)


def add_two(a, a_own, b, b_own, a_out, b_out):
    here = a.shape[0]
    rest = b_own.shape[0] - b.shape[0]
    a_out[:here, :] = (a[...].astype(F32) + a_own[:here, :].astype(F32)).astype(BF)
    b_out[rest:, :] = (b[...].astype(F32) + b_own[rest:, :].astype(F32)).astype(BF)
    if rest:
        a_out[here:, :] = a_own[here:, :]
        b_out[:rest, :] = b_own[:rest, :]


def norm_pull(upper, normal, scale, gain):
    inner = upper * gain
    return scale * (
        inner
        - jnp.mean(inner, axis=-1, keepdims=True)
        - normal * jnp.mean(inner * normal, axis=-1, keepdims=True)
    )


def middle_back(part0, part1, part2, x, cot, factor, table, grad_out, low_out, sums_out):
    upper = part0[...].astype(F32) + part1[...].astype(F32) + part2[...].astype(F32)
    normal, scale = standardize(x[...])
    upstream = cot[...].astype(F32) * factor[...]
    grad = upstream + norm_pull(upper, normal, scale, table[GAIN_TWO, : x.shape[1]])
    low = grad.astype(BF)
    grad_out[...] = grad
    low_out[...] = low
    sums_out[0:1, :] = jnp.sum(upper * normal, axis=0, keepdims=True)
    sums_out[1:2, :] = jnp.sum(upper, axis=0, keepdims=True)
    sums_out[2:3, :] = jnp.sum(low.astype(F32), axis=0, keepdims=True)
    sums_out[3:4, :] = jnp.sum(upstream, axis=0, keepdims=True)


def attend_back(order, *refs):
    grads = refs[:SEQ]
    w_rows, qkv, stat, key_mask, g_out, out, sums_out, hold = refs[SEQ:]
    rows = grads[0].shape[0]
    for k in range(SEQ):
        hold[k * rows : (k + 1) * rows, :] = grads[k][...].astype(F32)
    g_out[...] = hold[...].astype(BF)
    width = qkv.shape[1] // 3
    size = width // (HEADS // SEQ)
    d_out = mm_nt(g_out[...], w_rows[...]).astype(BF)
    q, key, value = (qkv[:, i * width : (i + 1) * width] for i in range(3))
    valid = key_mask[...] > 0
    dq = dk = dv = None
    for h in range(HEADS // SEQ):
        lanes = head_lanes(width, h, size)
        q_h = jnp.where(lanes, q, jnp.zeros_like(q))
        d_h = jnp.where(lanes, d_out, jnp.zeros_like(d_out))
        logits = mm_nt(q_h, key)
        scores = jnp.where(valid, logits * size ** (-0.5), -1000000000.0)
        top = stat[:, h : h + 1]
        inverse = stat[:, HEADS // SEQ + h : HEADS // SEQ + h + 1]
        probs = jnp.exp(scores - top) * inverse
        prob_grad = mm_nt(d_h, value)
        center = jnp.sum(probs * prob_grad, axis=-1, keepdims=True)
        low = jnp.where(valid, probs * (prob_grad - center) * size ** (-0.5), 0.0).astype(BF)
        dv_h = mm_tn(probs.astype(BF), d_h)
        dk_h = mm_tn(low, q_h)
        dq_h = mm(low, jnp.where(lanes, key, jnp.zeros_like(key)))
        dq = dq_h if dq is None else dq + dq_h
        dk = dk_h if dk is None else dk + dk_h
        dv = dv_h if dv is None else dv + dv_h
    dq, dk, dv = dq.astype(BF), dk.astype(BF), dv.astype(BF)
    out[:, :width] = dq
    out[:, width : 2 * width] = dk
    out[:, 2 * width :] = dv
    sums_out[0:1, :] = jnp.sum(dq.astype(F32), axis=0, keepdims=True)
    sums_out[1:2, :] = jnp.sum(dv.astype(F32), axis=0, keepdims=True)


def attention_grads(idx, order, a, d, g, sums, *refs):
    o = refs[:SEQ]
    outs = refs[SEQ : SEQ + BLOCKS + 1]
    hold, turned = refs[SEQ + BLOCKS + 1 :]
    rows = g.shape[0] // SEQ
    width = o[0].shape[1]
    full = hold.shape[0]
    step = full // BLOCKS
    mine = g[:, rows_at(order[0] * width, width)].astype(F32)
    for m in range(SEQ):
        for k in range(SEQ):
            there = (k ^ m) * rows
            turned[k * rows : (k + 1) * rows, :] = mine[there : there + rows, :]
        hold[rows_at(order[m] * width, width), :] = mm_tn(o[m][...], turned[...].astype(BF)).astype(BF)
    count, wide = sums.shape[0], step
    biases = sums[:, pl.ds(pl.multiple_of(full + order[0] * wide, wide), wide)]
    row = lax.broadcasted_iota(jnp.int32, biases.shape, 0)
    for k in range(BLOCKS):
        at = rows_at(idx[k] * step, step)
        value = mm_tn(a[:, at], d[...]).astype(BF)
        size = step if k < BLOCKS - 1 else step // 2
        outs[k][:size, : 3 * width] = value[:size]
        outs[k][:size, 3 * width :] = hold[rows_at(idx[k] * step, size), :]
        below = outs[k]
        if k == BLOCKS - 1:
            below = outs[k + 1]
            below[:size, : 3 * width] = value[size:]
            below[:size, 3 * width :] = hold[rows_at(idx[k] * step + size, size), :]
        if below.shape[0] > size:
            extra = below.shape[0] - size
            bias = jnp.sum(jnp.where(row == idx[k], biases, 0.0), axis=0, keepdims=True)
            below[size:, :wide] = sums[:, rows_at(idx[k] * wide, wide)].astype(BF)
            below[size:, wide : 2 * wide] = jnp.broadcast_to(bias, (extra, wide)).astype(BF)
            below[size:, 2 * wide :] = jnp.zeros((extra, below.shape[1] - 2 * wide), BF)


def normed_back(order, d, w, normal, sums_qv, sums_mid, sum_e, sums, *outs):
    rows, width = outs[0].shape
    part, wide = sums_qv.shape[1], sum_e.shape[1]
    upper = mm_nt(d[...], w[...])
    for k in range(SEQ):
        outs[k][...] = upper[k * rows : (k + 1) * rows, :].astype(BF)
    sums[...] = jnp.zeros_like(sums)
    sums[GAIN_ONE, :width] = jnp.sum(upper * normal[...].astype(F32), axis=0, keepdims=True)
    sums[SHIFT_ONE, :width] = jnp.sum(upper, axis=0, keepdims=True)
    mine = rows_at(order[0] * part, part)
    sums[BIAS_Q, mine] = sums_qv[0:1, :]
    sums[BIAS_V, mine] = sums_qv[1:2, :]
    sums[BIAS_O, :width] = sums_mid[2:3, :]
    sums[GAIN_TWO, :width] = sums_mid[0:1, :]
    sums[SHIFT_TWO, :width] = sums_mid[1:2, :]
    sums[BIAS_R, :width] = sums_mid[3:4, :]
    sums[:, pl.ds(pl.multiple_of(width + order[0] * wide, wide), wide)] = sum_e[...]


def last(part0, part1, part2, x, grad, y0, y1, y2, x_mid, table, grad_out, y_out):
    width = x.shape[1]
    upper = part0[...].astype(F32) + part1[...].astype(F32) + part2[...].astype(F32)
    normal, scale = standardize(x[...].astype(F32))
    grad_out[...] = (grad[...] + norm_pull(upper, normal, scale, table[GAIN_ONE, :width])).astype(BF)
    y = x_mid[...] + table[BIAS_R, :width] + y0[...].astype(F32)
    y_out[...] = (y + y1[...].astype(F32) + y2[...].astype(F32)).astype(BF)


def finish(p0, p1, p2, w0, w1, w2, w3, sums, bias):
    high, part = w0.shape
    _, wide = sums.shape
    for i, out in enumerate((w0, w1, w2, w3)):
        at = slice(i * part, (i + 1) * part)
        out[...] = p0[:high, at].astype(F32) + p1[:high, at].astype(F32) + p2[:high, at].astype(F32)
    both = slice(0, 2 * wide)
    below = p0[high:, both].astype(F32) + p1[high:, both].astype(F32) + p2[high:, both].astype(F32)
    sums[...] = below[:, :wide]
    bias[...] = below[:1, wide:]


def seq_swap(value, flip):
    return lax.ppermute(value, "seq", [(s, s ^ flip) for s in range(SEQ)])


def after(value, *others):
    return lax.optimization_barrier((value,) + others)[0]


def add(a, b):
    return (a.astype(F32) + b.astype(F32)).astype(BF)


def ring_order(data_count):
    return list(range(0, data_count, 2)) + list(range(data_count - 1, 0, -2))


def ring_hop(value, data_count, step):
    ring = ring_order(data_count)
    pairs = [(ring[r], ring[(r + step) % data_count]) for r in range(data_count)]
    return lax.ppermute(value, "dp", pairs)


RELATIVE = (0, -1, -2, -3, 1, 2, 3, 4)


def relative_order(data_count):
    if data_count != RING:
        return jnp.arange(BLOCKS, dtype=jnp.int32)
    me = lax.axis_index("dp")
    z, y = me // 2, me % 2
    place = jnp.where(y == 0, z, BLOCKS - 1 - z)
    there = (place + jnp.array(RELATIVE, dtype=jnp.int32) + BLOCKS) % BLOCKS
    half = BLOCKS // 2
    return jnp.where(there < half, 2 * there, 2 * (BLOCKS - 1 - there) + 1).astype(jnp.int32)


@jax.tree_util.register_pytree_node_class
class Gather:
    def __init__(self, value, data_count, parts, cut, back=(), front=()):
        self.value, self.data_count, self.parts, self.cut = value, data_count, parts, cut
        self.back, self.front = list(back), list(front)

    def tree_flatten(self):
        return (self.value, self.back, self.front), (self.data_count, self.parts, self.cut)

    @classmethod
    def tree_unflatten(cls, aux, parts):
        return cls(parts[0], *aux, *parts[1:])

    def hop(self):
        if self.data_count != RING:
            if not self.back:
                whole = lax.all_gather(self.value, "dp", axis=0, tiled=False)
                parts = [p.reshape((BLOCKS, -1) + p.shape[2:]) for p in jnp.split(whole, self.parts, axis=1)]
                self.back = list(jnp.concatenate(parts, axis=1))
            return
        back, front = (self.back or [self.value])[-1], (self.front or [self.value])[-1]
        if len(self.back) == BLOCKS // 2 - 1:
            back, front = back[: self.cut], front[self.cut :]
        self.back.append(ring_hop(back, self.data_count, 1))
        self.front.append(ring_hop(front, self.data_count, -1))

    def blocks(self, last=(0, 1)):
        if self.data_count != RING:
            halves = (self.back[-1][: self.cut], self.back[-1][self.cut :])
            return self.back[:-1] + [halves[i] for i in last]
        halves = (self.back[3], self.front[3])
        return [self.value] + self.back[:3] + self.front[:3] + [halves[i] for i in last]


@jax.tree_util.register_pytree_node_class
class Scatter:
    def __init__(self, pieces, data_count, parts, hops=0, left=None, right=None):
        self.pieces, self.data_count, self.parts = pieces, data_count, parts
        self.hops, self.left, self.right = hops, left, right

    def tree_flatten(self):
        return (self.pieces, self.left, self.right), (self.data_count, self.parts, self.hops)

    @classmethod
    def tree_unflatten(cls, aux, parts):
        return cls(parts[0], *aux, *parts[1:])

    def hop(self):
        n, self.hops = self.hops, self.hops + 1
        if self.data_count != RING:
            if n == 0:
                whole = jnp.concatenate(self.pieces, axis=0)
                wide = whole.shape[1]
                whole = whole.reshape(BLOCKS, self.parts, self.data_count // BLOCKS, -1, wide)
                whole = whole.transpose(0, 2, 1, 3, 4).reshape(-1, wide)
                self.left = lax.psum_scatter(whole, "dp", scatter_dimension=0, tiled=True)
            return self.left
        own = dict(zip(RELATIVE, self.pieces))
        left, right = self.left, self.right
        if n == 0:
            left, right = self.pieces[-2:]
        else:
            ahead, behind = own[4 - n], own[n - 4]
            outs = (shape(ahead.shape, BF),) * 2
            left, right = kernel_call(add_two, outs, left, ahead, right, behind)
        self.left = ring_hop(left, self.data_count, 1)
        self.right = ring_hop(right, self.data_count, -1)
        return left

    def terms(self):
        if self.data_count != RING:
            return [self.left, jnp.zeros_like(self.left), jnp.zeros_like(self.left)]
        return [self.pieces[0], self.left, self.right]


def sum_slot(value):
    value = value + seq_swap(value, 1)
    return value + seq_swap(value, 2)


def trade(parts, data_count):
    return [parts[0]] + [seq_swap(parts[m], m) for m in range(1, SEQ)]


def pack_hidden_weights(order, w_expand, w_reduce, data_count):
    high, low, part = w_expand.shape[0], w_reduce.shape[0] // SEQ, w_reduce.shape[1]
    if data_count == RING:
        piece = shape((high + low, part), BF)
        sems = [pltpu.SemaphoreType.DMA((3 * SEQ,))]
        return list(
            kernel_call(pack_hidden, (piece,) * SEQ, order, w_expand, w_reduce, far=(1, 2), scratch=sems)
        )
    e = w_expand.reshape(high, -1, SEQ, low).transpose(2, 0, 1, 3).reshape(SEQ, high, part)
    both = jnp.concatenate([e, w_reduce.reshape(SEQ, low, part)], axis=1)
    return [lax.dynamic_index_in_dim(both, order[m], 0, False) for m in range(SEQ)]


def join_hidden_weights(order, parts, data_count):
    rows, part = parts[0].shape
    if data_count == RING:
        return kernel_call(join_hidden, (shape((rows, SEQ * part), BF),), order, *parts)[0]
    both = jnp.zeros((rows, SEQ * part), BF)
    for m in range(SEQ):
        both = lax.dynamic_update_slice(both, parts[m], (0, order[m] * part))
    return both


def part_hidden_grads(order, terms, part, data_count):
    if data_count == RING:
        piece = (terms[0].shape[0], part)
        outs = (shape(piece, F32),) + (shape(piece, BF),) * (SEQ - 1)
        return list(kernel_call(part_hidden, outs, order, *terms))
    return [lax.dynamic_slice_in_dim(terms[0], order[m] * part, part, 1) for m in range(SEQ)]


def place_hidden_grads(order, parts, e_shape, r_shape, data_count):
    if data_count == RING:
        outs = (shape(e_shape, F32), shape(r_shape, F32))
        return kernel_call(place_hidden, outs, order, *parts)
    high, low = e_shape[0], r_shape[0] // SEQ
    both = jnp.zeros((SEQ,) + parts[0].shape, F32)
    for m in range(SEQ):
        both = lax.dynamic_update_slice(both, parts[m].astype(F32)[None], (order[m], 0, 0))
    e = both[:, :high].reshape(SEQ, high, -1, low).transpose(1, 2, 0, 3).reshape(e_shape)
    return e, both[:, high:].reshape(r_shape)


def eight(deep, wide):
    return (shape((deep, wide), BF),) * (BLOCKS - 1) + (shape((deep // 2, wide), BF),) * 2


def sync(state):
    return lax.optimization_barrier(state)


def local(
    block_input,
    cotangent,
    image_valid,
    token_valid,
    first_gain,
    first_shift,
    query_weight,
    query_bias,
    key_weight,
    value_weight,
    value_bias,
    output_weight,
    output_bias,
    second_gain,
    second_shift,
    expand_weight,
    expand_bias,
    reduce_weight,
    reduce_bias,
):
    data_count = lax.axis_size("dp")
    ring = data_count == RING
    me = lax.axis_index("seq")
    rows, width = block_input.shape[1:]
    tokens = rows * SEQ
    part = width // SEQ
    deep = expand_weight.shape[1]
    step = width // BLOCKS
    full = shape((tokens, width), BF)
    block = shape((rows, width), BF)
    s = {}
    s["idx"] = relative_order(data_count)
    dp = lax.axis_index("dp")
    s["order"] = jnp.stack([me ^ k for k in range(SEQ)] + [dp]).astype(jnp.int32)

    vectors = (
        first_gain,
        first_shift,
        query_bias,
        value_bias,
        output_bias,
        second_gain,
        second_shift,
        reduce_bias,
    )
    each = first_gain.shape[0]
    place = dp * SEQ + me
    count = len(vectors)
    group = deep // BLOCKS
    bias_row = expand_bias.astype(F32)[None]
    bias_length = expand_bias.shape[0]
    bias_at = dp * bias_length
    bias_at = (bias_at // group, me * group + bias_at % group)
    table = shape((count, width + SEQ * group), F32)

    valid = token_valid.astype(F32).reshape(SEQ, rows)
    valid = jnp.concatenate([lax.dynamic_slice_in_dim(valid, s["order"][k], 1, 0) for k in range(SEQ)], axis=1)
    s["valid"] = valid
    s["factor"] = (valid * image_valid.astype(F32)[0]).reshape(tokens, 1)

    attention_weights = (query_weight, key_weight, value_weight, output_weight)
    extra = count if ring else 0
    if ring:
        args = attention_weights + vectors + (expand_bias,)
        scratch = [pltpu.SemaphoreType.DMA((len(args),)), pltpu.VMEM((extra, 2 * group), F32)]
        scratch += [pltpu.VMEM(v.shape, BF) for v in args[4:]]
        outs = (shape((step + extra, width), BF),)
        (piece,) = kernel_call(pack_columns, outs, *args, far=range(len(args)), scratch=scratch)
    else:
        piece = jnp.concatenate(attention_weights, axis=1)
    s["attention"] = Gather(piece, data_count, 1, step // 2)
    s["attention"].hop()
    s["x"] = [block_input[0]]
    s["x"] += [seq_swap(s["x"][0], m) for m in (1, 2)]
    s["cot"] = [cotangent[0]]
    s["hidden"] = pack_hidden_weights(s["order"], expand_weight, reduce_weight, data_count)
    s = sync(s)

    s["attention"].hop()
    hidden = s.pop("hidden")
    s["hidden"] = [hidden[0]] + [seq_swap(hidden[m], m) for m in (1, 2)]
    s["hidden_last"] = hidden[3]
    s = sync(s)

    s["attention"].hop()
    s["hidden"].append(seq_swap(s.pop("hidden_last"), 3))
    s["x"].append(seq_swap(s["x"][2], 1))
    s["cot"].append(seq_swap(s["cot"][0], 2))
    s = sync(s)

    s["attention"].hop()
    s["cot"] = [s["cot"][0], seq_swap(s["cot"][0], 1), s["cot"][1], seq_swap(s["cot"][1], 1)]
    feed = join_hidden_weights(s["order"], s.pop("hidden"), data_count)
    s["feed"] = Gather(feed, data_count, 2, step)
    s = sync(s)

    s["feed"].hop()
    half = shape((width // 2, part), BF)
    s["w_qkv"], w_low, w_high, s["table"] = kernel_call(
        stack_rows,
        (shape((width, 3 * part), BF), half, half, table),
        s["idx"],
        s["order"],
        *s.pop("attention").blocks(),
    )
    s["w_low"], s["w_high"] = [w_low], [w_high]
    s["w_low"].append(seq_swap(after(w_low, s["w_qkv"]), 2))
    if ring:
        s["table"] = sum_slot(s["table"])
    else:
        every = lax.broadcasted_iota(jnp.int32, (each, width), 1)
        every = every == place * each + lax.broadcasted_iota(jnp.int32, (each, width), 0)
        stacked = sum(
            jnp.pad(v[None], ((i, count - 1 - i), (0, 0))) for i, v in enumerate(vectors)
        )
        placed = jnp.dot(stacked, every.astype(BF), preferred_element_type=F32)
        placed_bias = lax.dynamic_update_slice(
            jnp.zeros((count, table.shape[1] - width), F32), bias_row, bias_at
        )
        s["table"] = lax.psum(jnp.concatenate([placed, placed_bias], axis=1), ("dp", "seq"))
    s = sync(s)

    s["feed"].hop()
    s["w_high"] += [seq_swap(s["w_high"][0], m) for m in (1, 2)]
    s["a"], s["normal"] = kernel_call(
        norm_one, (full, full), *s["x"], s["table"], scratch=[pltpu.VMEM((tokens, width), F32)]
    )
    s["qkv"], o, s["stat"] = kernel_call(
        attend,
        (shape((tokens, 3 * part), BF), shape((tokens, part), BF), shape((tokens, 128), F32)),
        s["order"],
        s["a"],
        s["w_qkv"],
        s["table"],
        s["valid"],
        flops=2 * tokens * part * (3 * width + 8 * tokens),
    )
    s["o"] = [o]
    s = sync(s)

    s["feed"].hop()
    s["o"].append(seq_swap(s["o"][0], 2))
    (s["g"],) = kernel_call(
        mask_rows, (full,), *s["cot"], s["factor"], scratch=[pltpu.VMEM((tokens, width), F32)]
    )
    s["cot"] = s["cot"][0]
    s["w_low"].append(seq_swap(s["w_low"][1], 1))
    s = sync(s)

    s["feed"].hop()
    o_mine, o_two = s["o"]
    s["o"] = [o_mine, seq_swap(o_mine, 1), o_two, seq_swap(o_two, 1)]
    s["w_high"].append(seq_swap(s["w_high"][2], 1))
    s["w_low"].insert(1, seq_swap(s["w_low"][0], 1))
    s["c"], s["x_mid"], s["w_rows"] = kernel_call(
        middle,
        (full, shape((rows, width), F32), shape((part, width), BF)),
        s["order"],
        *s["o"],
        *s.pop("w_low"),
        *s.pop("w_high"),
        *s["x"],
        s["table"],
        scratch=[pltpu.VMEM((tokens, width), F32), pltpu.VMEM((width, width), BF)],
        flops=2 * tokens * width * width,
    )
    s["x"] = s["x"][0]
    s = sync(s)

    h, du, s["sum_e"], w_r, *c_part, e_far, r_far = kernel_call(
        feed_forward,
        (
            shape((tokens, deep), BF),
            shape((tokens, deep), BF),
            shape((BLOCKS, group), F32),
            shape((deep, width), BF),
            block,
            block,
            block,
            block,
            shape((step, deep), BF),
            shape((step, width), BF),
        ),
        s["idx"],
        s["order"],
        s["c"],
        s["g"],
        s["table"],
        *s.pop("feed").blocks(),
        scratch=[pltpu.VMEM((width, deep), BF)],
        flops=7 * tokens * width * deep,
    )
    s["c_part"] = c_part
    s["c_got"] = [seq_swap(c_part[m], 1) for m in (1, 3)]
    far = [e_far, r_far]
    args = (s["idx"], s.pop("c"), du, h, s.pop("g"))
    s["c_two"] = seq_swap(add(after(s["c_part"][2], s["c_got"][0]), s["c_got"][1]), 2)
    pieces = kernel_call(
        feed_grads,
        (shape((2 * step, deep), BF),) * (BLOCKS - 1),
        after(args[0], far[0]),
        *args[1:],
        flops=3 * tokens * width * deep,
    )
    s["feed_grad"] = Scatter(list(pieces) + list(far), data_count, 2)
    s["feed_grad"].hop()
    s["y_part"] = kernel_call(
        reduce_part,
        (block, block, block, block),
        after(h, pieces[0]),
        w_r,
        flops=2 * tokens * width * deep,
    )
    s = sync(s)

    s["mid_grad"], branch, s["sums_mid"] = kernel_call(
        middle_back,
        (shape((rows, width), F32), block, shape((4, width), F32)),
        s.pop("c_part")[0],
        s.pop("c_got")[0],
        s.pop("c_two"),
        s["x_mid"],
        s["cot"],
        s["factor"][:rows],
        s["table"],
    )
    branch_two = seq_swap(branch, 2)
    s["feed_grad"].hop()
    s["y_got"] = [seq_swap(s["y_part"][1], 1)]
    s["branch"] = [branch, branch_two]
    s = sync(s)

    branch, branch_two = s.pop("branch")
    s["branch"] = [branch, seq_swap(branch, 1), branch_two, seq_swap(branch_two, 1)]
    s["feed_grad"].hop()
    s["y_got"].append(seq_swap(s["y_part"][3], 1))
    s["branch_full"], s["dqkv"], s["sums_qv"] = kernel_call(
        attend_back,
        (full, shape((tokens, 3 * part), BF), shape((2, part), F32)),
        s["order"],
        *s.pop("branch"),
        s.pop("w_rows"),
        s.pop("qkv"),
        s.pop("stat"),
        s["valid"],
        scratch=[pltpu.VMEM((tokens, width), F32)],
        flops=2 * tokens * part * (width + 20 * tokens),
    )
    s = sync(s)

    sent = s["feed_grad"].hop()
    s["sums"], *s["a_part"] = kernel_call(
        normed_back,
        (table, block, block, block, block),
        s["order"],
        after(s["dqkv"], sent),
        s.pop("w_qkv"),
        s.pop("normal"),
        s.pop("sums_qv"),
        s.pop("sums_mid"),
        s.pop("sum_e"),
        flops=6 * tokens * width * part,
    )
    if not ring:
        s["sums"] = lax.psum(s["sums"], ("dp", "seq"))
    s["a_got"] = [seq_swap(s["a_part"][m], 1) for m in (1, 3)]
    half = step // 2
    pieces = kernel_call(
        attention_grads,
        (shape((step + extra, width), BF),) * (BLOCKS - 1)
        + (shape((half, width), BF), shape((half + extra, width), BF)),
        s["idx"],
        s["order"],
        after(s.pop("a"), *s["a_got"]),
        s.pop("dqkv"),
        s.pop("branch_full"),
        s["sums"],
        *s.pop("o"),
        scratch=[pltpu.VMEM((width, part), BF), pltpu.VMEM((tokens, part), F32)],
        flops=8 * tokens * width * part,
    )
    s["attention_grad"] = Scatter(list(pieces), data_count, 1)
    s["attention_grad"].hop()
    s = sync(s)

    sent = s["attention_grad"].hop()
    s["hidden"] = part_hidden_grads(s["order"], s.pop("feed_grad").terms(), part, data_count)
    s["a_two"] = seq_swap(add(after(s["a_part"][2], sent), s["a_got"][1]), 2)
    s["y_two"] = add(after(s["y_part"][2], sent), s["y_got"][1])
    s = sync(s)

    s["attention_grad"].hop()
    s["y_two"] = seq_swap(s["y_two"], 2)
    s["hidden_got"] = [seq_swap(s["hidden"][1], 1)]
    s = sync(s)

    s["attention_grad"].hop()
    s["hidden_got"] += [seq_swap(s["hidden"][m], m) for m in (2, 3)]
    s["input_gradient"], s["y"] = kernel_call(
        last,
        (block, block),
        s["a_part"][0],
        s["a_got"][0],
        s["a_two"],
        s["x"],
        s["mid_grad"],
        s["y_part"][0],
        s["y_got"][0],
        s["y_two"],
        s["x_mid"],
        s["table"],
    )
    s = sync(s)

    terms = s["attention_grad"].terms()
    high = attention_weights[0].shape[0]
    if ring:
        matrix = shape((high, part), F32)
        outs = (matrix,) * 4 + (shape((count, group), F32), shape((1, group), F32))
        *matrices, sums, bias_sum = kernel_call(finish, outs, *terms)
        grads = lax.dynamic_slice(sum_slot(sums), (0, me * each), (count, each))
        expand_bias_grad = bias_sum[0, :bias_length]
    else:
        grads = lax.dynamic_slice_in_dim(s["sums"], place * each, each, 1)
        expand_bias_grad = lax.dynamic_slice(s["sums"][:, width:], bias_at, (1, bias_length))[0]
        total = sum(t.astype(F32) for t in terms)
        matrices = [total[:, i * part : (i + 1) * part] for i in range(4)]
    expand_weight_grad, reduce_weight_grad = place_hidden_grads(
        s["order"], s["hidden"][:1] + s["hidden_got"], expand_weight.shape, reduce_weight.shape, data_count
    )
    return (
        s["y"][None],
        s["input_gradient"][None],
        grads[0],
        grads[1],
        matrices[0],
        grads[2],
        matrices[1],
        matrices[2],
        grads[3],
        matrices[3],
        grads[4],
        grads[5],
        grads[6],
        expand_weight_grad,
        expand_bias_grad,
        reduce_weight_grad,
        grads[7],
    )


def solution(mesh):
    vector = P(("dp", "seq"))
    matrix = P("dp", "seq")
    tokens = P("dp", "seq", None)
    return jax.shard_map(
        local,
        mesh=mesh,
        in_specs=(
            tokens,
            tokens,
            P("dp"),
            P(),
            vector,
            vector,
            matrix,
            vector,
            matrix,
            matrix,
            vector,
            matrix,
            vector,
            vector,
            vector,
            matrix,
            vector,
            matrix,
            vector,
        ),
        out_specs=(
            tokens,
            tokens,
            vector,
            vector,
            matrix,
            vector,
            matrix,
            matrix,
            vector,
            matrix,
            vector,
            vector,
            vector,
            matrix,
            vector,
            matrix,
            vector,
        ),
        check_vma=False,
    )
```
